256 devices in a mesh: dp: 64 (over x_lo, y, z), mp: 4 (over x_hi, core).
Axes of the slice: x: 4 (x_hi: 2, x_lo: 2; x = x_hi * 2 + x_lo), y: 4, z: 8, core: 2. Of those that a mesh axis runs over, the one named last changes fastest.
Arguments:
- activations: bfloat16 [16384, 2560], P('dp', 'mp'), may hold values from -6 to 6
- grad_out: bfloat16 [16384, 5120], P('dp', 'mp'), may hold values from -0.001953125 to 0.001953125
- stats_old: float32 [4, 1, 64, 160, 640], P('mp', None, 'dp'), may hold values from -1 to 1, as said below
- owner_map: int32 [8], replicated, may hold values from 0 to 7, each once
- rotation: int32 [1], replicated, may hold values from 0 to 7
Outputs:
- update: bfloat16 [8, 2560, 640], P('mp')
- stats_new: float32 [4, 1, 64, 160, 640], P('mp', None, 'dp')
- roots_new: float32 [4, 1, 64, 160, 640], P('mp', None, 'dp')
The draws below stay inside these ranges and needn't reach their ends.
Inputs may be any that keep to these rules, and one draw needn't show every extreme that they name: `stats_old`: each of the 4 x 8 x 2 matrices read by the reshape to [4, 8, 2, 640, 640] is symmetric positive definite. `owner_map`: a permutation of the 8 positions.
All inputs are finite; a program needn't handle non-finite values.
Results may differ from the reference program's by a relative error of at most 0.0053.
Values may be sent and summed in bfloat16 or wider, within the bound.
A program may use at most 192 MiB of HBM per device.

```python
import jax
import jax.numpy as jnp
from jax import lax

D = 5120
B = 640
DIN = 2560
ITERS = 4
TOKENS = 16384
RB = 4
CB = 2
NB = 8
SLOTS = 1
QR = 160
N_DP = 64
N_MP = 4


def draw_stats_old(key, part):
    key = jax.random.fold_in(key, 7)
    diag_key, noise_key = jax.random.split(key)
    low_end, high_end = (0.05, 0.5)
    exponent = jax.random.uniform(diag_key, (N_MP, NB, 2, B, 1), jnp.float32, jnp.log(low_end), jnp.log(high_end))
    root_diag = jnp.sqrt(jnp.exp(exponent))
    noise_draw = jax.random.uniform(noise_key, (N_MP, NB, 2, B, B), jnp.float32, -1.0, 1.0)
    symmetric = 0.5 * (noise_draw + jnp.swapaxes(noise_draw, -1, -2))
    rows_index = jnp.arange(B)[:, None]
    cols_index = jnp.arange(B)[None, :]
    identity = (rows_index == cols_index).astype(jnp.float32)
    matrix = root_diag * jnp.swapaxes(root_diag, -1, -2) * (identity + 0.5 / B * symmetric)
    return matrix.reshape(N_MP, SLOTS, N_DP, QR, B).astype(jnp.float32)


def steps_of(rng, dims, cuts, least, top_value):
    def one(axis_at, shards_of):
        steps = jax.random.uniform(jax.random.fold_in(jax.random.fold_in(rng, 6), axis_at), (shards_of,), jnp.float32, least / len(cuts), top_value / len(cuts))
        return jnp.repeat(jnp.exp(steps), dims[axis_at] // shards_of).reshape((-1,) + (1,) * (len(dims) - axis_at - 1))

    gain = one(*cuts[0])
    for cut in cuts[1:]:
        gain = gain * one(*cut)
    return gain


def normal_values(stream_key, dims, width, limit, cuts=(), kind=jnp.bfloat16):
    values = jax.random.normal(stream_key, dims, jnp.float32) * width
    if len(cuts) > 0:
        values = steps_of(stream_key, dims, cuts, -0.22, 0.18) * values
    return jnp.clip(values, min=-limit, max=limit).astype(kind)


def setup_inputs(seed: int = 0) -> dict:
    keys = jax.random.split(jax.random.key(seed), 6)
    activations = normal_values(keys[0], (TOKENS, DIN), 1.0, 6.0, ((0, 64), (1, 4)))
    grad_out = normal_values(keys[1], (TOKENS, D), (B * TOKENS) ** -0.5, 0.001953125, ((0, 64), (1, 4)))
    stats_old = draw_stats_old(jax.random.fold_in(keys[5], 71), 0)
    owner_map = jax.random.permutation(keys[3], NB).astype(jnp.int32)
    rotation = jax.random.randint(keys[4], (1,), 0, NB).astype(jnp.int32)
    return {"activations": activations, "grad_out": grad_out, "stats_old": stats_old, "owner_map": owner_map, "rotation": rotation}


BETA = 0.9

def matmul_f32(left_op, right_op):
    return jnp.einsum('kij,kjl->kil', left_op, right_op, precision=lax.Precision.HIGHEST)

def inverse_root(statistic):
    identity = jnp.eye(statistic.shape[-1], dtype=jnp.float32)
    frobenius = jnp.sqrt(lax.optimization_barrier(jnp.sum(statistic * statistic, axis=(1, 2))))
    scale = 2.5 / frobenius
    moment = scale[:, None, None] * statistic
    iterate = jnp.power(scale, 0.25)[:, None, None] * identity
    for iteration in range(ITERS):
        factor = (5.0 * identity - moment) * 0.25
        iterate = matmul_f32(iterate, factor)
        if iteration + 1 < ITERS:
            square = matmul_f32(factor, factor)
            fourth = matmul_f32(square, square)
            moment = matmul_f32(fourth, moment)
    return iterate

def reference(activations, grad_out, stats_old, owner_map, rotation):
    gradient = jnp.dot(activations.astype(jnp.float32).T, grad_out.astype(jnp.float32), precision=lax.Precision.HIGHEST).astype(jnp.bfloat16)
    blocks = gradient.reshape(RB, B, N_MP, CB, B).transpose(2, 3, 0, 1, 4).reshape(N_MP, NB, B, B)
    places = jnp.arange(NB, dtype=jnp.int32)
    inverse = lax.optimization_barrier(jnp.sum(places[:, None] * (owner_map[:, None] == places[None, :]).astype(jnp.int32), axis=0)).astype(jnp.int32)
    placed = blocks[:, inverse].astype(jnp.float32)
    placed_flat = placed.reshape(N_MP * NB, B, B)
    flipped = jnp.swapaxes(placed_flat, 1, 2)
    old_stats = stats_old.reshape(N_MP, NB, 2, B, B)
    left_stat = BETA * old_stats[:, :, 0] + (1.0 - BETA) * matmul_f32(placed_flat, flipped).reshape(N_MP, NB, B, B)
    right_stat = BETA * old_stats[:, :, 1] + (1.0 - BETA) * matmul_f32(flipped, placed_flat).reshape(N_MP, NB, B, B)
    fresh = jnp.stack([left_stat, right_stat], axis=2)
    root_stack = inverse_root(fresh.reshape(N_MP * NB * 2, B, B)).reshape(N_MP, NB, 2, B, B)
    source = ((places - rotation[0]) % NB).astype(jnp.int32)
    moved = root_stack[:, source]
    left_roots = root_stack[:, :, 0].reshape(N_MP * NB, B, B)
    right_roots = root_stack[:, :, 1].reshape(N_MP * NB, B, B)
    update_placed = matmul_f32(matmul_f32(left_roots, placed_flat), right_roots).reshape(N_MP, NB, B, B).astype(jnp.bfloat16)
    ordered = update_placed[:, owner_map].reshape(N_MP * CB, RB * B, B)
    return (ordered, fresh.reshape(stats_old.shape), moved.reshape(stats_old.shape))
```

```python
import jax
import jax.numpy as jnp
from jax import lax
from jax.experimental import pallas as pl
from jax.experimental.pallas import tpu as pltpu
from jax.sharding import PartitionSpec as P

BETA = 0.9
MESH = pl.DeviceIdType.MESH
VMEM = pl.BlockSpec(memory_space=pltpu.VMEM)
SMEM = pl.BlockSpec(memory_space=pltpu.SMEM)
F32 = jnp.float32
BF16 = jnp.bfloat16


def place():
    dp = lax.axis_index("dp")
    mp = lax.axis_index("mp")
    return dp // 32, lax.rem(dp // 8, 4), lax.rem(dp, 8), mp // 2, lax.rem(mp, 2)


def device(x_lo, y, z, x_hi, core):
    return {"dp": x_lo * 32 + y * 8 + z, "mp": x_hi * 2 + core}


def greet(peers):
    barrier = pltpu.get_barrier_semaphore()
    for peer in peers:
        pl.semaphore_signal(barrier, inc=1, device_id=peer, device_id_type=MESH)
    pl.semaphore_wait(barrier, len(peers))


def remote(src, dst, send, recv, peer):
    return pltpu.make_async_remote_copy(
        src_ref=src, dst_ref=dst, send_sem=send, recv_sem=recv, device_id=peer, device_id_type=MESH
    )


class Ring:
    def __init__(self, slot, send, recv, peers, z):
        self.slot, self.send, self.recv = slot, send, recv
        self.up, self.down = peers
        self.z = z

    def copy_up(self, step):
        i = lax.rem(self.z - step + 8, 8)
        return remote(self.slot(i), self.slot(i), self.send.at[step], self.recv.at[step], self.up)

    def copy_down(self, step):
        i = lax.rem(self.z + step, 8)
        return remote(
            self.slot(i), self.slot(i), self.send.at[4 + step], self.recv.at[4 + step], self.down
        )

    def start(self, step):
        self.copy_up(step).start()
        if step < 3:
            self.copy_down(step).start()

    def arrived(self, step):
        self.copy_up(step).wait_recv()
        if step < 3:
            self.copy_down(step).wait_recv()

    def drain(self):
        for step in range(4):
            self.copy_up(step).wait_send()
            if step < 3:
                self.copy_down(step).wait_send()


def gather_kernel(
    act_ref, gout_ref, stat_ref, owner_ref, grad_ref, stats_ref,
    actg, goutg, total, part, rsbuf, gbuf,
    x_sem, a1_sem, a2_send, a_recv, g_send, g_recv, f_send, f_recv,
    st_send, st_recv, rs_send, rs_recv, gg_send, gg_recv, zz_send, zz_recv, loc_sem,
):
    x_lo, y, z, x_hi, core = place()
    mp = x_hi * 2 + core
    group = x_lo * 4 + y
    y_up, y_down, y_far = lax.rem(y + 1, 4), lax.rem(y + 3, 4), lax.rem(y + 2, 4)
    other_x = 1 - x_lo
    partner = device(other_x, y, z, x_hi, core)
    outer = device(other_x, y, z, 1 - x_hi, core)
    twin = device(x_lo, y, z, x_hi, 1 - core)
    z_peer = [device(x_lo, y, lax.rem(z + k, 8), x_hi, core) for k in range(1, 8)]
    up_y = device(x_lo, y_up, z, x_hi, core)
    down_y = device(x_lo, y_down, z, x_hi, core)
    g_peer = []
    for k in range(1, 8):
        g = lax.rem(group + k, 8)
        g_peer.append(device(g // 4, lax.rem(g, 4), z, x_hi, core))
    greet(z_peer + g_peer + [outer, twin])

    same = core == lax.rem(y, 2)
    root = jnp.logical_and(same, x_hi == y // 2)
    mid = jnp.logical_and(same, x_hi != y // 2)
    stray = y != mp

    half = gout_ref.at[:, pl.ds(pl.multiple_of(x_lo * 640, 128), 640)]
    away = gout_ref.at[:, pl.ds(pl.multiple_of(other_x * 640, 128), 640)]
    x_copy = remote(away, goutg.at[group], x_sem.at[0], x_sem.at[1], partner)
    x_copy.start()
    a1_copy = remote(
        act_ref, actg.at[group], a1_sem, a_recv.at[group], device(x_lo, mp, z, x_hi, core)
    )

    @pl.when(stray)
    def _():
        a1_copy.start()

    own_up = remote(half, goutg.at[group], g_send.at[0], g_recv.at[0], up_y)
    own_down = remote(half, goutg.at[group], g_send.at[1], g_recv.at[1], down_y)
    own_up.start()
    own_down.start()
    keep = pltpu.make_async_copy(half, goutg.at[group], loc_sem.at[0])
    keep.start()
    mine = pltpu.make_async_copy(act_ref, actg.at[group], loc_sem.at[1])

    @pl.when(jnp.logical_not(stray))
    def _():
        mine.start()

    stats_ref[z] = stat_ref[...]
    stats = Ring(lambda i: stats_ref.at[i], st_send, st_recv, (z_peer[0], z_peer[6]), z)
    stats.start(0)

    first = jnp.where(root, x_lo, other_x)

    def a_landed(slot):
        remote(actg.at[slot], actg.at[slot], a1_sem, a_recv.at[slot], partner).wait_recv()

    def a_send(slot, index, peer):
        return remote(actg.at[slot], actg.at[slot], a2_send.at[index], a_recv.at[slot], peer)

    def from_root():
        for k in range(4):
            slot = x_lo * 4 + k

            @pl.when(y == k)
            def _():
                mine.wait()

            @pl.when(y != k)
            def _():
                a_landed(slot)

            a_send(slot, k, partner).start()
            a_send(slot, 12 + k, outer).start()
            a_send(slot, 4 + k, twin).start()

    def from_mid(ks):
        for k in ks:
            slot = other_x * 4 + k
            a_landed(slot)
            a_send(slot, k, partner).start()
            a_send(slot, 4 + k, twin).start()

    stats.arrived(0)
    stats.start(1)
    pl.when(root)(from_root)

    pair_slot = other_x * 4 + y
    remote(goutg.at[pair_slot], goutg.at[pair_slot], x_sem.at[0], x_sem.at[1], partner).wait_recv()
    pair_up = remote(goutg.at[pair_slot], goutg.at[pair_slot], g_send.at[2], g_recv.at[2], up_y)
    pair_down = remote(goutg.at[pair_slot], goutg.at[pair_slot], g_send.at[3], g_recv.at[3], down_y)
    pair_up.start()
    pair_down.start()
    stats.arrived(1)
    stats.start(2)
    pl.when(mid)(lambda: from_mid((0, 1)))

    def along_y(column, index):
        low = column * 4 + y_down
        high = column * 4 + y_up
        remote(goutg.at[low], goutg.at[low], g_send.at[index], g_recv.at[index], up_y).wait_recv()
        on_up = remote(
            goutg.at[low, pl.ds(0, 128)], goutg.at[low, pl.ds(0, 128)],
            f_send.at[index], f_recv.at[index], up_y,
        )
        on_up.start()
        remote(
            goutg.at[high], goutg.at[high], g_send.at[index + 1], g_recv.at[index + 1], down_y
        ).wait_recv()
        on_down = remote(
            goutg.at[high, pl.ds(128, 128)], goutg.at[high, pl.ds(128, 128)],
            f_send.at[index + 1], f_recv.at[index + 1], down_y,
        )
        on_down.start()
        return [on_up, on_down]

    passed = along_y(x_lo, 0)
    stats.arrived(2)
    stats.start(3)
    pl.when(mid)(lambda: from_mid((2, 3)))
    passed += along_y(other_x, 2)
    stats.arrived(3)

    def to_twin():
        for k in range(4):
            slot = (1 - first) * 4 + k
            a_landed(slot)
            a_send(slot, 8 + k, twin).start()

    pl.when(same)(to_twin)

    @pl.when(jnp.logical_not(same))
    def _():
        for slot in range(8):
            a_landed(slot)

    for copy in passed:
        copy.wait_recv()
    keep.wait()

    def multiply(step):
        left = actg[pl.ds(step * 2, 2)].reshape(512, 640)
        right = goutg[pl.ds(step * 2, 2)].reshape(512, 640)
        return lax.dot_general(left, right, (((0,), (0,)), ((), ())), preferred_element_type=F32)

    total[...] = multiply(0)

    def accumulate(step, carry):
        total[...] += multiply(step)
        return carry

    lax.fori_loop(1, 4, accumulate, 0)
    for k in range(8):
        part[k] = total[pl.ds(k * 80, 80), :].astype(BF16)

    sums = []
    for k in range(1, 8):
        to = lax.rem(z + k, 8)
        copy = remote(part.at[to], rsbuf.at[k], rs_send.at[k], rs_recv.at[k], z_peer[k - 1])
        copy.start()
        sums.append(copy)
    rows = total[pl.ds(pl.multiple_of(z * 80, 8), 80), :]
    for k in range(1, 8):
        sums[k - 1].wait_recv()
        rows = rows + rsbuf[k].astype(F32)
    gbuf[group] = rows.astype(BF16)

    spread = []
    for k in range(1, 8):
        copy = remote(gbuf.at[group], gbuf.at[group], gg_send.at[k], gg_recv.at[k], g_peer[k - 1])
        copy.start()
        spread.append(copy)
    block = jnp.int32(0)
    for b in range(8):
        block = jnp.where(owner_ref[b] == group, b, block)
    for copy in spread:
        copy.wait_recv()
    grad_ref[z] = gbuf[block]
    ring = Ring(lambda i: grad_ref.at[i], zz_send, zz_recv, (z_peer[0], z_peer[6]), z)
    for step in range(4):
        ring.start(step)
        ring.arrived(step)

    ring.drain()
    stats.drain()
    for copy in spread + sums + passed + [x_copy, own_up, own_down, pair_up, pair_down]:
        copy.wait_send()

    @pl.when(stray)
    def _():
        a1_copy.wait_send()

    @pl.when(same)
    def _():
        for k in range(4):
            a_send(k, k, partner).wait_send()
            a_send(k, 4 + k, twin).wait_send()
            a_send(k, 8 + k, twin).wait_send()

    @pl.when(root)
    def _():
        for k in range(4):
            a_send(k, 12 + k, outer).wait_send()


def gather_gradient(activations, grad_out, stat_rows, owner_map):
    dma = pltpu.SemaphoreType.DMA
    return pl.pallas_call(
        gather_kernel,
        out_shape=(
            jax.ShapeDtypeStruct((8, 80, 640), BF16),
            jax.ShapeDtypeStruct((8, 160, 640), BF16),
        ),
        in_specs=[VMEM, VMEM, VMEM, SMEM],
        out_specs=(VMEM, VMEM),
        scratch_shapes=[
            pltpu.VMEM((8, 256, 640), BF16),
            pltpu.VMEM((8, 256, 640), BF16),
            pltpu.VMEM((640, 640), F32),
            pltpu.VMEM((8, 80, 640), BF16),
            pltpu.VMEM((8, 80, 640), BF16),
            pltpu.VMEM((8, 80, 640), BF16),
            dma((2,)), dma, dma((16,)), dma((8,)), dma((4,)), dma((4,)), dma((4,)), dma((4,)),
            dma((7,)), dma((7,)), dma((8,)), dma((8,)), dma((8,)), dma((8,)), dma((7,)), dma((7,)),
            dma((2,)),
        ],
        compiler_params=pltpu.CompilerParams(
            collective_id=0, has_side_effects=True, vmem_limit_bytes=48 * 2**20
        ),
        name="gather_gradient",
    )(activations, grad_out, stat_rows, owner_map)


def dot(a, b):
    return jnp.dot(a, b, preferred_element_type=F32)


def root_kernel(
    grad_ref, stats_ref, old_ref, stats_out, roots_out, update_out,
    both, moment, wide, low1, low2, low3, low_w, scales,
):
    z = lax.rem(lax.axis_index("dp"), 8)
    side = z // 4
    quarter = pl.multiple_of(lax.rem(z, 4) * 160, 16)
    eighth = pl.multiple_of(z * 80, 16)
    both[0] = grad_ref[...]
    both[1] = grad_ref[...].astype(F32).T.astype(BF16)

    own = dot(both[side, pl.ds(quarter, 160), :], both[1 - side])
    stats_out[...] = BETA * old_ref[...] + (1.0 - BETA) * own

    def start(s, carry):
        a = BETA * stats_ref[s].astype(F32) + (1.0 - BETA) * dot(both[s], both[1 - s])
        moment[s] = a
        norm = jnp.sqrt(jnp.sum(a * a, keepdims=True))
        scale = 2.5 / norm
        scales[s] = jnp.broadcast_to(jnp.sqrt(jnp.sqrt(scale)), (8, 128))
        m = moment[s] * scale
        moment[s] = m
        low1[s] = m.astype(BF16)
        return carry

    lax.fori_loop(0, 2, start, 0)

    def advance(now, later):
        def square(s, carry):
            w = dot(now[s], now[s]) - 10.0 * moment[s]
            wide[s] = w
            low_w[s] = w.astype(BF16)
            return carry

        def fourth(s, carry):
            h = dot(low_w[s], low_w[s]) + 50.0 * wide[s]
            wide[s] = h
            return carry

        def finish(s, carry):
            m = (625.0 * moment[s] + dot(now[s], wide[s].astype(BF16))) * (1.0 / 256.0)
            moment[s] = m
            later[s] = m.astype(BF16)
            return carry

        lax.fori_loop(0, 2, square, 0)
        lax.fori_loop(0, 2, fourth, 0)
        lax.fori_loop(0, 2, finish, 0)

    advance(low1, low2)
    advance(low2, low3)

    def factor(r, low, s):
        return 1.25 * r - 0.25 * dot(r.astype(BF16), low[s])

    def chain(r, s):
        r = factor(r, low2, s)
        r = factor(r, low3, s)
        t = r
        for _ in range(4):
            t = factor(t, low3, s)
        return 1.25 * r - 0.25 * dot(t.astype(BF16), low3[s])

    def identity(rows, offset):
        across = lax.broadcasted_iota(jnp.int32, (rows, 640), 1)
        down = lax.broadcasted_iota(jnp.int32, (rows, 640), 0) + offset
        return (across == down).astype(F32)

    def first(rows, offset, s):
        m = low1[s, pl.ds(offset, rows), :].astype(F32)
        return (1.25 * identity(rows, offset) - 0.25 * m) * scales[s, 0:1, 0:1]

    roots_out[...] = chain(first(160, quarter, side), side).astype(BF16)
    left = chain(first(80, eighth, 0), 0)
    high = left.astype(BF16)
    low = (left - high.astype(F32)).astype(BF16)
    y = dot(high, both[0]) + dot(low, both[0])
    y = factor(y, low1, 1) * scales[1, 0:1, 0:1]
    update_out[...] = chain(y, 1).astype(BF16)


def compute_roots(grad, stats, old_rows):
    return pl.pallas_call(
        root_kernel,
        out_shape=(
            jax.ShapeDtypeStruct((160, 640), F32),
            jax.ShapeDtypeStruct((160, 640), BF16),
            jax.ShapeDtypeStruct((80, 640), BF16),
        ),
        in_specs=[VMEM, VMEM, VMEM],
        out_specs=(VMEM, VMEM, VMEM),
        scratch_shapes=[
            pltpu.VMEM((2, 640, 640), BF16),
            pltpu.VMEM((2, 640, 640), F32),
            pltpu.VMEM((2, 640, 640), F32),
            pltpu.VMEM((2, 640, 640), BF16),
            pltpu.VMEM((2, 640, 640), BF16),
            pltpu.VMEM((2, 640, 640), BF16),
            pltpu.VMEM((2, 640, 640), BF16),
            pltpu.VMEM((2, 8, 128), F32),
        ],
        compiler_params=pltpu.CompilerParams(vmem_limit_bytes=48 * 2**20),
        name="compute_roots",
    )(grad, stats, old_rows)


def spread_kernel(
    piece_ref, root_ref, rotation_ref, update_ref, roots_out, rot0, rot1, rot2,
    a_send, a_recv, az_send, az_recv, bz_send, bz_recv,
    x_send, x_recv, y_send, y_recv, f_send, f_recv, c_send, c_recv, rot_send, rot_recv,
):
    x_lo, y, z, x_hi, core = place()
    group = x_lo * 4 + y
    other_x = 1 - x_lo
    pair = other_x * 4 + y
    y_up, y_down, y_far = lax.rem(y + 1, 4), lax.rem(y + 3, 4), lax.rem(y + 2, 4)
    partner = device(other_x, y, z, x_hi, core)
    up_y = device(x_lo, y_up, z, x_hi, core)
    down_y = device(x_lo, y_down, z, x_hi, core)
    up_z = device(x_lo, y, lax.rem(z + 1, 8), x_hi, core)
    down_z = device(x_lo, y, lax.rem(z + 7, 8), x_hi, core)
    g_peer = []
    for k in range(1, 8):
        g = lax.rem(group + k, 8)
        g_peer.append(device(g // 4, lax.rem(g, 4), z, x_hi, core))
    greet(g_peer + [up_z, down_z])

    update_ref[group, z] = piece_ref[...]
    rots = (rot0, rot1, rot2)
    rot0[0] = root_ref[...]

    ring_b = Ring(
        lambda i: update_ref.at[group, i, pl.ds(32, 48)], bz_send, bz_recv, (up_z, down_z), z
    )
    ring_a = Ring(lambda i: update_ref.at[:, i, pl.ds(0, 32)], az_send, az_recv, (up_z, down_z), z)
    ring_b.start(0)
    over = []
    for k in range(1, 8):
        own = update_ref.at[group, z, pl.ds(0, 32)]
        copy = remote(own, own, a_send.at[k], a_recv.at[k], g_peer[k - 1])
        copy.start()
        over.append(copy)

    def rotate(step):
        return remote(
            rots[step].at[0], rots[step].at[1], rot_send.at[step], rot_recv.at[step],
            g_peer[(1 << step) - 1],
        )

    def rotated(step):
        rotate(step).wait_recv()
        bit = lax.rem(rotation_ref[0] // (1 << step), 2)
        return rots[step][bit]

    rotate(0).start()
    ring_b.arrived(0)
    ring_b.start(1)
    ring_b.arrived(1)
    ring_b.start(2)
    for copy in over:
        copy.wait_recv()
    ring_a.start(0)
    ring_b.arrived(2)
    ring_b.start(3)
    ring_b.arrived(3)

    def rows(g, start, count, z0=0, zs=8):
        return update_ref.at[g, pl.ds(z0, zs), pl.ds(start, count)]

    def send(ref, sems, index, peer):
        copy = remote(ref, ref, sems[0].at[index], sems[1].at[index], peer)
        copy.start()
        return copy

    def landed(ref, sems, index):
        remote(ref, ref, sems[0].at[index], sems[1].at[index], partner).wait_recv()

    ys, fs, cs, xs = (y_send, y_recv), (f_send, f_recv), (c_send, c_recv), (x_send, x_recv)
    sent = []
    sent.append(send(rows(group, 32, 48), xs, 0, partner))
    sent.append(send(rows(group, 32, 48), ys, 0, up_y))
    sent.append(send(rows(group, 32, 48), ys, 1, down_y))

    rot1[0] = rotated(0)
    rotate(1).start()
    ring_a.arrived(0)
    ring_a.start(1)

    landed(rows(pair, 32, 48), xs, 0)
    sent.append(send(rows(pair, 32, 32), ys, 2, up_y))
    sent.append(send(rows(pair, 32, 32), ys, 3, down_y))

    low, high, far = x_lo * 4 + y_down, x_lo * 4 + y_up, x_lo * 4 + y_far
    landed(rows(low, 32, 48), ys, 0)
    sent.append(send(rows(low, 32, 48, 0, 4), fs, 0, up_y))
    sent.append(send(rows(low, 64, 16), cs, 0, partner))
    landed(rows(high, 32, 48), ys, 1)
    sent.append(send(rows(high, 32, 48, 4, 4), fs, 1, down_y))
    sent.append(send(rows(high, 64, 16), cs, 1, partner))

    ring_a.arrived(1)
    ring_a.start(2)
    rot2[0] = rotated(1)
    rotate(2).start()

    p_low, p_high, p_far = other_x * 4 + y_down, other_x * 4 + y_up, other_x * 4 + y_far
    landed(rows(p_low, 32, 32), ys, 2)
    sent.append(send(rows(p_low, 32, 32, 0, 4), fs, 2, up_y))
    landed(rows(p_high, 32, 32), ys, 3)
    sent.append(send(rows(p_high, 32, 32, 4, 4), fs, 3, down_y))
    landed(rows(far, 32, 48, 0, 4), fs, 0)
    landed(rows(far, 32, 48, 4, 4), fs, 1)
    sent.append(send(rows(far, 64, 16), cs, 2, partner))

    ring_a.arrived(2)
    ring_a.start(3)
    roots_out[...] = rotated(2).astype(F32)

    landed(rows(p_low, 64, 16), cs, 0)
    landed(rows(p_high, 64, 16), cs, 1)
    landed(rows(p_far, 32, 32, 0, 4), fs, 2)
    landed(rows(p_far, 32, 32, 4, 4), fs, 3)
    landed(rows(p_far, 64, 16), cs, 2)
    ring_a.arrived(3)

    ring_a.drain()
    ring_b.drain()
    for copy in sent + over:
        copy.wait_send()
    for step in range(3):
        rotate(step).wait_send()


def spread_update(piece, root_rows, rotation):
    dma = pltpu.SemaphoreType.DMA
    return pl.pallas_call(
        spread_kernel,
        out_shape=(
            jax.ShapeDtypeStruct((8, 8, 80, 640), BF16),
            jax.ShapeDtypeStruct((160, 640), F32),
        ),
        in_specs=[VMEM, VMEM, SMEM],
        out_specs=(VMEM, VMEM),
        scratch_shapes=[
            pltpu.VMEM((2, 160, 640), BF16),
            pltpu.VMEM((2, 160, 640), BF16),
            pltpu.VMEM((2, 160, 640), BF16),
            dma((8,)), dma((8,)), dma((7,)), dma((7,)), dma((7,)), dma((7,)),
            dma((1,)), dma((1,)), dma((4,)), dma((4,)), dma((4,)), dma((4,)),
            dma((3,)), dma((3,)), dma((3,)), dma((3,)),
        ],
        compiler_params=pltpu.CompilerParams(
            collective_id=1, has_side_effects=True, vmem_limit_bytes=48 * 2**20
        ),
        name="spread_update",
    )(piece, root_rows, rotation)


def order_kernel(owner_ref, in_ref, out_ref):
    out_ref[...] = in_ref[...]


def order_blocks(by_place, owner_map):
    return pl.pallas_call(
        order_kernel,
        out_shape=jax.ShapeDtypeStruct((8, 640, 640), BF16),
        grid_spec=pltpu.PrefetchScalarGridSpec(
            num_scalar_prefetch=1,
            grid=(8,),
            in_specs=[pl.BlockSpec((1, 640, 640), lambda b, owner: (owner[b], 0, 0))],
            out_specs=pl.BlockSpec((1, 640, 640), lambda b, owner: (b, 0, 0)),
        ),
        name="order_blocks",
    )(owner_map, by_place)


def local(activations, grad_out, stats_old, owner_map, rotation):
    old_rows = stats_old.reshape(160, 640)
    grad, stats = gather_gradient(activations, grad_out, old_rows.astype(BF16), owner_map)
    stats_new, root_rows, piece = compute_roots(
        grad.reshape(640, 640), stats.reshape(2, 640, 640), old_rows
    )
    by_place, roots_new = spread_update(piece, root_rows, rotation)
    update = order_blocks(by_place.reshape(8, 640, 640), owner_map)
    return (
        update.reshape(2, 2560, 640),
        stats_new.reshape(stats_old.shape),
        roots_new.reshape(stats_old.shape),
    )


def solution(mesh):
    return jax.shard_map(
        local,
        mesh=mesh,
        in_specs=(P("dp", "mp"), P("dp", "mp"), P("mp", None, "dp", None, None), P(), P()),
        out_specs=(
            P("mp", None, None),
            P("mp", None, "dp", None, None),
            P("mp", None, "dp", None, None),
        ),
        check_vma=False,
    )
```

```python
import jax
import jax.numpy as jnp
from jax import lax
from jax.experimental import pallas as pl
from jax.experimental.pallas import tpu as pltpu
from jax.sharding import PartitionSpec as P

BETA = 0.9
MESH = pl.DeviceIdType.MESH
VMEM = pl.BlockSpec(memory_space=pltpu.VMEM)
SMEM = pl.BlockSpec(memory_space=pltpu.SMEM)
F32 = jnp.float32
BF16 = jnp.bfloat16


def place():
    dp = lax.axis_index("dp")
    mp = lax.axis_index("mp")
    return dp // 32, lax.rem(dp // 8, 4), lax.rem(dp, 8), mp // 2, lax.rem(mp, 2)


def device(x_lo, y, z, x_hi, core):
    return {"dp": x_lo * 32 + y * 8 + z, "mp": x_hi * 2 + core}


def remote(src, dst, send, recv, peer):
    return pltpu.make_async_remote_copy(
        src_ref=src, dst_ref=dst, send_sem=send, recv_sem=recv, device_id=peer, device_id_type=MESH
    )


class Ring:
    def __init__(self, slot, send, recv, peers, z):
        self.slot, self.send, self.recv = slot, send, recv
        self.up, self.down = peers
        self.z = z

    def copy_up(self, step):
        i = lax.rem(self.z - step + 8, 8)
        return remote(self.slot(i), self.slot(i), self.send.at[step], self.recv.at[step], self.up)

    def copy_down(self, step):
        i = lax.rem(self.z + step, 8)
        return remote(
            self.slot(i), self.slot(i), self.send.at[4 + step], self.recv.at[4 + step], self.down
        )

    def start(self, step):
        self.copy_up(step).start()
        if step < 3:
            self.copy_down(step).start()

    def arrived(self, step):
        self.copy_up(step).wait_recv()
        if step < 3:
            self.copy_down(step).wait_recv()

    def drain(self):
        for step in range(4):
            self.copy_up(step).wait_send()
            if step < 3:
                self.copy_down(step).wait_send()


def swap(v):
    return lax.rem(v, 2) * 2 + v // 2


SWAP = (0, 2, 1, 3)
CHUNKS = ((0, 384), (384, 256))
OWN, PAIR, ON_OWN, ON_PAIR = range(4)


def gather_kernel(
    act_ref, gout_ref, old_ref, owner_ref, grad_ref, stats_ref,
    act_in, act_t, old_in, actg, goutg, total0, total1, part0, part1, rs0, rs1, gg0, gg1,
    x_send, x_recv, a1_sem, a2_send, a_recv, g_send, g_recv,
    st_send, st_recv, rs_send, rs_recv, gg_send, gg_recv, z0_send, z0_recv, z1_send, z1_recv,
    loc_sem,
):
    totals, parts, rss, ggs = (total0, total1), (part0, part1), (rs0, rs1), (gg0, gg1)
    x_lo, y, z, x_hi, core = place()
    mp = x_hi * 2 + core
    group = x_lo * 4 + y
    y_up, y_down, y_far = lax.rem(y + 1, 4), lax.rem(y + 3, 4), lax.rem(y + 2, 4)
    other_x = 1 - x_lo
    partner = device(other_x, y, z, x_hi, core)
    outer = device(other_x, y, z, 1 - x_hi, core)
    twin = device(x_lo, y, z, x_hi, 1 - core)
    z_peer = [device(x_lo, y, lax.rem(z + k, 8), x_hi, core) for k in range(1, 8)]
    y_peer = (device(x_lo, y_up, z, x_hi, core), device(x_lo, y_down, z, x_hi, core))
    g_peer = []
    for k in range(1, 8):
        g = lax.rem(group + k, 8)
        g_peer.append(device(g // 4, lax.rem(g, 4), z, x_hi, core))

    load_act = pltpu.make_async_copy(act_ref, act_in, loc_sem.at[0])
    load_act.start()
    load_old = pltpu.make_async_copy(old_ref, old_in, loc_sem.at[1])
    load_old.start()
    peers = z_peer + g_peer + [outer, twin]
    barrier = pltpu.get_barrier_semaphore()
    for peer in peers:
        pl.semaphore_signal(barrier, inc=1, device_id=peer, device_id_type=MESH)
    load_act.wait()
    act_t[...] = act_in[...].T
    load_old.wait()
    stats_ref[z] = old_in[...].astype(BF16)
    pl.semaphore_wait(barrier, len(peers))

    feature = swap(y)
    same = core == lax.rem(feature, 2)
    root = jnp.logical_and(same, x_hi == feature // 2)
    mid = jnp.logical_and(same, x_hi != feature // 2)
    stray = feature != mp

    def out_columns(side, chunk):
        offset, width = CHUNKS[chunk]
        return gout_ref.at[:, pl.ds(pl.multiple_of(side * 640 + offset, 128), width)]

    def g_slot(slot, chunk):
        offset, width = CHUNKS[chunk]
        return goutg.at[slot, :, pl.ds(offset, width)]

    def g_half(slot, chunk, way):
        offset, width = CHUNKS[chunk]
        return goutg.at[slot, pl.ds(way * 128, 128), pl.ds(offset, width)]

    def x_copy(chunk):
        return remote(
            out_columns(other_x, chunk), g_slot(group, chunk),
            x_send.at[chunk], x_recv.at[chunk], partner,
        )

    def x_landed(chunk):
        ref = g_slot(other_x * 4 + y, chunk)
        remote(ref, ref, x_send.at[chunk], x_recv.at[chunk], partner).wait_recv()

    def y_copy(chunk, kind, way):
        index = chunk * 8 + kind * 2 + way
        column = other_x if kind in (PAIR, ON_PAIR) else x_lo
        if kind in (OWN, PAIR):
            dst = g_slot(column * 4 + y, chunk)
            src = out_columns(x_lo, chunk) if kind == OWN else dst
        else:
            dst = g_half(column * 4 + (y_down if way == 0 else y_up), chunk, way)
            src = dst
        return remote(src, dst, g_send.at[index], g_recv.at[index], y_peer[way])

    def y_landed(chunk, kind, way):
        index = chunk * 8 + kind * 2 + way
        column = other_x if kind in (PAIR, ON_PAIR) else x_lo
        if kind in (OWN, PAIR):
            ref = g_slot(column * 4 + (y_down if way == 0 else y_up), chunk)
        else:
            ref = g_half(column * 4 + y_far, chunk, way)
        remote(ref, ref, g_send.at[index], g_recv.at[index], y_peer[way]).wait_recv()

    def y_send(chunk, kind):
        for way in range(2):
            if kind in (ON_OWN, ON_PAIR):
                y_landed(chunk, kind - 2, way)
            y_copy(chunk, kind, way).start()

    def a_slot(slot):
        return actg.at[:, pl.ds(pl.multiple_of(slot * 256, 256), 256)]

    def a_landed(slot):
        remote(a_slot(slot), a_slot(slot), a1_sem, a_recv.at[slot], partner).wait_recv()

    def a_send(slot, index, peer, src=None):
        src = a_slot(slot) if src is None else src
        return remote(src, a_slot(slot), a2_send.at[index], a_recv.at[slot], peer)

    arrivals = (y, y_down, y_up, y_far)
    a1_copy = remote(
        act_t, a_slot(group), a1_sem, a_recv.at[group], device(x_lo, swap(mp), z, x_hi, core)
    )

    def from_root(i):
        slot = x_lo * 4 + arrivals[i]
        if i > 0:
            a_landed(slot)
        src = act_t if i == 0 else None
        a_send(slot, i, partner, src).start()
        a_send(slot, 12 + i, outer, src).start()
        a_send(slot, 4 + i, twin, src).start()

    def from_mid(i):
        slot = other_x * 4 + arrivals[i]
        a_landed(slot)
        a_send(slot, i, partner).start()
        a_send(slot, 4 + i, twin).start()

    stats = Ring(lambda i: stats_ref.at[i], st_send, st_recv, (z_peer[0], z_peer[6]), z)

    pl.when(stray)(lambda: a1_copy.start())
    x_copy(0).start()
    pl.when(root)(lambda: from_root(0))
    y_send(0, OWN)
    stats.start(0)
    x_copy(1).start()
    keep = pltpu.make_async_copy(
        gout_ref.at[:, pl.ds(pl.multiple_of(x_lo * 640, 128), 640)], goutg.at[group], loc_sem.at[2]
    )
    keep.start()

    @pl.when(jnp.logical_not(stray))
    def _():
        actg[:, pl.ds(pl.multiple_of(group * 256, 256), 256)] = act_t[...]

    pl.when(root)(lambda: from_root(1))
    x_landed(0)
    y_send(0, PAIR)
    stats.arrived(0)
    stats.start(1)

    @pl.when(root)
    def _():
        from_root(2)
        from_root(3)

    pl.when(mid)(lambda: from_mid(0))
    y_send(1, OWN)
    x_landed(1)
    y_send(1, PAIR)
    y_send(0, ON_OWN)
    pl.when(mid)(lambda: from_mid(1))
    stats.arrived(1)
    stats.start(2)
    y_send(0, ON_PAIR)
    pl.when(mid)(lambda: from_mid(2))
    stats.arrived(2)
    stats.start(3)
    y_send(1, ON_OWN)
    pl.when(mid)(lambda: from_mid(3))
    y_send(1, ON_PAIR)

    first = jnp.where(root, x_lo, other_x)

    @pl.when(same)
    def _():
        for i in range(4):
            slot = (1 - first) * 4 + arrivals[i]
            a_landed(slot)
            a_send(slot, 8 + i, twin).start()

    @pl.when(jnp.logical_not(same))
    def _():
        for slot in range(8):
            a_landed(slot)

    keep.wait()

    def z_sum(chunk):
        offset, width = CHUNKS[chunk]
        for kind in (ON_OWN, ON_PAIR):
            for way in range(2):
                y_landed(chunk, kind, way)
        right = goutg[:, :, offset : offset + width].reshape(2048, width)
        product = jnp.dot(actg[...], right, preferred_element_type=F32)
        totals[chunk][...] = product
        parts[chunk][...] = product.astype(BF16).reshape(8, 80, width)
        sent = []
        for k in range(1, 8):
            to = lax.rem(z + k, 8)
            copy = remote(
                parts[chunk].at[to], rss[chunk].at[k],
                rs_send.at[chunk * 8 + k], rs_recv.at[chunk * 8 + k], z_peer[k - 1],
            )
            copy.start()
            sent.append(copy)
        return sent

    def group_spread(chunk, sums):
        rows = totals[chunk][pl.ds(pl.multiple_of(z * 80, 8), 80), :]
        for k in range(1, 8):
            sums[k - 1].wait_recv()
            rows = rows + rss[chunk][k].astype(F32)
        ggs[chunk][group] = rows.astype(BF16)
        sent = []
        for k in range(1, 8):
            own = ggs[chunk].at[group]
            copy = remote(
                own, own, gg_send.at[chunk * 8 + k], gg_recv.at[chunk * 8 + k], g_peer[k - 1]
            )
            copy.start()
            sent.append(copy)
        return sent

    block = jnp.int32(0)
    for b in range(8):
        block = jnp.where(owner_ref[b] == group, b // 4 * 4 + SWAP[b % 4], block)

    def pick(chunk, spread):
        offset, width = CHUNKS[chunk]
        for copy in spread:
            copy.wait_recv()
        grad_ref[z, :, offset : offset + width] = ggs[chunk][block]
        sems = ((z0_send, z0_recv), (z1_send, z1_recv))[chunk]
        ring = Ring(
            lambda i: grad_ref.at[i, :, pl.ds(offset, width)], *sems, (z_peer[0], z_peer[6]), z
        )
        ring.start(0)
        return ring

    sums0 = z_sum(0)
    sums1 = z_sum(1)
    stats.arrived(3)
    spread0 = group_spread(0, sums0)
    ring0 = pick(0, spread0)
    spread1 = group_spread(1, sums1)
    ring0.arrived(0)
    ring0.start(1)
    ring1 = pick(1, spread1)
    ring0.arrived(1)
    ring0.start(2)
    ring1.arrived(0)
    ring1.start(1)
    ring0.arrived(2)
    ring0.start(3)
    ring1.arrived(1)
    ring1.start(2)
    ring0.arrived(3)
    ring1.arrived(2)
    ring1.start(3)
    ring1.arrived(3)

    ring0.drain()
    ring1.drain()
    stats.drain()
    for copy in spread0 + spread1 + sums0 + sums1 + [x_copy(0), x_copy(1)]:
        copy.wait_send()
    for chunk in range(2):
        for kind in range(4):
            for way in range(2):
                y_copy(chunk, kind, way).wait_send()

    pl.when(stray)(lambda: a1_copy.wait_send())

    @pl.when(same)
    def _():
        for k in range(4):
            a_send(k, k, partner).wait_send()
            a_send(k, 4 + k, twin).wait_send()
            a_send(k, 8 + k, twin).wait_send()

    @pl.when(root)
    def _():
        for k in range(4):
            a_send(k, 12 + k, outer).wait_send()


def gather_gradient(activations, grad_out, old_rows, owner_map):
    dma = pltpu.SemaphoreType.DMA
    hbm = pl.BlockSpec(memory_space=pl.ANY)
    widths = [width for _, width in CHUNKS]
    return pl.pallas_call(
        gather_kernel,
        out_shape=(
            jax.ShapeDtypeStruct((8, 80, 640), BF16),
            jax.ShapeDtypeStruct((8, 160, 640), BF16),
        ),
        in_specs=[hbm, hbm, hbm, SMEM],
        out_specs=(VMEM, VMEM),
        scratch_shapes=[
            pltpu.VMEM((256, 640), BF16),
            pltpu.VMEM((640, 256), BF16),
            pltpu.VMEM((160, 640), F32),
            pltpu.VMEM((640, 2048), BF16),
            pltpu.VMEM((8, 256, 640), BF16),
            *[pltpu.VMEM((640, width), F32) for width in widths],
            *[pltpu.VMEM((8, 80, width), BF16) for _ in range(3) for width in widths],
            dma((2,)), dma((2,)), dma, dma((16,)), dma((8,)), dma((16,)), dma((16,)),
            dma((7,)), dma((7,)), dma((16,)), dma((16,)), dma((16,)), dma((16,)),
            dma((7,)), dma((7,)), dma((7,)), dma((7,)), dma((3,)),
        ],
        compiler_params=pltpu.CompilerParams(
            collective_id=0, has_side_effects=True, vmem_limit_bytes=32 * 2**20
        ),
        name="gather_gradient",
    )(activations, grad_out, old_rows, owner_map)


def dot(a, b):
    return jnp.dot(a, b, preferred_element_type=F32)


def finish_kernel(
    grad_ref, stats_ref, old_ref, rotation_ref, update_ref, stats_out, roots_out,
    both, moment, wide, low1, low2, low3, low_w, scales, rot0, rot1, rot2,
    a_send, a_recv, az_send, az_recv, ay_send, ay_recv, bz_send, bz_recv,
    x_send, x_recv, y_send, y_recv, p_send, p_recv, f_send, f_recv, q_send, q_recv,
    c_send, c_recv, rot_send, rot_recv,
):
    x_lo, y, z, x_hi, core = place()
    group = x_lo * 4 + y
    other_x = 1 - x_lo
    pair = other_x * 4 + y
    y_up, y_down, y_far = lax.rem(y + 1, 4), lax.rem(y + 3, 4), lax.rem(y + 2, 4)
    partner = device(other_x, y, z, x_hi, core)
    up_y = device(x_lo, y_up, z, x_hi, core)
    down_y = device(x_lo, y_down, z, x_hi, core)
    up_z = device(x_lo, y, lax.rem(z + 1, 8), x_hi, core)
    down_z = device(x_lo, y, lax.rem(z + 7, 8), x_hi, core)
    g_peer = []
    for k in range(1, 8):
        g = lax.rem(group + k, 8)
        g_peer.append(device(g // 4, lax.rem(g, 4), z, x_hi, core))
    peers = g_peer + [up_z, down_z]
    barrier = pltpu.get_barrier_semaphore()
    for peer in peers:
        pl.semaphore_signal(barrier, inc=1, device_id=peer, device_id_type=MESH)

    rots = (rot0, rot1, rot2)

    def rotate(step):
        return remote(
            rots[step].at[0], rots[step].at[1], rot_send.at[step], rot_recv.at[step],
            g_peer[(1 << step) - 1],
        )

    def rotated(step):
        rotate(step).wait_recv()
        bit = lax.rem(rotation_ref[0] // (1 << step), 2)
        return rots[step][bit]

    side = z // 4
    quarter = pl.multiple_of(lax.rem(z, 4) * 160, 16)
    eighth = pl.multiple_of(z * 80, 16)
    grad = grad_ref[...].reshape(640, 640)
    both[0] = grad
    both[1] = grad.T

    own = dot(both[side, pl.ds(quarter, 160), :], both[1 - side])
    stats_out[...] = BETA * old_ref[...] + (1.0 - BETA) * own

    def start(s, carry):
        a = BETA * stats_ref[s].astype(F32) + (1.0 - BETA) * dot(both[s], both[1 - s])
        moment[s] = a
        norm = jnp.sqrt(jnp.sum(a * a, keepdims=True))
        scale = 2.5 / norm
        scales[s] = jnp.broadcast_to(jnp.sqrt(jnp.sqrt(scale)), (8, 128))
        m = moment[s] * scale
        moment[s] = m
        low1[s] = m.astype(BF16)
        return carry

    lax.fori_loop(0, 2, start, 0)

    def advance(now, later):
        def square(s, carry):
            w = dot(now[s], now[s]) - 10.0 * moment[s]
            wide[s] = w
            low_w[s] = w.astype(BF16)
            return carry

        def fourth(s, carry):
            h = dot(low_w[s], low_w[s]) + 50.0 * wide[s]
            wide[s] = h
            return carry

        def finish(s, carry):
            m = (625.0 * moment[s] + dot(now[s], wide[s].astype(BF16))) * (1.0 / 256.0)
            moment[s] = m
            later[s] = m.astype(BF16)
            return carry

        lax.fori_loop(0, 2, square, 0)
        lax.fori_loop(0, 2, fourth, 0)
        lax.fori_loop(0, 2, finish, 0)

    advance(low1, low2)
    advance(low2, low3)

    def factor(r, low, s):
        return 1.25 * r - 0.25 * dot(r.astype(BF16), low[s])

    def chain(r, s):
        r = factor(r, low2, s)
        r = factor(r, low3, s)
        t = r
        for _ in range(4):
            t = factor(t, low3, s)
        return 1.25 * r - 0.25 * dot(t.astype(BF16), low3[s])

    def identity(rows, offset):
        across = lax.broadcasted_iota(jnp.int32, (rows, 640), 1)
        down = lax.broadcasted_iota(jnp.int32, (rows, 640), 0) + offset
        return (across == down).astype(F32)

    def first(rows, offset, s):
        m = low1[s, pl.ds(offset, rows), :].astype(F32)
        return (1.25 * identity(rows, offset) - 0.25 * m) * scales[s, 0:1, 0:1]

    rot0[0] = chain(first(160, quarter, side), side).astype(BF16)
    pl.semaphore_wait(barrier, len(peers))
    rotate(0).start()
    left = chain(first(80, eighth, 0), 0)
    rot1[0] = rotated(0)
    rotate(1).start()
    high = left.astype(BF16)
    low = (left - high.astype(F32)).astype(BF16)
    right = dot(high, both[0]) + dot(low, both[0])
    right = factor(right, low1, 1) * scales[1, 0:1, 0:1]
    right = chain(right, 1)
    rot2[0] = rotated(1)
    rotate(2).start()
    update_ref[group, z] = right.astype(BF16)

    def slot(r):
        return lax.rem(z + r, 8)

    def rows(g, r, start, count):
        return update_ref.at[g, slot(r), pl.ds(start, count)]

    sent = []

    def send(ref, sems, index, peer):
        copy = remote(ref, ref, sems[0].at[index], sems[1].at[index], peer)
        copy.start()
        sent.append(copy)

    def landed(ref, sems, index):
        remote(ref, ref, sems[0].at[index], sems[1].at[index], partner).wait_recv()

    xs, ys, ps = (x_send, x_recv), (y_send, y_recv), (p_send, p_recv)
    fs, qs, cs = (f_send, f_recv), (q_send, q_recv), (c_send, c_recv)
    low, high, far = x_lo * 4 + y_down, x_lo * 4 + y_up, x_lo * 4 + y_far
    p_low, p_high, p_far = other_x * 4 + y_down, other_x * 4 + y_up, other_x * 4 + y_far

    ring_b = Ring(
        lambda i: update_ref.at[group, i, pl.ds(32, 48)], bz_send, bz_recv, (up_z, down_z), z
    )
    ring_a = Ring(
        lambda i: update_ref.at[pl.ds(0, 4), i, pl.ds(0, 32)], az_send, az_recv, (up_z, down_z), z
    )
    ring_c = Ring(
        lambda i: update_ref.at[pl.ds(4, 4), i, pl.ds(0, 32)], ay_send, ay_recv, (up_z, down_z), z
    )

    def own_out(r):
        send(rows(group, r, 32, 48), xs, r, partner)
        send(rows(group, r, 32, 48), ys, r, up_y)
        send(rows(group, r, 32, 48), ys, 8 + r, down_y)

    def pair_out(r):
        landed(rows(pair, r, 32, 48), xs, r)
        send(rows(pair, r, 32, 32), ps, r, up_y)
        send(rows(pair, r, 32, 32), ps, 8 + r, down_y)

    def own_on(r):
        landed(rows(low, r, 32, 48), ys, r)
        if r < 4:
            send(rows(low, r, 32, 48), fs, r, up_y)
        landed(rows(high, r, 32, 48), ys, 8 + r)
        if r >= 4:
            send(rows(high, r, 32, 48), fs, r, down_y)

    def pair_on(r):
        landed(rows(p_low, r, 32, 32), ps, r)
        if r < 4:
            send(rows(p_low, r, 32, 32), qs, r, up_y)
        landed(rows(p_high, r, 32, 32), ps, 8 + r)
        if r >= 4:
            send(rows(p_high, r, 32, 32), qs, r, down_y)

    def across(g, index):
        send(update_ref.at[g, :, pl.ds(64, 16)], cs, index, partner)

    ring_b.start(0)
    over = []
    for k in range(1, 8):
        own = update_ref.at[group, z, pl.ds(0, 32)]
        copy = remote(own, own, a_send.at[k], a_recv.at[k], g_peer[k - 1])
        copy.start()
        over.append(copy)
    own_out(0)

    ring_b.arrived(0)
    ring_b.start(1)
    own_out(7)
    own_out(1)
    pair_out(0)
    ring_b.arrived(1)
    ring_b.start(2)
    own_out(6)
    own_out(2)
    for copy in over:
        copy.wait_recv()
    ring_a.start(0)
    ring_c.start(0)
    pair_out(7)
    pair_out(1)
    ring_b.arrived(2)
    ring_b.start(3)
    own_out(5)
    own_out(3)
    own_on(0)
    pair_out(6)
    pair_out(2)
    ring_b.arrived(3)
    own_out(4)
    own_on(7)
    own_on(1)
    pair_out(5)
    pair_out(3)
    ring_a.arrived(0)
    ring_a.start(1)
    ring_c.arrived(0)
    ring_c.start(1)
    own_on(6)
    own_on(2)
    pair_out(4)
    own_on(5)
    own_on(3)
    own_on(4)
    across(low, 0)
    across(high, 1)
    pair_on(0)
    pair_on(7)
    pair_on(1)
    ring_a.arrived(1)
    ring_a.start(2)
    ring_c.arrived(1)
    ring_c.start(2)
    for r in (6, 2, 5, 3, 4):
        pair_on(r)
    for r in range(8):
        landed(rows(far, r, 32, 48), fs, r)
    across(far, 2)
    ring_a.arrived(2)
    ring_a.start(3)
    ring_c.arrived(2)
    ring_c.start(3)
    roots_out[...] = rotated(2).astype(F32)
    for r in range(8):
        landed(rows(p_far, r, 32, 32), qs, r)
    for index, g in enumerate((p_low, p_high, p_far)):
        landed(update_ref.at[g, :, pl.ds(64, 16)], cs, index)
    ring_a.arrived(3)
    ring_c.arrived(3)

    ring_a.drain()
    ring_b.drain()
    ring_c.drain()
    for copy in sent + over:
        copy.wait_send()
    for step in range(3):
        rotate(step).wait_send()


def finish(grad, stats, old_rows, rotation):
    dma = pltpu.SemaphoreType.DMA
    return pl.pallas_call(
        finish_kernel,
        out_shape=(
            jax.ShapeDtypeStruct((8, 8, 80, 640), BF16),
            jax.ShapeDtypeStruct((160, 640), F32),
            jax.ShapeDtypeStruct((160, 640), F32),
        ),
        in_specs=[VMEM, VMEM, VMEM, SMEM],
        out_specs=(VMEM, VMEM, VMEM),
        scratch_shapes=[
            pltpu.VMEM((2, 640, 640), BF16),
            pltpu.VMEM((2, 640, 640), F32),
            pltpu.VMEM((2, 640, 640), F32),
            pltpu.VMEM((2, 640, 640), BF16),
            pltpu.VMEM((2, 640, 640), BF16),
            pltpu.VMEM((2, 640, 640), BF16),
            pltpu.VMEM((2, 640, 640), BF16),
            pltpu.VMEM((2, 8, 128), F32),
            pltpu.VMEM((2, 160, 640), BF16),
            pltpu.VMEM((2, 160, 640), BF16),
            pltpu.VMEM((2, 160, 640), BF16),
            dma((8,)), dma((8,)), dma((7,)), dma((7,)), dma((7,)), dma((7,)), dma((7,)), dma((7,)),
            dma((8,)), dma((8,)), dma((16,)), dma((16,)), dma((16,)), dma((16,)),
            dma((8,)), dma((8,)), dma((8,)), dma((8,)), dma((3,)), dma((3,)), dma((3,)), dma((3,)),
        ],
        compiler_params=pltpu.CompilerParams(
            collective_id=1, has_side_effects=True, vmem_limit_bytes=36 * 2**20
        ),
        name="finish",
    )(grad, stats, old_rows, rotation)


def order_kernel(owner_ref, in_ref, out_ref, sems):
    copies = []
    for b in range(8):
        copy = pltpu.make_async_copy(in_ref.at[owner_ref[b]], out_ref.at[b], sems.at[b])
        copy.start()
        copies.append(copy)
    for copy in copies:
        copy.wait()


def order_blocks(by_place, owner_map):
    return pl.pallas_call(
        order_kernel,
        out_shape=jax.ShapeDtypeStruct((8, 640, 640), BF16),
        in_specs=[SMEM, VMEM],
        out_specs=pl.BlockSpec(memory_space=pl.ANY),
        scratch_shapes=[pltpu.SemaphoreType.DMA((8,))],
        compiler_params=pltpu.CompilerParams(vmem_limit_bytes=16 * 2**20),
        name="order_blocks",
    )(owner_map, by_place)


def local(activations, grad_out, stats_old, owner_map, rotation):
    old_rows = stats_old.reshape(160, 640)
    grad, stats = gather_gradient(activations, grad_out, old_rows, owner_map)
    by_place, stats_new, roots_new = finish(
        grad, stats.reshape(2, 640, 640), old_rows, rotation
    )
    update = order_blocks(by_place.reshape(8, 640, 640), owner_map)
    return (
        update.reshape(2, 2560, 640),
        stats_new.reshape(stats_old.shape),
        roots_new.reshape(stats_old.shape),
    )


def solution(mesh):
    return jax.shard_map(
        local,
        mesh=mesh,
        in_specs=(P("dp", "mp"), P("dp", "mp"), P("mp", None, "dp", None, None), P(), P()),
        out_specs=(
            P("mp", None, None),
            P("mp", None, "dp", None, None),
            P("mp", None, "dp", None, None),
        ),
        check_vma=False,
    )
```

```python
import jax
import jax.numpy as jnp
from jax import lax
from jax.experimental import pallas as pl
from jax.experimental.pallas import tpu as pltpu
from jax.sharding import PartitionSpec as P

BETA = 0.9
MESH = pl.DeviceIdType.MESH
VMEM = pl.BlockSpec(memory_space=pltpu.VMEM)
SMEM = pl.BlockSpec(memory_space=pltpu.SMEM)
F32 = jnp.float32
BF16 = jnp.bfloat16


def place():
    dp = lax.axis_index("dp")
    mp = lax.axis_index("mp")
    return dp // 32, lax.rem(dp // 8, 4), lax.rem(dp, 8), mp // 2, lax.rem(mp, 2)


def device(x_lo, y, z, x_hi, core):
    return {"dp": x_lo * 32 + y * 8 + z, "mp": x_hi * 2 + core}


def remote(src, dst, send, recv, peer):
    return pltpu.make_async_remote_copy(
        src_ref=src, dst_ref=dst, send_sem=send, recv_sem=recv, device_id=peer, device_id_type=MESH
    )


class Ring:
    def __init__(self, slot, send, recv, peers, z):
        self.slot, self.send, self.recv = slot, send, recv
        self.up, self.down = peers
        self.z = z

    def copy_up(self, step):
        i = lax.rem(self.z - step + 8, 8)
        return remote(self.slot(i), self.slot(i), self.send.at[step], self.recv.at[step], self.up)

    def copy_down(self, step):
        i = lax.rem(self.z + step, 8)
        return remote(
            self.slot(i), self.slot(i), self.send.at[4 + step], self.recv.at[4 + step], self.down
        )

    def start(self, step):
        self.copy_up(step).start()
        if step < 3:
            self.copy_down(step).start()

    def arrived(self, step):
        self.copy_up(step).wait_recv()
        if step < 3:
            self.copy_down(step).wait_recv()

    def drain(self):
        for step in range(4):
            self.copy_up(step).wait_send()
            if step < 3:
                self.copy_down(step).wait_send()


class Near:
    def __init__(self, piece, send, recv, peers, z):
        self.piece, self.send, self.recv, self.peers = piece, send, recv, peers
        self.z = z

    def copy(self, index):
        ahead, behind, part = (
            (2, 0, 0), (-2, 0, 0), (1, 0, 0), (-1, 0, 0), (1, 2, 0), (-1, 2, 0), (2, 2, 1), (-2, 2, 2)
        )[index]
        way = 1 if ahead > 0 else -1
        ref = self.piece(lax.rem(self.z - way * behind + 8, 8), part)
        return remote(ref, ref, self.send.at[index], self.recv.at[index], self.peers[ahead % 8 - 1])

    def landed(self, index):
        ahead, behind, part = (
            (2, 0, 0), (-2, 0, 0), (1, 0, 0), (-1, 0, 0), (1, 2, 0), (-1, 2, 0), (2, 2, 1), (-2, 2, 2)
        )[index]
        way = 1 if ahead > 0 else -1
        ref = self.piece(lax.rem(self.z - ahead - way * behind + 8, 8), part)
        remote(ref, ref, self.send.at[index], self.recv.at[index], self.peers[0]).wait_recv()

    def start(self):
        for index in range(4):
            self.copy(index).start()

    def relay(self):
        for index in (0, 1):
            self.landed(index)
            self.copy(4 + index).start()
            self.copy(6 + index).start()

    def finish(self):
        for index in (2, 3, 4, 5, 6, 7):
            self.landed(index)

    def drain(self):
        for index in range(8):
            self.copy(index).wait_send()


def swap(v):
    return lax.rem(v, 2) * 2 + v // 2


SWAP = (0, 2, 1, 3)
CHUNKS = ((0, 384), (384, 256))
OWN, PAIR, ON_OWN, ON_PAIR = range(4)


def gather_part(
    act_ref, gout_ref, old_ref, owner_ref, grad_ref, stats_ref, old_in,
    act_in, act_t, actg, goutg, total0, total1, part0, part1, rs0, rs1, gg0, gg1,
    x_send, x_recv, a1_sem, a2_send, a_recv, g_send, g_recv,
    st_send, st_recv, rs_send, rs_recv, gg_send, gg_recv, z0_send, z0_recv, z1_send, z1_recv,
    loc_sem,
):
    totals, parts, rss, ggs = (total0, total1), (part0, part1), (rs0, rs1), (gg0, gg1)
    x_lo, y, z, x_hi, core = place()
    mp = x_hi * 2 + core
    group = x_lo * 4 + y
    y_up, y_down, y_far = lax.rem(y + 1, 4), lax.rem(y + 3, 4), lax.rem(y + 2, 4)
    other_x = 1 - x_lo
    partner = device(other_x, y, z, x_hi, core)
    outer = device(other_x, y, z, 1 - x_hi, core)
    twin = device(x_lo, y, z, x_hi, 1 - core)
    z_peer = [device(x_lo, y, lax.rem(z + k, 8), x_hi, core) for k in range(1, 8)]
    y_peer = (device(x_lo, y_up, z, x_hi, core), device(x_lo, y_down, z, x_hi, core))
    g_peer = []
    for k in range(1, 8):
        g = lax.rem(group + k, 8)
        g_peer.append(device(g // 4, lax.rem(g, 4), z, x_hi, core))

    load_act = pltpu.make_async_copy(act_ref, act_in, loc_sem.at[0])
    load_act.start()
    load_old = pltpu.make_async_copy(old_ref, old_in, loc_sem.at[1])
    load_old.start()
    peers = z_peer + g_peer + [outer, twin]
    barrier = pltpu.get_barrier_semaphore()
    for peer in peers:
        pl.semaphore_signal(barrier, inc=1, device_id=peer, device_id_type=MESH)
    load_act.wait()
    act_t[...] = act_in[...].T
    load_old.wait()
    stats_ref[z] = old_in[...].astype(BF16)
    pl.semaphore_wait(barrier, len(peers))

    feature = swap(y)
    same = core == lax.rem(feature, 2)
    root = jnp.logical_and(same, x_hi == feature // 2)
    mid = jnp.logical_and(same, x_hi != feature // 2)
    stray = feature != mp

    def out_columns(side, chunk):
        offset, width = CHUNKS[chunk]
        return gout_ref.at[:, pl.ds(pl.multiple_of(side * 640 + offset, 128), width)]

    def g_slot(slot, chunk):
        offset, width = CHUNKS[chunk]
        return goutg.at[slot, :, pl.ds(offset, width)]

    def g_half(slot, chunk, way):
        offset, width = CHUNKS[chunk]
        return goutg.at[slot, pl.ds(way * 128, 128), pl.ds(offset, width)]

    def x_copy(chunk):
        return remote(
            out_columns(other_x, chunk), g_slot(group, chunk),
            x_send.at[chunk], x_recv.at[chunk], partner,
        )

    def x_landed(chunk):
        ref = g_slot(other_x * 4 + y, chunk)
        remote(ref, ref, x_send.at[chunk], x_recv.at[chunk], partner).wait_recv()

    def y_copy(chunk, kind, way):
        index = chunk * 8 + kind * 2 + way
        column = other_x if kind in (PAIR, ON_PAIR) else x_lo
        if kind in (OWN, PAIR):
            dst = g_slot(column * 4 + y, chunk)
            src = out_columns(x_lo, chunk) if kind == OWN else dst
        else:
            dst = g_half(column * 4 + (y_down if way == 0 else y_up), chunk, way)
            src = dst
        return remote(src, dst, g_send.at[index], g_recv.at[index], y_peer[way])

    def y_landed(chunk, kind, way):
        index = chunk * 8 + kind * 2 + way
        column = other_x if kind in (PAIR, ON_PAIR) else x_lo
        if kind in (OWN, PAIR):
            ref = g_slot(column * 4 + (y_down if way == 0 else y_up), chunk)
        else:
            ref = g_half(column * 4 + y_far, chunk, way)
        remote(ref, ref, g_send.at[index], g_recv.at[index], y_peer[way]).wait_recv()

    def y_send(chunk, kind):
        for way in range(2):
            if kind in (ON_OWN, ON_PAIR):
                y_landed(chunk, kind - 2, way)
            y_copy(chunk, kind, way).start()

    def a_slot(slot):
        return actg.at[:, pl.ds(pl.multiple_of(slot * 256, 256), 256)]

    def a_landed(slot):
        remote(a_slot(slot), a_slot(slot), a1_sem, a_recv.at[slot], partner).wait_recv()

    def a_send(slot, index, peer, src=None):
        src = a_slot(slot) if src is None else src
        return remote(src, a_slot(slot), a2_send.at[index], a_recv.at[slot], peer)

    arrivals = (y, y_down, y_up, y_far)
    a1_copy = remote(
        act_t, a_slot(group), a1_sem, a_recv.at[group], device(x_lo, swap(mp), z, x_hi, core)
    )

    def from_root(i):
        slot = x_lo * 4 + arrivals[i]
        if i > 0:
            a_landed(slot)
        src = act_t if i == 0 else None
        a_send(slot, i, partner, src).start()
        a_send(slot, 12 + i, outer, src).start()
        a_send(slot, 4 + i, twin, src).start()

    def from_mid(i):
        slot = other_x * 4 + arrivals[i]
        a_landed(slot)
        a_send(slot, i, partner).start()
        a_send(slot, 4 + i, twin).start()

    stats = Ring(lambda i: stats_ref.at[i], st_send, st_recv, (z_peer[0], z_peer[6]), z)

    pl.when(stray)(lambda: a1_copy.start())
    x_copy(0).start()
    pl.when(root)(lambda: from_root(0))
    y_send(0, OWN)
    stats.start(0)
    x_copy(1).start()
    keep = pltpu.make_async_copy(
        gout_ref.at[:, pl.ds(pl.multiple_of(x_lo * 640, 128), 640)], goutg.at[group], loc_sem.at[2]
    )
    keep.start()

    @pl.when(jnp.logical_not(stray))
    def _():
        actg[:, pl.ds(pl.multiple_of(group * 256, 256), 256)] = act_t[...]

    pl.when(root)(lambda: from_root(1))
    x_landed(0)
    y_send(0, PAIR)
    stats.arrived(0)
    stats.start(1)

    @pl.when(root)
    def _():
        from_root(2)
        from_root(3)

    pl.when(mid)(lambda: from_mid(0))
    y_send(1, OWN)
    x_landed(1)
    y_send(1, PAIR)
    y_send(0, ON_OWN)
    pl.when(mid)(lambda: from_mid(1))
    stats.arrived(1)
    stats.start(2)
    y_send(0, ON_PAIR)
    pl.when(mid)(lambda: from_mid(2))
    stats.arrived(2)
    stats.start(3)
    y_send(1, ON_OWN)
    pl.when(mid)(lambda: from_mid(3))
    y_send(1, ON_PAIR)

    first = jnp.where(root, x_lo, other_x)

    @pl.when(same)
    def _():
        for i in range(4):
            slot = (1 - first) * 4 + arrivals[i]
            a_landed(slot)
            a_send(slot, 8 + i, twin).start()

    @pl.when(jnp.logical_not(same))
    def _():
        for slot in range(8):
            a_landed(slot)

    keep.wait()

    def z_sum(chunk):
        offset, width = CHUNKS[chunk]
        for kind in (ON_OWN, ON_PAIR):
            for way in range(2):
                y_landed(chunk, kind, way)
        right = goutg[:, :, offset : offset + width].reshape(2048, width)
        product = jnp.dot(actg[...], right, preferred_element_type=F32)
        totals[chunk][...] = product
        parts[chunk][...] = product.astype(BF16).reshape(8, 80, width)
        sent = []
        for k in range(1, 8):
            to = lax.rem(z + k, 8)
            copy = remote(
                parts[chunk].at[to], rss[chunk].at[k],
                rs_send.at[chunk * 8 + k], rs_recv.at[chunk * 8 + k], z_peer[k - 1],
            )
            copy.start()
            sent.append(copy)
        return sent

    def group_spread(chunk, sums):
        rows = totals[chunk][pl.ds(pl.multiple_of(z * 80, 8), 80), :]
        for k in range(1, 8):
            sums[k - 1].wait_recv()
            rows = rows + rss[chunk][k].astype(F32)
        ggs[chunk][group] = rows.astype(BF16)
        sent = []
        for k in range(1, 8):
            own = ggs[chunk].at[group]
            copy = remote(
                own, own, gg_send.at[chunk * 8 + k], gg_recv.at[chunk * 8 + k], g_peer[k - 1]
            )
            copy.start()
            sent.append(copy)
        return sent

    block = jnp.int32(0)
    for b in range(8):
        block = jnp.where(owner_ref[b] == group, b // 4 * 4 + SWAP[b % 4], block)

    def pick(chunk, spread):
        offset, width = CHUNKS[chunk]
        for copy in spread:
            copy.wait_recv()
        grad_ref[z, :, offset : offset + width] = ggs[chunk][block]
        sems = ((z0_send, z0_recv), (z1_send, z1_recv))[chunk]

        def piece(i, part):
            start, count = ((0, 80), (0, 48), (48, 32))[part]
            return grad_ref.at[i, pl.ds(start, count), pl.ds(offset, width)]

        near = Near(piece, *sems, z_peer, z)
        near.start()
        return near

    sums0 = z_sum(0)
    sums1 = z_sum(1)
    stats.arrived(3)
    spread0 = group_spread(0, sums0)
    near0 = pick(0, spread0)
    spread1 = group_spread(1, sums1)
    near0.relay()
    near1 = pick(1, spread1)
    near1.relay()
    near0.finish()
    near1.finish()

    def drain():
        near0.drain()
        near1.drain()
        stats.drain()
        for copy in spread0 + spread1 + sums0 + sums1 + [x_copy(0), x_copy(1)]:
            copy.wait_send()
        for chunk in range(2):
            for kind in range(4):
                for way in range(2):
                    y_copy(chunk, kind, way).wait_send()

        pl.when(stray)(lambda: a1_copy.wait_send())

        @pl.when(same)
        def _():
            for k in range(4):
                a_send(k, k, partner).wait_send()
                a_send(k, 4 + k, twin).wait_send()
                a_send(k, 8 + k, twin).wait_send()

        @pl.when(root)
        def _():
            for k in range(4):
                a_send(k, 12 + k, outer).wait_send()

    return drain


def dot(a, b):
    return jnp.dot(a, b, preferred_element_type=F32)


def finish_part(
    grad_ref, stats_ref, old_ref, rotation_ref, update_ref, stats_out, roots_out,
    both, moment, wide, low1, low2, low3, low_w, scales, rot0, rot1, rot2,
    a_send, a_recv, az_send, az_recv, ay_send, ay_recv, bz_send, bz_recv,
    x_send, x_recv, y_send, y_recv, p_send, p_recv, f_send, f_recv, q_send, q_recv,
    c_send, c_recv, rot_send, rot_recv,
):
    x_lo, y, z, x_hi, core = place()
    group = x_lo * 4 + y
    other_x = 1 - x_lo
    pair = other_x * 4 + y
    y_up, y_down, y_far = lax.rem(y + 1, 4), lax.rem(y + 3, 4), lax.rem(y + 2, 4)
    partner = device(other_x, y, z, x_hi, core)
    up_y = device(x_lo, y_up, z, x_hi, core)
    down_y = device(x_lo, y_down, z, x_hi, core)
    up_z = device(x_lo, y, lax.rem(z + 1, 8), x_hi, core)
    down_z = device(x_lo, y, lax.rem(z + 7, 8), x_hi, core)
    g_peer = []
    for k in range(1, 8):
        g = lax.rem(group + k, 8)
        g_peer.append(device(g // 4, lax.rem(g, 4), z, x_hi, core))
    z_peer = [device(x_lo, y, lax.rem(z + k, 8), x_hi, core) for k in range(1, 8)]
    rots = (rot0, rot1, rot2)

    def rotate(step):
        return remote(
            rots[step].at[0], rots[step].at[1], rot_send.at[step], rot_recv.at[step],
            g_peer[(1 << step) - 1],
        )

    def rotated(step):
        rotate(step).wait_recv()
        bit = lax.rem(rotation_ref[0] // (1 << step), 2)
        return rots[step][bit]

    side = z // 4
    quarter = pl.multiple_of(lax.rem(z, 4) * 160, 16)
    eighth = pl.multiple_of(z * 80, 16)
    grad = grad_ref[...].reshape(640, 640)
    both[0] = grad
    both[1] = grad.T

    own = dot(both[side, pl.ds(quarter, 160), :], both[1 - side])
    stats_out[...] = BETA * old_ref[...] + (1.0 - BETA) * own

    def start(s, carry):
        a = BETA * stats_ref[pl.ds(s * 4, 4)].reshape(640, 640).astype(F32) + (1.0 - BETA) * dot(both[s], both[1 - s])
        moment[s] = a
        norm = jnp.sqrt(jnp.sum(a * a, keepdims=True))
        scale = 2.5 / norm
        scales[s] = jnp.broadcast_to(jnp.sqrt(jnp.sqrt(scale)), (8, 128))
        m = moment[s] * scale
        moment[s] = m
        low1[s] = m.astype(BF16)
        return carry

    lax.fori_loop(0, 2, start, 0)

    def advance(now, later):
        def square(s, carry):
            w = dot(now[s], now[s]) - 10.0 * moment[s]
            wide[s] = w
            low_w[s] = w.astype(BF16)
            return carry

        def fourth(s, carry):
            h = dot(low_w[s], low_w[s]) + 50.0 * wide[s]
            wide[s] = h
            return carry

        def finish(s, carry):
            m = (625.0 * moment[s] + dot(now[s], wide[s].astype(BF16))) * (1.0 / 256.0)
            moment[s] = m
            later[s] = m.astype(BF16)
            return carry

        lax.fori_loop(0, 2, square, 0)
        lax.fori_loop(0, 2, fourth, 0)
        lax.fori_loop(0, 2, finish, 0)

    advance(low1, low2)
    advance(low2, low3)

    def factor(r, low, s):
        return 1.25 * r - 0.25 * dot(r.astype(BF16), low[s])

    def chain(r, s):
        r = factor(r, low2, s)
        r = factor(r, low3, s)
        t = r
        for _ in range(4):
            t = factor(t, low3, s)
        return 1.25 * r - 0.25 * dot(t.astype(BF16), low3[s])

    def identity(rows, offset):
        across = lax.broadcasted_iota(jnp.int32, (rows, 640), 1)
        down = lax.broadcasted_iota(jnp.int32, (rows, 640), 0) + offset
        return (across == down).astype(F32)

    def first(rows, offset, s):
        m = low1[s, pl.ds(offset, rows), :].astype(F32)
        return (1.25 * identity(rows, offset) - 0.25 * m) * scales[s, 0:1, 0:1]

    rot0[0] = chain(first(160, quarter, side), side).astype(BF16)
    rotate(0).start()
    left = chain(first(80, eighth, 0), 0)
    high = left.astype(BF16)
    low = (left - high.astype(F32)).astype(BF16)
    right = dot(high, both[0]) + dot(low, both[0])
    right = factor(right, low1, 1) * scales[1, 0:1, 0:1]
    right = chain(right, 1)
    update_ref[group, z] = right.astype(BF16)

    def slot(r):
        return lax.rem(z + r, 8)

    def rows(g, r, start, count):
        return update_ref.at[g, slot(r), pl.ds(start, count)]

    sent = []

    def send(ref, sems, index, peer):
        copy = remote(ref, ref, sems[0].at[index], sems[1].at[index], peer)
        copy.start()
        sent.append(copy)

    def landed(ref, sems, index):
        remote(ref, ref, sems[0].at[index], sems[1].at[index], partner).wait_recv()

    xs, ys, ps = (x_send, x_recv), (y_send, y_recv), (p_send, p_recv)
    fs, qs, cs = (f_send, f_recv), (q_send, q_recv), (c_send, c_recv)
    low, high, far = x_lo * 4 + y_down, x_lo * 4 + y_up, x_lo * 4 + y_far
    p_low, p_high, p_far = other_x * 4 + y_down, other_x * 4 + y_up, other_x * 4 + y_far

    def piece(i, part):
        start, count = ((32, 48), (32, 32), (64, 16))[part]
        return update_ref.at[group, i, pl.ds(start, count)]

    near = Near(piece, bz_send, bz_recv, z_peer, z)
    ring_a = Ring(
        lambda i: update_ref.at[pl.ds(0, 4), i, pl.ds(0, 32)], az_send, az_recv, (up_z, down_z), z
    )
    ring_c = Ring(
        lambda i: update_ref.at[pl.ds(4, 4), i, pl.ds(0, 32)], ay_send, ay_recv, (up_z, down_z), z
    )

    def own_out(r):
        send(rows(group, r, 32, 48), xs, r, partner)
        send(rows(group, r, 32, 48), ys, r, up_y)
        send(rows(group, r, 32, 48), ys, 8 + r, down_y)

    def pair_out(r):
        landed(rows(pair, r, 32, 48), xs, r)
        send(rows(pair, r, 32, 32), ps, r, up_y)
        send(rows(pair, r, 32, 32), ps, 8 + r, down_y)

    def own_on(r):
        landed(rows(low, r, 32, 48), ys, r)
        if r < 4:
            send(rows(low, r, 32, 48), fs, r, up_y)
        landed(rows(high, r, 32, 48), ys, 8 + r)
        if r >= 4:
            send(rows(high, r, 32, 48), fs, r, down_y)

    def pair_on(r):
        landed(rows(p_low, r, 32, 32), ps, r)
        if r < 4:
            send(rows(p_low, r, 32, 32), qs, r, up_y)
        landed(rows(p_high, r, 32, 32), ps, 8 + r)
        if r >= 4:
            send(rows(p_high, r, 32, 32), qs, r, down_y)

    def across(g, index):
        send(update_ref.at[g, :, pl.ds(64, 16)], cs, index, partner)

    near.start()
    own_out(0)
    over = []
    for k in range(1, 8):
        own = update_ref.at[group, z, pl.ds(0, 32)]
        copy = remote(own, own, a_send.at[k], a_recv.at[k], g_peer[k - 1])
        copy.start()
        over.append(copy)

    near.relay()
    own_out(6)
    own_out(2)
    near.landed(2)
    own_out(7)
    near.landed(3)
    own_out(1)
    for copy in over:
        copy.wait_recv()
    ring_a.start(0)
    ring_c.start(0)
    rot1[0] = rotated(0)
    rotate(1).start()
    pair_out(0)
    own_on(0)
    for r in (6, 2, 7, 1):
        pair_out(r)
    near.landed(4)
    own_out(5)
    near.landed(5)
    own_out(3)
    near.landed(6)
    near.landed(7)
    own_out(4)
    for r in (6, 2, 7, 1):
        own_on(r)
    ring_a.arrived(0)
    ring_a.start(1)
    ring_c.arrived(0)
    ring_c.start(1)
    for r in (5, 3, 4):
        pair_out(r)
    for r in (5, 3, 4):
        own_on(r)
    across(low, 0)
    across(high, 1)
    rot2[0] = rotated(1)
    rotate(2).start()
    for r in (0, 6, 2, 7, 1):
        pair_on(r)
    ring_a.arrived(1)
    ring_a.start(2)
    ring_c.arrived(1)
    ring_c.start(2)
    for r in (5, 3, 4):
        pair_on(r)
    for r in range(8):
        landed(rows(far, r, 32, 48), fs, r)
    across(far, 2)
    ring_a.arrived(2)
    ring_a.start(3)
    ring_c.arrived(2)
    ring_c.start(3)
    roots_out[...] = rotated(2).astype(F32)
    for r in range(8):
        landed(rows(p_far, r, 32, 32), qs, r)
    for index, g in enumerate((p_low, p_high, p_far)):
        landed(update_ref.at[g, :, pl.ds(64, 16)], cs, index)
    ring_a.arrived(3)
    ring_c.arrived(3)

    near.drain()
    ring_a.drain()
    ring_c.drain()
    for copy in sent + over:
        copy.wait_send()
    for step in range(3):
        rotate(step).wait_send()


GATHER_REFS = 30


def step_kernel(
    act_ref, gout_ref, old_ref, owner_ref, rotation_ref, update_ref, stats_out, roots_out,
    grad_ref, stats_ref, old_in, *rest,
):
    drain = gather_part(
        act_ref, gout_ref, old_ref, owner_ref, grad_ref, stats_ref, old_in, *rest[:GATHER_REFS]
    )
    finish_part(
        grad_ref, stats_ref, old_in, rotation_ref, update_ref, stats_out, roots_out,
        *rest[GATHER_REFS:],
    )
    drain()


def shampoo_step(activations, grad_out, old_rows, owner_map, rotation):
    hbm = pl.BlockSpec(memory_space=pltpu.HBM)
    widths = [width for _, width in CHUNKS]

    def sems(*counts):
        return [pltpu.SemaphoreType.DMA((count,)) for count in counts]

    return pl.pallas_call(
        step_kernel,
        out_shape=(
            jax.ShapeDtypeStruct((8, 8, 80, 640), BF16),
            jax.ShapeDtypeStruct((160, 640), F32),
            jax.ShapeDtypeStruct((160, 640), F32),
        ),
        in_specs=[hbm, hbm, hbm, SMEM, SMEM],
        out_specs=(VMEM, VMEM, VMEM),
        scratch_shapes=[
            pltpu.VMEM((8, 80, 640), BF16),
            pltpu.VMEM((8, 160, 640), BF16),
            pltpu.VMEM((160, 640), F32),
            pltpu.VMEM((256, 640), BF16),
            pltpu.VMEM((640, 256), BF16),
            pltpu.VMEM((640, 2048), BF16),
            pltpu.VMEM((8, 256, 640), BF16),
            *[pltpu.VMEM((640, width), F32) for width in widths],
            *[pltpu.VMEM((8, 80, width), BF16) for _ in range(3) for width in widths],
            *sems(2, 2), pltpu.SemaphoreType.DMA,
            *sems(16, 8, 16, 16, 7, 7, 16, 16, 16, 16, 8, 8, 8, 8, 3),
            pltpu.VMEM((2, 640, 640), BF16),
            pltpu.VMEM((2, 640, 640), F32),
            pltpu.VMEM((2, 640, 640), F32),
            pltpu.VMEM((2, 640, 640), BF16),
            pltpu.VMEM((2, 640, 640), BF16),
            pltpu.VMEM((2, 640, 640), BF16),
            pltpu.VMEM((2, 640, 640), BF16),
            pltpu.VMEM((2, 8, 128), F32),
            pltpu.VMEM((2, 160, 640), BF16),
            pltpu.VMEM((2, 160, 640), BF16),
            pltpu.VMEM((2, 160, 640), BF16),
            *sems(8, 8, 7, 7, 7, 7, 8, 8, 8, 8, 16, 16, 16, 16, 8, 8, 8, 8, 3, 3, 3, 3),
        ],
        compiler_params=pltpu.CompilerParams(
            collective_id=0, has_side_effects=True, vmem_limit_bytes=44 * 2**20
        ),
        name="shampoo_step",
    )(activations, grad_out, old_rows, owner_map, rotation)


def order_kernel(owner_ref, in_ref, stats_ref, roots_ref, out_ref, stats_out, roots_out, sems):
    copies = [
        pltpu.make_async_copy(in_ref.at[owner_ref[b]], out_ref.at[b], sems.at[b]) for b in range(8)
    ]
    copies.append(pltpu.make_async_copy(stats_ref, stats_out, sems.at[8]))
    copies.append(pltpu.make_async_copy(roots_ref, roots_out, sems.at[9]))
    for copy in copies:
        copy.start()
    for copy in copies:
        copy.wait()


def order_blocks(by_place, stats_new, roots_new, owner_map):
    hbm = pl.BlockSpec(memory_space=pltpu.HBM)
    return pl.pallas_call(
        order_kernel,
        out_shape=(
            jax.ShapeDtypeStruct((8, 640, 640), BF16),
            jax.ShapeDtypeStruct((160, 640), F32),
            jax.ShapeDtypeStruct((160, 640), F32),
        ),
        in_specs=[SMEM, VMEM, VMEM, VMEM],
        out_specs=(hbm, hbm, hbm),
        scratch_shapes=[pltpu.SemaphoreType.DMA((10,))],
        compiler_params=pltpu.CompilerParams(vmem_limit_bytes=16 * 2**20),
        name="order_blocks",
    )(owner_map, by_place, stats_new, roots_new)


def local(activations, grad_out, stats_old, owner_map, rotation):
    old_rows = stats_old.reshape(160, 640)
    by_place, stats_new, roots_new = shampoo_step(
        activations, grad_out, old_rows, owner_map, rotation
    )
    update, stats_new, roots_new = order_blocks(
        by_place.reshape(8, 640, 640), stats_new, roots_new, owner_map
    )
    return (
        update.reshape(2, 2560, 640),
        stats_new.reshape(stats_old.shape),
        roots_new.reshape(stats_old.shape),
    )


def solution(mesh):
    return jax.shard_map(
        local,
        mesh=mesh,
        in_specs=(P("dp", "mp"), P("dp", "mp"), P("mp", None, "dp", None, None), P(), P()),
        out_specs=(
            P("mp", None, None),
            P("mp", None, "dp", None, None),
            P("mp", None, "dp", None, None),
        ),
        check_vma=False,
    )
```

```python
import jax
import jax.numpy as jnp
from jax import lax
from jax.experimental import pallas as pl
from jax.experimental.pallas import tpu as pltpu
from jax.sharding import PartitionSpec as P

BETA = 0.9
MESH = pl.DeviceIdType.MESH
VMEM = pl.BlockSpec(memory_space=pltpu.VMEM)
SMEM = pl.BlockSpec(memory_space=pltpu.SMEM)
F32 = jnp.float32
BF16 = jnp.bfloat16


def place():
    dp = lax.axis_index("dp")
    mp = lax.axis_index("mp")
    return dp // 32, lax.rem(dp // 8, 4), lax.rem(dp, 8), mp // 2, lax.rem(mp, 2)


def device(x_lo, y, z, x_hi, core):
    return {"dp": x_lo * 32 + y * 8 + z, "mp": x_hi * 2 + core}


def remote(src, dst, send, recv, peer):
    return pltpu.make_async_remote_copy(
        src_ref=src, dst_ref=dst, send_sem=send, recv_sem=recv, device_id=peer, device_id_type=MESH
    )


class Ring:
    def __init__(self, slot, send, recv, peers, z, down_last=False):
        self.slot, self.send, self.recv = slot, send, recv
        self.up, self.down = peers
        self.z = z
        self.steps = (3, 4) if down_last else (4, 3)

    def copy_up(self, step):
        i = lax.rem(self.z - step + 8, 8)
        return remote(self.slot(i), self.slot(i), self.send.at[step], self.recv.at[step], self.up)

    def copy_down(self, step):
        i = lax.rem(self.z + step, 8)
        index = self.steps[0] + step
        return remote(
            self.slot(i), self.slot(i), self.send.at[index], self.recv.at[index], self.down
        )

    def copies(self, step):
        ways = ((self.copy_up, self.steps[0]), (self.copy_down, self.steps[1]))
        return [copy(step) for copy, steps in ways if step < steps]

    def start(self, step):
        for copy in self.copies(step):
            copy.start()

    def arrived(self, step):
        for copy in self.copies(step):
            copy.wait_recv()

    def drain(self):
        for step in range(4):
            for copy in self.copies(step):
                copy.wait_send()


class Near:
    def __init__(self, piece, send, recv, peers, z):
        self.piece, self.send, self.recv, self.peers = piece, send, recv, peers
        self.z = z

    def copy(self, index):
        ahead, behind, part = (
            (2, 0, 0), (-2, 0, 0), (1, 0, 0), (-1, 0, 0), (1, 2, 0), (-1, 2, 0), (2, 2, 1), (-2, 2, 2)
        )[index]
        way = 1 if ahead > 0 else -1
        ref = self.piece(lax.rem(self.z - way * behind + 8, 8), part)
        return remote(ref, ref, self.send.at[index], self.recv.at[index], self.peers[ahead % 8 - 1])

    def landed(self, index):
        ahead, behind, part = (
            (2, 0, 0), (-2, 0, 0), (1, 0, 0), (-1, 0, 0), (1, 2, 0), (-1, 2, 0), (2, 2, 1), (-2, 2, 2)
        )[index]
        way = 1 if ahead > 0 else -1
        ref = self.piece(lax.rem(self.z - ahead - way * behind + 8, 8), part)
        remote(ref, ref, self.send.at[index], self.recv.at[index], self.peers[0]).wait_recv()

    def start(self):
        for index in range(4):
            self.copy(index).start()

    def relay(self):
        for index in (0, 1):
            self.landed(index)
            self.copy(4 + index).start()
            self.copy(6 + index).start()

    def finish(self):
        for index in (2, 3, 4, 5, 6, 7):
            self.landed(index)

    def drain(self):
        for index in range(8):
            self.copy(index).wait_send()


def swap(v):
    return lax.rem(v, 2) * 2 + v // 2


SWAP = (0, 2, 1, 3)
CHUNKS = ((0, 384), (384, 256))
OWN, PAIR, ON_OWN, ON_PAIR = range(4)


def gather_part(
    act_ref, gout_ref, old_ref, owner_ref, grad_ref, stats_ref, old_in,
    act_in, act_t, actg, goutg, total0, total1, part0, part1, rs0, rs1, gg0, gg1,
    x_send, x_recv, a1_sem, a2_send, a_recv, g_send, g_recv,
    st_send, st_recv, rs_send, rs_recv, gg_send, gg_recv, z0_send, z0_recv, z1_send, z1_recv,
    loc_sem,
):
    totals, parts, rss, ggs = (total0, total1), (part0, part1), (rs0, rs1), (gg0, gg1)
    x_lo, y, z, x_hi, core = place()
    mp = x_hi * 2 + core
    group = x_lo * 4 + y
    y_up, y_down, y_far = lax.rem(y + 1, 4), lax.rem(y + 3, 4), lax.rem(y + 2, 4)
    other_x = 1 - x_lo
    partner = device(other_x, y, z, x_hi, core)
    outer = device(other_x, y, z, 1 - x_hi, core)
    twin = device(x_lo, y, z, x_hi, 1 - core)
    z_peer = [device(x_lo, y, lax.rem(z + k, 8), x_hi, core) for k in range(1, 8)]
    y_peer = (device(x_lo, y_up, z, x_hi, core), device(x_lo, y_down, z, x_hi, core))
    g_peer = []
    for k in range(1, 8):
        g = lax.rem(group + k, 8)
        g_peer.append(device(g // 4, lax.rem(g, 4), z, x_hi, core))

    load_act = pltpu.make_async_copy(act_ref, act_in, loc_sem.at[0])
    load_act.start()
    load_old = pltpu.make_async_copy(old_ref, old_in, loc_sem.at[1])
    load_old.start()
    peers = z_peer + g_peer + [outer, twin]
    barrier = pltpu.get_barrier_semaphore()
    for peer in peers:
        pl.semaphore_signal(barrier, inc=1, device_id=peer, device_id_type=MESH)
    load_act.wait()
    act_t[...] = act_in[...].T
    load_old.wait()
    stats_ref[z] = old_in[...].astype(BF16)
    pl.semaphore_wait(barrier, len(peers))

    feature = swap(y)
    same = core == lax.rem(feature, 2)
    root = jnp.logical_and(same, x_hi == feature // 2)
    mid = jnp.logical_and(same, x_hi != feature // 2)
    stray = feature != mp

    def out_columns(side, chunk):
        offset, width = CHUNKS[chunk]
        return gout_ref.at[:, pl.ds(pl.multiple_of(side * 640 + offset, 128), width)]

    def g_slot(slot, chunk):
        offset, width = CHUNKS[chunk]
        return goutg.at[slot, :, pl.ds(offset, width)]

    def g_half(slot, chunk, way):
        offset, width = CHUNKS[chunk]
        return goutg.at[slot, pl.ds(way * 128, 128), pl.ds(offset, width)]

    def x_copy(chunk):
        return remote(
            out_columns(other_x, chunk), g_slot(group, chunk),
            x_send.at[chunk], x_recv.at[chunk], partner,
        )

    def x_landed(chunk):
        ref = g_slot(other_x * 4 + y, chunk)
        remote(ref, ref, x_send.at[chunk], x_recv.at[chunk], partner).wait_recv()

    def y_copy(chunk, kind, way):
        index = chunk * 8 + kind * 2 + way
        column = other_x if kind in (PAIR, ON_PAIR) else x_lo
        if kind in (OWN, PAIR):
            dst = g_slot(column * 4 + y, chunk)
            src = out_columns(x_lo, chunk) if kind == OWN else dst
        else:
            dst = g_half(column * 4 + (y_down if way == 0 else y_up), chunk, way)
            src = dst
        return remote(src, dst, g_send.at[index], g_recv.at[index], y_peer[way])

    def y_landed(chunk, kind, way):
        index = chunk * 8 + kind * 2 + way
        column = other_x if kind in (PAIR, ON_PAIR) else x_lo
        if kind in (OWN, PAIR):
            ref = g_slot(column * 4 + (y_down if way == 0 else y_up), chunk)
        else:
            ref = g_half(column * 4 + y_far, chunk, way)
        remote(ref, ref, g_send.at[index], g_recv.at[index], y_peer[way]).wait_recv()

    def y_send(chunk, kind):
        for way in range(2):
            if kind in (ON_OWN, ON_PAIR):
                y_landed(chunk, kind - 2, way)
            y_copy(chunk, kind, way).start()

    def a_slot(slot, part):
        return actg.at[pl.ds(part * 320, 320), pl.ds(pl.multiple_of(slot * 256, 256), 256)]

    def a_copy(slot, part, send, peer, own=False):
        dst = a_slot(slot, part)
        src = act_t.at[pl.ds(part * 320, 320)] if own else dst
        return remote(src, dst, send, a_recv.at[slot * 2 + part], peer)

    def a_landed(slot, part):
        a_copy(slot, part, a1_sem.at[part], partner).wait_recv()

    def a_send(slot, part, index, peer, own=False):
        return a_copy(slot, part, a2_send.at[index * 2 + part], peer, own)

    arrivals = (y, y_down, y_up, y_far)
    def a1_copy(part):
        target = device(x_lo, swap(mp), z, x_hi, core)
        return a_copy(group, part, a1_sem.at[part], target, True)

    def from_root(i):
        slot = x_lo * 4 + arrivals[i]
        for part in range(2):
            if i > 0:
                a_landed(slot, part)
            a_send(slot, part, i, partner, i == 0).start()
            a_send(slot, part, 12 + i, outer, i == 0).start()
            a_send(slot, part, 4 + i, twin, i == 0).start()

    def from_mid(i):
        slot = other_x * 4 + arrivals[i]
        for part in range(2):
            a_landed(slot, part)
            a_send(slot, part, i, partner).start()
            a_send(slot, part, 4 + i, twin).start()

    stats = Ring(lambda i: stats_ref.at[i], st_send, st_recv, (z_peer[0], z_peer[6]), z)

    @pl.when(stray)
    def _():
        a1_copy(0).start()
        a1_copy(1).start()

    x_copy(0).start()
    pl.when(root)(lambda: from_root(0))
    y_send(0, OWN)
    stats.start(0)
    x_copy(1).start()
    keep = pltpu.make_async_copy(
        gout_ref.at[:, pl.ds(pl.multiple_of(x_lo * 640, 128), 640)], goutg.at[group], loc_sem.at[2]
    )
    keep.start()

    @pl.when(jnp.logical_not(stray))
    def _():
        actg[:, pl.ds(pl.multiple_of(group * 256, 256), 256)] = act_t[...]

    pl.when(root)(lambda: from_root(1))
    x_landed(0)
    y_send(0, PAIR)
    stats.arrived(0)
    stats.start(1)

    @pl.when(root)
    def _():
        from_root(2)
        from_root(3)

    pl.when(mid)(lambda: from_mid(0))
    y_send(1, OWN)
    x_landed(1)
    y_send(1, PAIR)
    y_send(0, ON_OWN)
    pl.when(mid)(lambda: from_mid(1))
    stats.arrived(1)
    stats.start(2)
    y_send(0, ON_PAIR)
    pl.when(mid)(lambda: from_mid(2))
    stats.arrived(2)
    stats.start(3)
    y_send(1, ON_OWN)
    pl.when(mid)(lambda: from_mid(3))
    y_send(1, ON_PAIR)

    first = jnp.where(root, x_lo, other_x)

    @pl.when(same)
    def _():
        for i in range(4):
            slot = (1 - first) * 4 + arrivals[i]
            for part in range(2):
                a_landed(slot, part)
                a_send(slot, part, 8 + i, twin).start()

    @pl.when(jnp.logical_not(same))
    def _():
        for slot in range(8):
            a_landed(slot, 0)
            a_landed(slot, 1)

    keep.wait()

    def z_sum(chunk):
        offset, width = CHUNKS[chunk]
        for kind in (ON_OWN, ON_PAIR):
            for way in range(2):
                y_landed(chunk, kind, way)
        right = goutg[:, :, offset : offset + width].reshape(2048, width)
        product = jnp.dot(actg[...], right, preferred_element_type=F32)
        totals[chunk][...] = product
        parts[chunk][...] = product.astype(BF16).reshape(8, 80, width)
        sent = []
        for k in range(1, 8):
            to = lax.rem(z + k, 8)
            copy = remote(
                parts[chunk].at[to], rss[chunk].at[k],
                rs_send.at[chunk * 8 + k], rs_recv.at[chunk * 8 + k], z_peer[k - 1],
            )
            copy.start()
            sent.append(copy)
        return sent

    def group_spread(chunk, sums):
        rows = totals[chunk][pl.ds(pl.multiple_of(z * 80, 8), 80), :]
        for k in range(1, 8):
            sums[k - 1].wait_recv()
            rows = rows + rss[chunk][k].astype(F32)
        ggs[chunk][group] = rows.astype(BF16)
        sent = []
        for k in range(1, 8):
            own = ggs[chunk].at[group]
            copy = remote(
                own, own, gg_send.at[chunk * 8 + k], gg_recv.at[chunk * 8 + k], g_peer[k - 1]
            )
            copy.start()
            sent.append(copy)
        return sent

    block = jnp.int32(0)
    for b in range(8):
        block = jnp.where(owner_ref[b] == group, b // 4 * 4 + SWAP[b % 4], block)

    def pick(chunk, spread):
        offset, width = CHUNKS[chunk]
        for copy in spread:
            copy.wait_recv()
        grad_ref[z, :, offset : offset + width] = ggs[chunk][block]
        sems = ((z0_send, z0_recv), (z1_send, z1_recv))[chunk]

        def piece(i, part):
            start, count = ((0, 80), (0, 48), (48, 32))[part]
            return grad_ref.at[i, pl.ds(start, count), pl.ds(offset, width)]

        near = Near(piece, *sems, z_peer, z)
        near.start()
        return near

    sums0 = z_sum(0)
    sums1 = z_sum(1)
    stats.arrived(3)
    spread0 = group_spread(0, sums0)
    near0 = pick(0, spread0)
    spread1 = group_spread(1, sums1)
    near0.relay()
    near1 = pick(1, spread1)
    near1.relay()
    near0.finish()
    near1.finish()

    def drain():
        near0.drain()
        near1.drain()
        stats.drain()
        for copy in spread0 + spread1 + sums0 + sums1 + [x_copy(0), x_copy(1)]:
            copy.wait_send()
        for chunk in range(2):
            for kind in range(4):
                for way in range(2):
                    y_copy(chunk, kind, way).wait_send()

        @pl.when(stray)
        def _():
            a1_copy(0).wait_send()
            a1_copy(1).wait_send()

        @pl.when(same)
        def _():
            for k in range(4):
                for part in range(2):
                    a_send(k, part, k, partner).wait_send()
                    a_send(k, part, 4 + k, twin).wait_send()
                    a_send(k, part, 8 + k, twin).wait_send()

        @pl.when(root)
        def _():
            for k in range(4):
                for part in range(2):
                    a_send(k, part, 12 + k, outer).wait_send()

    return drain


def dot(a, b):
    return jnp.dot(a, b, preferred_element_type=F32)


def finish_part(
    grad_ref, stats_ref, old_ref, rotation_ref, update_ref, stats_out, roots_out,
    both, moment, wide, low1, low2, low3, low_w, scales, rot0, rot1, rot2,
    a_send, a_recv, az_send, az_recv, ay_send, ay_recv, bz_send, bz_recv,
    x_send, x_recv, y_send, y_recv, p_send, p_recv, f_send, f_recv, q_send, q_recv,
    c_send, c_recv, rot_send, rot_recv,
):
    x_lo, y, z, x_hi, core = place()
    group = x_lo * 4 + y
    other_x = 1 - x_lo
    pair = other_x * 4 + y
    y_up, y_down, y_far = lax.rem(y + 1, 4), lax.rem(y + 3, 4), lax.rem(y + 2, 4)
    partner = device(other_x, y, z, x_hi, core)
    up_y = device(x_lo, y_up, z, x_hi, core)
    down_y = device(x_lo, y_down, z, x_hi, core)
    up_z = device(x_lo, y, lax.rem(z + 1, 8), x_hi, core)
    down_z = device(x_lo, y, lax.rem(z + 7, 8), x_hi, core)
    g_peer = []
    for k in range(1, 8):
        g = lax.rem(group + k, 8)
        g_peer.append(device(g // 4, lax.rem(g, 4), z, x_hi, core))
    z_peer = [device(x_lo, y, lax.rem(z + k, 8), x_hi, core) for k in range(1, 8)]
    rots = (rot0, rot1, rot2)

    def rotate(step):
        return remote(
            rots[step].at[0], rots[step].at[1], rot_send.at[step], rot_recv.at[step],
            g_peer[(1 << step) - 1],
        )

    def rotated(step):
        rotate(step).wait_recv()
        bit = lax.rem(rotation_ref[0] // (1 << step), 2)
        return rots[step][bit]

    side = z // 4
    quarter = pl.multiple_of(lax.rem(z, 4) * 160, 16)
    eighth = pl.multiple_of(z * 80, 16)
    grad = grad_ref[...].reshape(640, 640)
    both[0] = grad
    both[1] = grad.T

    def advance(now, later, s):
        w = dot(now[s], now[s]) - 10.0 * moment[s]
        wide[s] = w
        low_w[s] = w.astype(BF16)
        h = dot(low_w[s], low_w[s]) + 50.0 * wide[s]
        low_w[s] = h.astype(BF16)
        m = (625.0 * moment[s] + dot(now[s], low_w[s])) * (1.0 / 256.0)
        moment[s] = m
        later[s] = m.astype(BF16)

    def grow(s):
        old = stats_ref[pl.ds(s * 4, 4)].reshape(640, 640).astype(F32)
        a = BETA * old + (1.0 - BETA) * dot(both[s], both[1 - s])
        moment[s] = a
        scale = 2.5 / jnp.sqrt(jnp.sum(a * a, keepdims=True))
        scales[s] = jnp.broadcast_to(jnp.sqrt(jnp.sqrt(scale)), (8, 128))
        m = moment[s] * scale
        moment[s] = m
        low1[s] = m.astype(BF16)
        advance(low1, low2, s)
        advance(low2, low3, s)

    def factor(r, low, s):
        return 1.25 * r - 0.25 * dot(r.astype(BF16), low[s])

    def chain(r, s):
        r = factor(r, low2, s)
        r = factor(r, low3, s)
        t = r
        for _ in range(4):
            t = factor(t, low3, s)
        return 1.25 * r - 0.25 * dot(t.astype(BF16), low3[s])

    def identity(rows, offset):
        across = lax.broadcasted_iota(jnp.int32, (rows, 640), 1)
        down = lax.broadcasted_iota(jnp.int32, (rows, 640), 0) + offset
        return (across == down).astype(F32)

    def first(rows, offset, s):
        m = low1[s, pl.ds(offset, rows), :].astype(F32)
        return (1.25 * identity(rows, offset) - 0.25 * m) * scales[s, 0:1, 0:1]

    grow(side)
    rot0[0] = chain(first(160, quarter, side), side).astype(BF16)
    rotate(0).start()
    grow(1 - side)
    left = chain(first(80, eighth, 0), 0)
    rot1[0] = rotated(0)
    rotate(1).start()
    high = left.astype(BF16)
    low = (left - high.astype(F32)).astype(BF16)
    right = dot(high, both[0]) + dot(low, both[0])
    right = factor(right, low1, 1) * scales[1, 0:1, 0:1]
    right = chain(right, 1)
    update_ref[group, z] = right.astype(BF16)

    def slot(r):
        return lax.rem(z + r, 8)

    def rows(g, r, start, count):
        return update_ref.at[g, slot(r), pl.ds(start, count)]

    sent = []

    def send(ref, sems, index, peer):
        copy = remote(ref, ref, sems[0].at[index], sems[1].at[index], peer)
        copy.start()
        sent.append(copy)

    def landed(ref, sems, index):
        remote(ref, ref, sems[0].at[index], sems[1].at[index], partner).wait_recv()

    xs, ys, ps = (x_send, x_recv), (y_send, y_recv), (p_send, p_recv)
    fs, qs, cs = (f_send, f_recv), (q_send, q_recv), (c_send, c_recv)
    low, high, far = x_lo * 4 + y_down, x_lo * 4 + y_up, x_lo * 4 + y_far
    p_low, p_high, p_far = other_x * 4 + y_down, other_x * 4 + y_up, other_x * 4 + y_far

    def piece(i, part):
        start, count = ((32, 48), (32, 32), (64, 16))[part]
        return update_ref.at[group, i, pl.ds(start, count)]

    near = Near(piece, bz_send, bz_recv, z_peer, z)
    ring_a = Ring(
        lambda i: update_ref.at[pl.ds(0, 4), i, pl.ds(0, 32)], az_send, az_recv, (up_z, down_z), z
    )
    ring_c = Ring(
        lambda i: update_ref.at[pl.ds(4, 4), i, pl.ds(0, 32)], ay_send, ay_recv, (up_z, down_z), z, True
    )

    def own_out(r):
        send(rows(group, r, 32, 48), xs, r, partner)
        send(rows(group, r, 32, 48), ys, r, up_y)
        send(rows(group, r, 32, 48), ys, 8 + r, down_y)

    def pair_out(r):
        landed(rows(pair, r, 32, 48), xs, r)
        send(rows(pair, r, 32, 32), ps, r, up_y)
        send(rows(pair, r, 32, 32), ps, 8 + r, down_y)

    def own_on(r):
        landed(rows(low, r, 32, 48), ys, r)
        if r < 4:
            send(rows(low, r, 32, 48), fs, r, up_y)
        landed(rows(high, r, 32, 48), ys, 8 + r)
        if r >= 4:
            send(rows(high, r, 32, 48), fs, r, down_y)

    def pair_on(r):
        landed(rows(p_low, r, 32, 32), ps, r)
        if r < 4:
            send(rows(p_low, r, 32, 32), qs, r, up_y)
        landed(rows(p_high, r, 32, 32), ps, 8 + r)
        if r >= 4:
            send(rows(p_high, r, 32, 32), qs, r, down_y)

    def across(g, index):
        send(update_ref.at[g, :, pl.ds(64, 16)], cs, index, partner)

    near.start()
    own_out(0)
    over = []
    for k in range(1, 8):
        own = update_ref.at[group, z, pl.ds(0, 32)]
        copy = remote(own, own, a_send.at[k], a_recv.at[k], g_peer[k - 1])
        copy.start()
        over.append(copy)

    own = dot(both[side, pl.ds(quarter, 160), :], both[1 - side])
    stats_out[...] = BETA * old_ref[...] + (1.0 - BETA) * own
    near.relay()
    own_out(6)
    own_out(2)
    near.landed(2)
    own_out(7)
    near.landed(3)
    own_out(1)
    for copy in over:
        copy.wait_recv()
    ring_a.start(0)
    ring_c.start(0)
    pair_out(0)
    own_on(0)
    for r in (6, 2, 7, 1):
        pair_out(r)
    near.landed(4)
    own_out(5)
    near.landed(5)
    own_out(3)
    near.landed(6)
    near.landed(7)
    own_out(4)
    for r in (6, 2, 7, 1):
        own_on(r)
    ring_a.arrived(0)
    ring_a.start(1)
    ring_c.arrived(0)
    ring_c.start(1)
    for r in (5, 3, 4):
        pair_out(r)
    for r in (5, 3, 4):
        own_on(r)
    across(low, 0)
    across(high, 1)
    rot2[0] = rotated(1)
    rotate(2).start()
    for r in (0, 6, 2, 7, 1):
        pair_on(r)
    ring_a.arrived(1)
    ring_a.start(2)
    ring_c.arrived(1)
    ring_c.start(2)
    for r in (5, 3, 4):
        pair_on(r)
    for r in range(8):
        landed(rows(far, r, 32, 48), fs, r)
    across(far, 2)
    ring_a.arrived(2)
    ring_a.start(3)
    ring_c.arrived(2)
    ring_c.start(3)
    roots_out[...] = rotated(2).astype(F32)
    for r in range(8):
        landed(rows(p_far, r, 32, 32), qs, r)
    for index, g in enumerate((p_low, p_high, p_far)):
        landed(update_ref.at[g, :, pl.ds(64, 16)], cs, index)
    ring_a.arrived(3)
    ring_c.arrived(3)

    near.drain()
    ring_a.drain()
    ring_c.drain()
    for copy in sent + over:
        copy.wait_send()
    for step in range(3):
        rotate(step).wait_send()


GATHER_REFS = 30


def step_kernel(
    act_ref, gout_ref, old_ref, owner_ref, rotation_ref, update_ref, stats_out, roots_out,
    grad_ref, stats_ref, old_in, *rest,
):
    drain = gather_part(
        act_ref, gout_ref, old_ref, owner_ref, grad_ref, stats_ref, old_in, *rest[:GATHER_REFS]
    )
    finish_part(
        grad_ref, stats_ref, old_in, rotation_ref, update_ref, stats_out, roots_out,
        *rest[GATHER_REFS:],
    )
    drain()


def shampoo_step(activations, grad_out, old_rows, owner_map, rotation):
    hbm = pl.BlockSpec(memory_space=pltpu.HBM)
    widths = [width for _, width in CHUNKS]

    def sems(*counts):
        return [pltpu.SemaphoreType.DMA((count,)) for count in counts]

    return pl.pallas_call(
        step_kernel,
        out_shape=(
            jax.ShapeDtypeStruct((8, 8, 80, 640), BF16),
            jax.ShapeDtypeStruct((160, 640), F32),
            jax.ShapeDtypeStruct((160, 640), F32),
        ),
        in_specs=[hbm, hbm, hbm, SMEM, SMEM],
        out_specs=(VMEM, VMEM, VMEM),
        scratch_shapes=[
            pltpu.VMEM((8, 80, 640), BF16),
            pltpu.VMEM((8, 160, 640), BF16),
            pltpu.VMEM((160, 640), F32),
            pltpu.VMEM((256, 640), BF16),
            pltpu.VMEM((640, 256), BF16),
            pltpu.VMEM((640, 2048), BF16),
            pltpu.VMEM((8, 256, 640), BF16),
            *[pltpu.VMEM((640, width), F32) for width in widths],
            *[pltpu.VMEM((8, 80, width), BF16) for _ in range(3) for width in widths],
            *sems(2, 2, 2, 32, 16, 16, 16, 7, 7, 16, 16, 16, 16, 8, 8, 8, 8, 3),
            pltpu.VMEM((2, 640, 640), BF16),
            pltpu.VMEM((2, 640, 640), F32),
            pltpu.VMEM((2, 640, 640), F32),
            pltpu.VMEM((2, 640, 640), BF16),
            pltpu.VMEM((2, 640, 640), BF16),
            pltpu.VMEM((2, 640, 640), BF16),
            pltpu.VMEM((2, 640, 640), BF16),
            pltpu.VMEM((2, 8, 128), F32),
            pltpu.VMEM((2, 160, 640), BF16),
            pltpu.VMEM((2, 160, 640), BF16),
            pltpu.VMEM((2, 160, 640), BF16),
            *sems(8, 8, 7, 7, 7, 7, 8, 8, 8, 8, 16, 16, 16, 16, 8, 8, 8, 8, 3, 3, 3, 3),
        ],
        compiler_params=pltpu.CompilerParams(
            collective_id=0, has_side_effects=True, vmem_limit_bytes=44 * 2**20
        ),
        name="shampoo_step",
    )(activations, grad_out, old_rows, owner_map, rotation)


def order_kernel(owner_ref, in_ref, stats_ref, roots_ref, out_ref, stats_out, roots_out, sems):
    copies = [
        pltpu.make_async_copy(in_ref.at[owner_ref[b]], out_ref.at[b], sems.at[b]) for b in range(8)
    ]
    copies.append(pltpu.make_async_copy(stats_ref, stats_out, sems.at[8]))
    copies.append(pltpu.make_async_copy(roots_ref, roots_out, sems.at[9]))
    for copy in copies:
        copy.start()
    for copy in copies:
        copy.wait()


def order_blocks(by_place, stats_new, roots_new, owner_map):
    hbm = pl.BlockSpec(memory_space=pltpu.HBM)
    return pl.pallas_call(
        order_kernel,
        out_shape=(
            jax.ShapeDtypeStruct((8, 640, 640), BF16),
            jax.ShapeDtypeStruct((160, 640), F32),
            jax.ShapeDtypeStruct((160, 640), F32),
        ),
        in_specs=[SMEM, VMEM, VMEM, VMEM],
        out_specs=(hbm, hbm, hbm),
        scratch_shapes=[pltpu.SemaphoreType.DMA((10,))],
        compiler_params=pltpu.CompilerParams(vmem_limit_bytes=16 * 2**20),
        name="order_blocks",
    )(owner_map, by_place, stats_new, roots_new)


def local(activations, grad_out, stats_old, owner_map, rotation):
    old_rows = stats_old.reshape(160, 640)
    by_place, stats_new, roots_new = shampoo_step(
        activations, grad_out, old_rows, owner_map, rotation
    )
    update, stats_new, roots_new = order_blocks(
        by_place.reshape(8, 640, 640), stats_new, roots_new, owner_map
    )
    return (
        update.reshape(2, 2560, 640),
        stats_new.reshape(stats_old.shape),
        roots_new.reshape(stats_old.shape),
    )


def solution(mesh):
    return jax.shard_map(
        local,
        mesh=mesh,
        in_specs=(P("dp", "mp"), P("dp", "mp"), P("mp", None, "dp", None, None), P(), P()),
        out_specs=(
            P("mp", None, None),
            P("mp", None, "dp", None, None),
            P("mp", None, "dp", None, None),
        ),
        check_vma=False,
    )
```

```python
import jax
import jax.numpy as jnp
from jax import lax
from jax.experimental import pallas as pl
from jax.experimental.pallas import tpu as pltpu
from jax.sharding import PartitionSpec as P

BETA = 0.9
MESH = pl.DeviceIdType.MESH
VMEM = pl.BlockSpec(memory_space=pltpu.VMEM)
SMEM = pl.BlockSpec(memory_space=pltpu.SMEM)
F32 = jnp.float32
BF16 = jnp.bfloat16


def place():
    dp = lax.axis_index("dp")
    mp = lax.axis_index("mp")
    return dp // 32, lax.rem(dp // 8, 4), lax.rem(dp, 8), mp // 2, lax.rem(mp, 2)


def device(x_lo, y, z, x_hi, core):
    return {"dp": x_lo * 32 + y * 8 + z, "mp": x_hi * 2 + core}


def remote(src, dst, send, recv, peer):
    return pltpu.make_async_remote_copy(
        src_ref=src, dst_ref=dst, send_sem=send, recv_sem=recv, device_id=peer, device_id_type=MESH
    )


class Ring:
    def __init__(self, slot, send, recv, peers, z, down_last=False):
        self.slot, self.send, self.recv = slot, send, recv
        self.up, self.down = peers
        self.z = z
        self.steps = (3, 4) if down_last else (4, 3)

    def copy_up(self, step):
        i = lax.rem(self.z - step + 8, 8)
        return remote(self.slot(i), self.slot(i), self.send.at[step], self.recv.at[step], self.up)

    def copy_down(self, step):
        i = lax.rem(self.z + step, 8)
        index = self.steps[0] + step
        return remote(
            self.slot(i), self.slot(i), self.send.at[index], self.recv.at[index], self.down
        )

    def copies(self, step):
        ways = ((self.copy_up, self.steps[0]), (self.copy_down, self.steps[1]))
        return [copy(step) for copy, steps in ways if step < steps]

    def start(self, step):
        for copy in self.copies(step):
            copy.start()

    def arrived(self, step):
        for copy in self.copies(step):
            copy.wait_recv()

    def drain(self):
        for step in range(4):
            for copy in self.copies(step):
                copy.wait_send()


class Near:
    def __init__(self, piece, send, recv, peers, z):
        self.piece, self.send, self.recv, self.peers = piece, send, recv, peers
        self.z = z

    def copy(self, index):
        ahead, behind, part = (
            (2, 0, 0), (-2, 0, 0), (1, 0, 0), (-1, 0, 0), (1, 2, 0), (-1, 2, 0), (2, 2, 1), (-2, 2, 2)
        )[index]
        way = 1 if ahead > 0 else -1
        ref = self.piece(lax.rem(self.z - way * behind + 8, 8), part)
        return remote(ref, ref, self.send.at[index], self.recv.at[index], self.peers[ahead % 8 - 1])

    def landed(self, index):
        ahead, behind, part = (
            (2, 0, 0), (-2, 0, 0), (1, 0, 0), (-1, 0, 0), (1, 2, 0), (-1, 2, 0), (2, 2, 1), (-2, 2, 2)
        )[index]
        way = 1 if ahead > 0 else -1
        ref = self.piece(lax.rem(self.z - ahead - way * behind + 8, 8), part)
        remote(ref, ref, self.send.at[index], self.recv.at[index], self.peers[0]).wait_recv()

    def start(self):
        for index in range(4):
            self.copy(index).start()

    def relay(self):
        for index in (0, 1):
            self.landed(index)
            self.copy(4 + index).start()
            self.copy(6 + index).start()

    def finish(self):
        for index in (2, 3, 4, 5, 6, 7):
            self.landed(index)

    def drain(self):
        for index in range(8):
            self.copy(index).wait_send()


def swap(v):
    return lax.rem(v, 2) * 2 + v // 2


SWAP = (0, 2, 1, 3)
CHUNKS = ((0, 384), (384, 256))
OWN, PAIR, ON_OWN, ON_PAIR = range(4)


def gather_part(
    act_ref, gout_ref, old_ref, owner_ref, grad_ref, stats_ref, old_in,
    act_in, act_t, actg, goutg, total0, total1, part0, part1, rs0, rs1, gg0, gg1,
    x_send, x_recv, a1_sem, a2_send, a_recv, g_send, g_recv,
    st_send, st_recv, rs_send, rs_recv, gg_send, gg_recv, z0_send, z0_recv, z1_send, z1_recv,
    loc_sem,
):
    totals, parts, rss, ggs = (total0, total1), (part0, part1), (rs0, rs1), (gg0, gg1)
    x_lo, y, z, x_hi, core = place()
    mp = x_hi * 2 + core
    group = x_lo * 4 + y
    y_up, y_down, y_far = lax.rem(y + 1, 4), lax.rem(y + 3, 4), lax.rem(y + 2, 4)
    other_x = 1 - x_lo
    partner = device(other_x, y, z, x_hi, core)
    outer = device(other_x, y, z, 1 - x_hi, core)
    twin = device(x_lo, y, z, x_hi, 1 - core)
    z_peer = [device(x_lo, y, lax.rem(z + k, 8), x_hi, core) for k in range(1, 8)]
    y_peer = (device(x_lo, y_up, z, x_hi, core), device(x_lo, y_down, z, x_hi, core))
    g_peer = []
    for k in range(1, 8):
        g = lax.rem(group + k, 8)
        g_peer.append(device(g // 4, lax.rem(g, 4), z, x_hi, core))

    load_act = pltpu.make_async_copy(act_ref, act_in, loc_sem.at[0])
    load_act.start()
    load_old = pltpu.make_async_copy(old_ref, old_in, loc_sem.at[1])
    load_old.start()
    peers = z_peer + g_peer + [outer, twin]
    barrier = pltpu.get_barrier_semaphore()
    for peer in peers:
        pl.semaphore_signal(barrier, inc=1, device_id=peer, device_id_type=MESH)
    load_act.wait()
    act_t[...] = act_in[...].T
    load_old.wait()
    stats_ref[z] = old_in[...].astype(BF16)
    pl.semaphore_wait(barrier, len(peers))

    feature = swap(y)
    same = core == lax.rem(feature, 2)
    root = jnp.logical_and(same, x_hi == feature // 2)
    mid = jnp.logical_and(same, x_hi != feature // 2)
    stray = feature != mp

    def out_columns(side, chunk):
        offset, width = CHUNKS[chunk]
        return gout_ref.at[:, pl.ds(pl.multiple_of(side * 640 + offset, 128), width)]

    def g_slot(slot, chunk):
        offset, width = CHUNKS[chunk]
        return goutg.at[slot, :, pl.ds(offset, width)]

    def g_half(slot, chunk, way):
        offset, width = CHUNKS[chunk]
        return goutg.at[slot, pl.ds(way * 128, 128), pl.ds(offset, width)]

    def x_copy(chunk):
        return remote(
            out_columns(other_x, chunk), g_slot(group, chunk),
            x_send.at[chunk], x_recv.at[chunk], partner,
        )

    def x_landed(chunk):
        ref = g_slot(other_x * 4 + y, chunk)
        remote(ref, ref, x_send.at[chunk], x_recv.at[chunk], partner).wait_recv()

    def y_copy(chunk, kind, way):
        index = chunk * 8 + kind * 2 + way
        column = other_x if kind in (PAIR, ON_PAIR) else x_lo
        if kind in (OWN, PAIR):
            dst = g_slot(column * 4 + y, chunk)
            src = out_columns(x_lo, chunk) if kind == OWN else dst
        else:
            dst = g_half(column * 4 + (y_down if way == 0 else y_up), chunk, way)
            src = dst
        return remote(src, dst, g_send.at[index], g_recv.at[index], y_peer[way])

    def y_landed(chunk, kind, way):
        index = chunk * 8 + kind * 2 + way
        column = other_x if kind in (PAIR, ON_PAIR) else x_lo
        if kind in (OWN, PAIR):
            ref = g_slot(column * 4 + (y_down if way == 0 else y_up), chunk)
        else:
            ref = g_half(column * 4 + y_far, chunk, way)
        remote(ref, ref, g_send.at[index], g_recv.at[index], y_peer[way]).wait_recv()

    def y_send(chunk, kind):
        for way in range(2):
            if kind in (ON_OWN, ON_PAIR):
                y_landed(chunk, kind - 2, way)
            y_copy(chunk, kind, way).start()

    def a_slot(slot, part):
        return actg.at[pl.ds(part * 320, 320), pl.ds(pl.multiple_of(slot * 256, 256), 256)]

    def a_copy(slot, part, send, peer, own=False):
        dst = a_slot(slot, part)
        src = act_t.at[pl.ds(part * 320, 320)] if own else dst
        return remote(src, dst, send, a_recv.at[slot * 2 + part], peer)

    def a_landed(slot, part):
        a_copy(slot, part, a1_sem.at[part], partner).wait_recv()

    def a_send(slot, part, index, peer, own=False):
        return a_copy(slot, part, a2_send.at[index * 2 + part], peer, own)

    arrivals = (y, y_down, y_up, y_far)
    def a1_copy(part):
        target = device(x_lo, swap(mp), z, x_hi, core)
        return a_copy(group, part, a1_sem.at[part], target, True)

    def from_root(i):
        slot = x_lo * 4 + arrivals[i]
        for part in range(2):
            if i > 0:
                a_landed(slot, part)
            a_send(slot, part, i, partner, i == 0).start()
            a_send(slot, part, 12 + i, outer, i == 0).start()
            a_send(slot, part, 4 + i, twin, i == 0).start()

    def from_mid(i):
        slot = other_x * 4 + arrivals[i]
        for part in range(2):
            a_landed(slot, part)
            a_send(slot, part, i, partner).start()
            a_send(slot, part, 4 + i, twin).start()

    stats = Ring(lambda i: stats_ref.at[i], st_send, st_recv, (z_peer[0], z_peer[6]), z)

    @pl.when(stray)
    def _():
        a1_copy(0).start()
        a1_copy(1).start()

    x_copy(0).start()
    pl.when(root)(lambda: from_root(0))
    stats.start(0)
    x_copy(1).start()
    keep = pltpu.make_async_copy(
        gout_ref.at[:, pl.ds(pl.multiple_of(x_lo * 640, 128), 640)], goutg.at[group], loc_sem.at[2]
    )
    keep.start()

    @pl.when(jnp.logical_not(stray))
    def _():
        actg[:, pl.ds(pl.multiple_of(group * 256, 256), 256)] = act_t[...]

    @pl.when(stray)
    def _():
        a1_copy(0).wait_send()
        a1_copy(1).wait_send()

    y_send(0, OWN)
    pl.when(root)(lambda: from_root(1))
    x_landed(0)
    y_send(0, PAIR)
    stats.arrived(0)
    stats.start(1)

    @pl.when(root)
    def _():
        from_root(2)
        from_root(3)

    pl.when(mid)(lambda: from_mid(0))
    y_send(1, OWN)
    x_landed(1)
    y_send(1, PAIR)
    y_send(0, ON_OWN)
    pl.when(mid)(lambda: from_mid(1))
    stats.arrived(1)
    stats.start(2)
    y_send(0, ON_PAIR)
    pl.when(mid)(lambda: from_mid(2))
    stats.arrived(2)
    stats.start(3)
    pl.when(mid)(lambda: from_mid(3))

    first = jnp.where(root, x_lo, other_x)

    @pl.when(same)
    def _():
        for i in range(4):
            slot = (1 - first) * 4 + arrivals[i]
            for part in range(2):
                a_landed(slot, part)
                a_send(slot, part, 8 + i, twin).start()

    @pl.when(jnp.logical_not(same))
    def _():
        for slot in range(8):
            a_landed(slot, 0)
            a_landed(slot, 1)

    keep.wait()

    def z_sum(chunk):
        offset, width = CHUNKS[chunk]
        for kind in (ON_OWN, ON_PAIR):
            for way in range(2):
                y_landed(chunk, kind, way)
        right = goutg[:, :, offset : offset + width].reshape(2048, width)
        product = jnp.dot(actg[...], right, preferred_element_type=F32)
        totals[chunk][...] = product
        parts[chunk][...] = product.astype(BF16).reshape(8, 80, width)
        sent = []
        for k in range(1, 8):
            to = lax.rem(z + k, 8)
            copy = remote(
                parts[chunk].at[to], rss[chunk].at[k],
                rs_send.at[chunk * 8 + k], rs_recv.at[chunk * 8 + k], z_peer[k - 1],
            )
            copy.start()
            sent.append(copy)
        return sent

    def group_spread(chunk, sums):
        rows = totals[chunk][pl.ds(pl.multiple_of(z * 80, 8), 80), :]
        for k in range(1, 8):
            sums[k - 1].wait_recv()
            rows = rows + rss[chunk][k].astype(F32)
        ggs[chunk][group] = rows.astype(BF16)
        sent = []
        for k in range(1, 8):
            own = ggs[chunk].at[group]
            copy = remote(
                own, own, gg_send.at[chunk * 8 + k], gg_recv.at[chunk * 8 + k], g_peer[k - 1]
            )
            copy.start()
            sent.append(copy)
        return sent

    block = jnp.int32(0)
    for b in range(8):
        block = jnp.where(owner_ref[b] == group, b // 4 * 4 + SWAP[b % 4], block)

    def pick(chunk, spread):
        offset, width = CHUNKS[chunk]
        for copy in spread:
            copy.wait_recv()
        grad_ref[z, :, offset : offset + width] = ggs[chunk][block]
        sems = ((z0_send, z0_recv), (z1_send, z1_recv))[chunk]

        def piece(i, part):
            start, count = ((0, 80), (0, 48), (48, 32))[part]
            return grad_ref.at[i, pl.ds(start, count), pl.ds(offset, width)]

        near = Near(piece, *sems, z_peer, z)
        near.start()
        return near

    sums0 = z_sum(0)
    y_send(1, ON_OWN)
    y_send(1, ON_PAIR)
    sums1 = z_sum(1)
    stats.arrived(3)
    spread0 = group_spread(0, sums0)
    near0 = pick(0, spread0)
    spread1 = group_spread(1, sums1)
    near0.relay()
    near1 = pick(1, spread1)
    near1.relay()
    near0.finish()
    near1.finish()

    def drain():
        near0.drain()
        near1.drain()
        stats.drain()
        for copy in spread0 + spread1 + sums0 + sums1 + [x_copy(0), x_copy(1)]:
            copy.wait_send()
        for chunk in range(2):
            for kind in range(4):
                for way in range(2):
                    y_copy(chunk, kind, way).wait_send()

        @pl.when(same)
        def _():
            for k in range(4):
                for part in range(2):
                    a_send(k, part, k, partner).wait_send()
                    a_send(k, part, 4 + k, twin).wait_send()
                    a_send(k, part, 8 + k, twin).wait_send()

        @pl.when(root)
        def _():
            for k in range(4):
                for part in range(2):
                    a_send(k, part, 12 + k, outer).wait_send()

    return drain


def dot(a, b):
    return jnp.dot(a, b, preferred_element_type=F32)


def finish_part(
    grad_ref, stats_ref, old_ref, rotation_ref, update_ref, stats_out, roots_out,
    both, moment, wide, low1, low2, low3, low_w, scales, rot0, rot1, rot2,
    a_send, a_recv, az_send, az_recv, ay_send, ay_recv, bz_send, bz_recv,
    x_send, x_recv, y_send, y_recv, p_send, p_recv, f_send, f_recv, q_send, q_recv,
    c_send, c_recv, rot_send, rot_recv,
):
    x_lo, y, z, x_hi, core = place()
    group = x_lo * 4 + y
    other_x = 1 - x_lo
    pair = other_x * 4 + y
    y_up, y_down, y_far = lax.rem(y + 1, 4), lax.rem(y + 3, 4), lax.rem(y + 2, 4)
    partner = device(other_x, y, z, x_hi, core)
    up_y = device(x_lo, y_up, z, x_hi, core)
    down_y = device(x_lo, y_down, z, x_hi, core)
    up_z = device(x_lo, y, lax.rem(z + 1, 8), x_hi, core)
    down_z = device(x_lo, y, lax.rem(z + 7, 8), x_hi, core)
    g_peer = []
    for k in range(1, 8):
        g = lax.rem(group + k, 8)
        g_peer.append(device(g // 4, lax.rem(g, 4), z, x_hi, core))
    z_peer = [device(x_lo, y, lax.rem(z + k, 8), x_hi, core) for k in range(1, 8)]
    rots = (rot0, rot1, rot2)

    def rotate(step):
        return remote(
            rots[step].at[0], rots[step].at[1], rot_send.at[step], rot_recv.at[step],
            g_peer[(1 << step) - 1],
        )

    def rotated(step):
        rotate(step).wait_recv()
        bit = lax.rem(rotation_ref[0] // (1 << step), 2)
        return rots[step][bit]

    side = z // 4
    quarter = pl.multiple_of(lax.rem(z, 4) * 160, 16)
    eighth = pl.multiple_of(z * 80, 16)
    grad = grad_ref[...].reshape(640, 640)
    both[0] = grad
    both[1] = grad.T

    def advance(now, later, s):
        w = dot(now[s], now[s]) - 10.0 * moment[s]
        wide[s] = w
        low_w[s] = w.astype(BF16)
        h = dot(low_w[s], low_w[s]) + 50.0 * wide[s]
        low_w[s] = h.astype(BF16)
        m = (625.0 * moment[s] + dot(now[s], low_w[s])) * (1.0 / 256.0)
        moment[s] = m
        later[s] = m.astype(BF16)

    def grow(s):
        old = stats_ref[pl.ds(s * 4, 4)].reshape(640, 640).astype(F32)
        a = BETA * old + (1.0 - BETA) * dot(both[s], both[1 - s])
        moment[s] = a
        scale = 2.5 / jnp.sqrt(jnp.sum(a * a, keepdims=True))
        scales[s] = jnp.broadcast_to(jnp.sqrt(jnp.sqrt(scale)), (8, 128))
        m = moment[s] * scale
        moment[s] = m
        low1[s] = m.astype(BF16)
        advance(low1, low2, s)
        advance(low2, low3, s)

    def factor(r, low, s):
        return 1.25 * r - 0.25 * dot(r.astype(BF16), low[s])

    def chain(r, s):
        r = factor(r, low2, s)
        r = factor(r, low3, s)
        t = r
        for _ in range(4):
            t = factor(t, low3, s)
        return 1.25 * r - 0.25 * dot(t.astype(BF16), low3[s])

    def identity(rows, offset):
        across = lax.broadcasted_iota(jnp.int32, (rows, 640), 1)
        down = lax.broadcasted_iota(jnp.int32, (rows, 640), 0) + offset
        return (across == down).astype(F32)

    def first(rows, offset, s):
        m = low1[s, pl.ds(offset, rows), :].astype(F32)
        return (1.25 * identity(rows, offset) - 0.25 * m) * scales[s, 0:1, 0:1]

    grow(side)
    rot0[0] = chain(first(160, quarter, side), side).astype(BF16)
    rotate(0).start()
    grow(1 - side)
    left = chain(first(80, eighth, 0), 0)
    rot1[0] = rotated(0)
    rotate(1).start()
    high = left.astype(BF16)
    low = (left - high.astype(F32)).astype(BF16)
    right = dot(high, both[0]) + dot(low, both[0])
    right = factor(right, low1, 1) * scales[1, 0:1, 0:1]
    right = chain(right, 1)
    update_ref[group, z] = right.astype(BF16)

    def slot(r):
        return lax.rem(z + r, 8)

    def rows(g, r, start, count):
        return update_ref.at[g, slot(r), pl.ds(start, count)]

    sent = []

    def send(ref, sems, index, peer):
        copy = remote(ref, ref, sems[0].at[index], sems[1].at[index], peer)
        copy.start()
        sent.append(copy)

    def landed(ref, sems, index):
        remote(ref, ref, sems[0].at[index], sems[1].at[index], partner).wait_recv()

    xs, ys, ps = (x_send, x_recv), (y_send, y_recv), (p_send, p_recv)
    fs, qs, cs = (f_send, f_recv), (q_send, q_recv), (c_send, c_recv)
    low, high, far = x_lo * 4 + y_down, x_lo * 4 + y_up, x_lo * 4 + y_far
    p_low, p_high, p_far = other_x * 4 + y_down, other_x * 4 + y_up, other_x * 4 + y_far

    def piece(i, part):
        start, count = ((32, 48), (32, 32), (64, 16))[part]
        return update_ref.at[group, i, pl.ds(start, count)]

    near = Near(piece, bz_send, bz_recv, z_peer, z)
    ring_a = Ring(
        lambda i: update_ref.at[pl.ds(0, 4), i, pl.ds(0, 32)], az_send, az_recv, (up_z, down_z), z
    )
    ring_c = Ring(
        lambda i: update_ref.at[pl.ds(4, 4), i, pl.ds(0, 32)], ay_send, ay_recv, (up_z, down_z), z, True
    )

    def own_out(r):
        send(rows(group, r, 32, 48), xs, r, partner)
        send(rows(group, r, 32, 48), ys, r, up_y)
        send(rows(group, r, 32, 48), ys, 8 + r, down_y)

    def pair_out(r):
        landed(rows(pair, r, 32, 48), xs, r)
        send(rows(pair, r, 32, 32), ps, r, up_y)
        send(rows(pair, r, 32, 32), ps, 8 + r, down_y)

    def own_on(r):
        landed(rows(low, r, 32, 48), ys, r)
        if r < 4:
            send(rows(low, r, 32, 48), fs, r, up_y)
        landed(rows(high, r, 32, 48), ys, 8 + r)
        if r >= 4:
            send(rows(high, r, 32, 48), fs, r, down_y)

    def pair_on(r):
        landed(rows(p_low, r, 32, 32), ps, r)
        if r < 4:
            send(rows(p_low, r, 32, 32), qs, r, up_y)
        landed(rows(p_high, r, 32, 32), ps, 8 + r)
        if r >= 4:
            send(rows(p_high, r, 32, 32), qs, r, down_y)

    def across(g, index):
        send(update_ref.at[g, :, pl.ds(64, 16)], cs, index, partner)

    over = []
    for k in range(1, 8):
        own = update_ref.at[group, z, pl.ds(0, 32)]
        copy = remote(own, own, a_send.at[k], a_recv.at[k], g_peer[k - 1])
        copy.start()
        over.append(copy)
    near.start()
    own_out(0)

    own = dot(both[side, pl.ds(quarter, 160), :], both[1 - side])
    stats_out[...] = BETA * old_ref[...] + (1.0 - BETA) * own
    near.relay()
    for copy in over:
        copy.wait_recv()
    ring_a.start(0)
    ring_c.start(0)
    own_out(6)
    own_out(2)
    near.landed(2)
    own_out(7)
    near.landed(3)
    own_out(1)
    pair_out(0)
    own_on(0)
    for r in (6, 2, 7, 1):
        pair_out(r)
    near.landed(4)
    own_out(5)
    near.landed(5)
    own_out(3)
    near.landed(6)
    near.landed(7)
    own_out(4)
    ring_a.arrived(0)
    ring_a.start(1)
    ring_c.arrived(0)
    ring_c.start(1)
    for r in (6, 2, 7, 1):
        own_on(r)
    for r in (5, 3, 4):
        pair_out(r)
    for r in (5, 3, 4):
        own_on(r)
    ring_a.arrived(1)
    ring_a.start(2)
    ring_c.arrived(1)
    ring_c.start(2)
    across(low, 0)
    across(high, 1)
    rot2[0] = rotated(1)
    rotate(2).start()
    for r in (0, 6, 2, 7, 1):
        pair_on(r)
    ring_a.arrived(2)
    ring_a.start(3)
    ring_c.arrived(2)
    ring_c.start(3)
    for r in (5, 3, 4):
        pair_on(r)
    for r in range(8):
        landed(rows(far, r, 32, 48), fs, r)
    across(far, 2)
    roots_out[...] = rotated(2).astype(F32)
    for r in range(8):
        landed(rows(p_far, r, 32, 32), qs, r)
    for index, g in enumerate((p_low, p_high, p_far)):
        landed(update_ref.at[g, :, pl.ds(64, 16)], cs, index)
    ring_a.arrived(3)
    ring_c.arrived(3)

    near.drain()
    ring_a.drain()
    ring_c.drain()
    for copy in sent + over:
        copy.wait_send()
    for step in range(3):
        rotate(step).wait_send()


GATHER_REFS = 30


def step_kernel(
    act_ref, gout_ref, old_ref, owner_ref, rotation_ref, update_ref, stats_out, roots_out,
    grad_ref, stats_ref, old_in, *rest,
):
    drain = gather_part(
        act_ref, gout_ref, old_ref, owner_ref, grad_ref, stats_ref, old_in, *rest[:GATHER_REFS]
    )
    finish_part(
        grad_ref, stats_ref, old_in, rotation_ref, update_ref, stats_out, roots_out,
        *rest[GATHER_REFS:],
    )
    drain()


def shampoo_step(activations, grad_out, old_rows, owner_map, rotation):
    hbm = pl.BlockSpec(memory_space=pltpu.HBM)
    widths = [width for _, width in CHUNKS]

    def sems(*counts):
        return [pltpu.SemaphoreType.DMA((count,)) for count in counts]

    return pl.pallas_call(
        step_kernel,
        out_shape=(
            jax.ShapeDtypeStruct((8, 8, 80, 640), BF16),
            jax.ShapeDtypeStruct((160, 640), F32),
            jax.ShapeDtypeStruct((160, 640), F32),
        ),
        in_specs=[hbm, hbm, hbm, SMEM, SMEM],
        out_specs=(VMEM, VMEM, VMEM),
        scratch_shapes=[
            pltpu.VMEM((8, 80, 640), BF16),
            pltpu.VMEM((8, 160, 640), BF16),
            pltpu.VMEM((160, 640), F32),
            pltpu.VMEM((256, 640), BF16),
            pltpu.VMEM((640, 256), BF16),
            pltpu.VMEM((640, 2048), BF16),
            pltpu.VMEM((8, 256, 640), BF16),
            *[pltpu.VMEM((640, width), F32) for width in widths],
            *[pltpu.VMEM((8, 80, width), BF16) for _ in range(3) for width in widths],
            *sems(2, 2, 2, 32, 16, 16, 16, 7, 7, 16, 16, 16, 16, 8, 8, 8, 8, 3),
            pltpu.VMEM((2, 640, 640), BF16),
            pltpu.VMEM((2, 640, 640), F32),
            pltpu.VMEM((2, 640, 640), F32),
            pltpu.VMEM((2, 640, 640), BF16),
            pltpu.VMEM((2, 640, 640), BF16),
            pltpu.VMEM((2, 640, 640), BF16),
            pltpu.VMEM((2, 640, 640), BF16),
            pltpu.VMEM((2, 8, 128), F32),
            pltpu.VMEM((2, 160, 640), BF16),
            pltpu.VMEM((2, 160, 640), BF16),
            pltpu.VMEM((2, 160, 640), BF16),
            *sems(8, 8, 7, 7, 7, 7, 8, 8, 8, 8, 16, 16, 16, 16, 8, 8, 8, 8, 3, 3, 3, 3),
        ],
        compiler_params=pltpu.CompilerParams(
            collective_id=0, has_side_effects=True, vmem_limit_bytes=44 * 2**20
        ),
        name="shampoo_step",
    )(activations, grad_out, old_rows, owner_map, rotation)


def order_kernel(owner_ref, in_ref, stats_ref, roots_ref, out_ref, stats_out, roots_out, sems):
    copies = [
        pltpu.make_async_copy(in_ref.at[owner_ref[b]], out_ref.at[b], sems.at[b]) for b in range(8)
    ]
    copies.append(pltpu.make_async_copy(stats_ref, stats_out, sems.at[8]))
    copies.append(pltpu.make_async_copy(roots_ref, roots_out, sems.at[9]))
    for copy in copies:
        copy.start()
    for copy in copies:
        copy.wait()


def order_blocks(by_place, stats_new, roots_new, owner_map):
    hbm = pl.BlockSpec(memory_space=pltpu.HBM)
    return pl.pallas_call(
        order_kernel,
        out_shape=(
            jax.ShapeDtypeStruct((8, 640, 640), BF16),
            jax.ShapeDtypeStruct((160, 640), F32),
            jax.ShapeDtypeStruct((160, 640), F32),
        ),
        in_specs=[SMEM, VMEM, VMEM, VMEM],
        out_specs=(hbm, hbm, hbm),
        scratch_shapes=[pltpu.SemaphoreType.DMA((10,))],
        compiler_params=pltpu.CompilerParams(vmem_limit_bytes=16 * 2**20),
        name="order_blocks",
    )(owner_map, by_place, stats_new, roots_new)


def local(activations, grad_out, stats_old, owner_map, rotation):
    old_rows = stats_old.reshape(160, 640)
    by_place, stats_new, roots_new = shampoo_step(
        activations, grad_out, old_rows, owner_map, rotation
    )
    update, stats_new, roots_new = order_blocks(
        by_place.reshape(8, 640, 640), stats_new, roots_new, owner_map
    )
    return (
        update.reshape(2, 2560, 640),
        stats_new.reshape(stats_old.shape),
        roots_new.reshape(stats_old.shape),
    )


def solution(mesh):
    return jax.shard_map(
        local,
        mesh=mesh,
        in_specs=(P("dp", "mp"), P("dp", "mp"), P("mp", None, "dp", None, None), P(), P()),
        out_specs=(
            P("mp", None, None),
            P("mp", None, "dp", None, None),
            P("mp", None, "dp", None, None),
        ),
        check_vma=False,
    )
```

```python
import jax
import jax.numpy as jnp
from jax import lax
from jax.experimental import pallas as pl
from jax.experimental.pallas import tpu as pltpu
from jax.sharding import PartitionSpec as P

BETA = 0.9
MESH = pl.DeviceIdType.MESH
VMEM = pl.BlockSpec(memory_space=pltpu.VMEM)
SMEM = pl.BlockSpec(memory_space=pltpu.SMEM)
F32 = jnp.float32
BF16 = jnp.bfloat16


def place():
    dp = lax.axis_index("dp")
    mp = lax.axis_index("mp")
    return dp // 32, lax.rem(dp // 8, 4), lax.rem(dp, 8), mp // 2, lax.rem(mp, 2)


def device(x_lo, y, z, x_hi, core):
    return {"dp": x_lo * 32 + y * 8 + z, "mp": x_hi * 2 + core}


def remote(src, dst, send, recv, peer):
    return pltpu.make_async_remote_copy(
        src_ref=src, dst_ref=dst, send_sem=send, recv_sem=recv, device_id=peer, device_id_type=MESH
    )


class Ring:
    def __init__(self, slot, send, recv, peers, z, down_last=False):
        self.slot, self.send, self.recv = slot, send, recv
        self.up, self.down = peers
        self.z = z
        self.steps = (3, 4) if down_last else (4, 3)

    def copy_up(self, step):
        i = lax.rem(self.z - step + 8, 8)
        return remote(self.slot(i), self.slot(i), self.send.at[step], self.recv.at[step], self.up)

    def copy_down(self, step):
        i = lax.rem(self.z + step, 8)
        index = self.steps[0] + step
        return remote(
            self.slot(i), self.slot(i), self.send.at[index], self.recv.at[index], self.down
        )

    def copies(self, step):
        ways = ((self.copy_up, self.steps[0]), (self.copy_down, self.steps[1]))
        return [copy(step) for copy, steps in ways if step < steps]

    def start(self, step):
        for copy in self.copies(step):
            copy.start()

    def arrived(self, step):
        for copy in self.copies(step):
            copy.wait_recv()

    def drain(self):
        for step in range(4):
            for copy in self.copies(step):
                copy.wait_send()


class Near:
    def __init__(self, piece, send, recv, peers, z):
        self.piece, self.send, self.recv, self.peers = piece, send, recv, peers
        self.z = z

    def copy(self, index):
        ahead, behind, part = (
            (2, 0, 0), (-2, 0, 0), (1, 0, 0), (-1, 0, 0), (1, 2, 0), (-1, 2, 0), (2, 2, 1), (-2, 2, 2)
        )[index]
        way = 1 if ahead > 0 else -1
        ref = self.piece(lax.rem(self.z - way * behind + 8, 8), part)
        return remote(ref, ref, self.send.at[index], self.recv.at[index], self.peers[ahead % 8 - 1])

    def landed(self, index):
        ahead, behind, part = (
            (2, 0, 0), (-2, 0, 0), (1, 0, 0), (-1, 0, 0), (1, 2, 0), (-1, 2, 0), (2, 2, 1), (-2, 2, 2)
        )[index]
        way = 1 if ahead > 0 else -1
        ref = self.piece(lax.rem(self.z - ahead - way * behind + 8, 8), part)
        remote(ref, ref, self.send.at[index], self.recv.at[index], self.peers[0]).wait_recv()

    def start(self):
        for index in range(4):
            self.copy(index).start()

    def relay(self):
        for index in (0, 1):
            self.landed(index)
            self.copy(4 + index).start()
            self.copy(6 + index).start()

    def finish(self):
        for index in (2, 3, 4, 5, 6, 7):
            self.landed(index)

    def drain(self):
        for index in range(8):
            self.copy(index).wait_send()


def swap(v):
    return lax.rem(v, 2) * 2 + v // 2


SWAP = (0, 2, 1, 3)
CHUNKS = ((0, 384), (384, 256))
OWN, PAIR, ON_OWN, ON_PAIR = range(4)


def gather_part(
    act_ref, gout_ref, old_ref, owner_ref, grad_ref, stats_ref, old_in,
    act_in, act_t, actg, goutg, total0, total1, part0, part1, rs0, rs1, gg0, gg1,
    x_send, x_recv, a1_sem, a2_send, a_recv, g_send, g_recv,
    st_send, st_recv, rs_send, rs_recv, gg_send, gg_recv, z0_send, z0_recv, z1_send, z1_recv,
    loc_sem,
):
    totals, parts, rss, ggs = (total0, total1), (part0, part1), (rs0, rs1), (gg0, gg1)
    x_lo, y, z, x_hi, core = place()
    mp = x_hi * 2 + core
    group = x_lo * 4 + y
    y_up, y_down, y_far = lax.rem(y + 1, 4), lax.rem(y + 3, 4), lax.rem(y + 2, 4)
    other_x = 1 - x_lo
    partner = device(other_x, y, z, x_hi, core)
    outer = device(other_x, y, z, 1 - x_hi, core)
    twin = device(x_lo, y, z, x_hi, 1 - core)
    z_peer = [device(x_lo, y, lax.rem(z + k, 8), x_hi, core) for k in range(1, 8)]
    y_peer = (device(x_lo, y_up, z, x_hi, core), device(x_lo, y_down, z, x_hi, core))
    g_peer = []
    for k in range(1, 8):
        g = lax.rem(group + k, 8)
        g_peer.append(device(g // 4, lax.rem(g, 4), z, x_hi, core))

    load_act = pltpu.make_async_copy(act_ref, act_in, loc_sem.at[0])
    load_act.start()
    load_old = pltpu.make_async_copy(old_ref, old_in, loc_sem.at[1])
    load_old.start()
    peers = z_peer + g_peer + [outer, twin]
    barrier = pltpu.get_barrier_semaphore()
    for peer in peers:
        pl.semaphore_signal(barrier, inc=1, device_id=peer, device_id_type=MESH)
    load_act.wait()
    act_t[...] = act_in[...].T
    load_old.wait()
    stats_ref[z] = old_in[...].astype(BF16)
    pl.semaphore_wait(barrier, len(peers))

    feature = swap(y)
    same = core == lax.rem(feature, 2)
    root = jnp.logical_and(same, x_hi == feature // 2)
    mid = jnp.logical_and(same, x_hi != feature // 2)
    stray = feature != mp

    def out_columns(side, chunk):
        offset, width = CHUNKS[chunk]
        return gout_ref.at[:, pl.ds(pl.multiple_of(side * 640 + offset, 128), width)]

    def g_slot(slot, chunk):
        offset, width = CHUNKS[chunk]
        return goutg.at[slot, :, pl.ds(offset, width)]

    def g_half(slot, chunk, way):
        offset, width = CHUNKS[chunk]
        return goutg.at[slot, pl.ds(way * 128, 128), pl.ds(offset, width)]

    def x_copy(chunk):
        return remote(
            out_columns(other_x, chunk), g_slot(group, chunk),
            x_send.at[chunk], x_recv.at[chunk], partner,
        )

    def x_landed(chunk):
        ref = g_slot(other_x * 4 + y, chunk)
        remote(ref, ref, x_send.at[chunk], x_recv.at[chunk], partner).wait_recv()

    def y_copy(chunk, kind, way):
        index = chunk * 8 + kind * 2 + way
        column = other_x if kind in (PAIR, ON_PAIR) else x_lo
        if kind in (OWN, PAIR):
            dst = g_slot(column * 4 + y, chunk)
            src = out_columns(x_lo, chunk) if kind == OWN else dst
        else:
            dst = g_half(column * 4 + (y_down if way == 0 else y_up), chunk, way)
            src = dst
        return remote(src, dst, g_send.at[index], g_recv.at[index], y_peer[way])

    def y_landed(chunk, kind, way):
        index = chunk * 8 + kind * 2 + way
        column = other_x if kind in (PAIR, ON_PAIR) else x_lo
        if kind in (OWN, PAIR):
            ref = g_slot(column * 4 + (y_down if way == 0 else y_up), chunk)
        else:
            ref = g_half(column * 4 + y_far, chunk, way)
        remote(ref, ref, g_send.at[index], g_recv.at[index], y_peer[way]).wait_recv()

    def y_send(chunk, kind):
        for way in range(2):
            if kind in (ON_OWN, ON_PAIR):
                y_landed(chunk, kind - 2, way)
            y_copy(chunk, kind, way).start()

    def a_slot(slot, part):
        return actg.at[pl.ds(part * 320, 320), pl.ds(pl.multiple_of(slot * 256, 256), 256)]

    def a_copy(slot, part, send, peer, own=False):
        dst = a_slot(slot, part)
        src = act_t.at[pl.ds(part * 320, 320)] if own else dst
        return remote(src, dst, send, a_recv.at[slot * 2 + part], peer)

    def a_landed(slot, part):
        a_copy(slot, part, a1_sem.at[part], partner).wait_recv()

    def a_send(slot, part, index, peer, own=False):
        return a_copy(slot, part, a2_send.at[index * 2 + part], peer, own)

    arrivals = (y, y_down, y_up, y_far)
    def a1_copy(part):
        target = device(x_lo, swap(mp), z, x_hi, core)
        return a_copy(group, part, a1_sem.at[part], target, True)

    def from_root(i):
        slot = x_lo * 4 + arrivals[i]
        for part in range(2):
            if i > 0:
                a_landed(slot, part)
            a_send(slot, part, i, partner, i == 0).start()
            a_send(slot, part, 12 + i, outer, i == 0).start()
            a_send(slot, part, 4 + i, twin, i == 0).start()

    def from_mid(i):
        slot = other_x * 4 + arrivals[i]
        for part in range(2):
            a_landed(slot, part)
            a_send(slot, part, i, partner).start()
            a_send(slot, part, 4 + i, twin).start()

    stats = Ring(lambda i: stats_ref.at[i], st_send, st_recv, (z_peer[0], z_peer[6]), z)

    @pl.when(stray)
    def _():
        a1_copy(0).start()
        a1_copy(1).start()

    x_copy(0).start()
    pl.when(root)(lambda: from_root(0))
    stats.start(0)
    x_copy(1).start()
    keep = pltpu.make_async_copy(
        gout_ref.at[:, pl.ds(pl.multiple_of(x_lo * 640, 128), 640)], goutg.at[group], loc_sem.at[2]
    )
    keep.start()

    @pl.when(jnp.logical_not(stray))
    def _():
        actg[:, pl.ds(pl.multiple_of(group * 256, 256), 256)] = act_t[...]

    @pl.when(stray)
    def _():
        a1_copy(0).wait_send()
        a1_copy(1).wait_send()

    y_send(0, OWN)
    pl.when(root)(lambda: from_root(1))
    x_landed(0)
    y_send(0, PAIR)
    stats.arrived(0)
    stats.start(1)

    @pl.when(root)
    def _():
        from_root(2)
        from_root(3)

    pl.when(mid)(lambda: from_mid(0))
    y_send(1, OWN)
    x_landed(1)
    y_send(1, PAIR)
    y_send(0, ON_OWN)
    pl.when(mid)(lambda: from_mid(1))
    stats.arrived(1)
    stats.start(2)
    y_send(0, ON_PAIR)
    pl.when(mid)(lambda: from_mid(2))
    stats.arrived(2)
    stats.start(3)
    pl.when(mid)(lambda: from_mid(3))

    first = jnp.where(root, x_lo, other_x)

    @pl.when(same)
    def _():
        for i in range(4):
            slot = (1 - first) * 4 + arrivals[i]
            for part in range(2):
                a_landed(slot, part)
                a_send(slot, part, 8 + i, twin).start()

    @pl.when(jnp.logical_not(same))
    def _():
        for slot in range(8):
            a_landed(slot, 0)
            a_landed(slot, 1)

    keep.wait()

    def z_sum(chunk):
        offset, width = CHUNKS[chunk]
        for kind in (ON_OWN, ON_PAIR):
            for way in range(2):
                y_landed(chunk, kind, way)
        right = goutg[:, :, offset : offset + width].reshape(2048, width)
        product = jnp.dot(actg[...], right, preferred_element_type=F32)
        totals[chunk][...] = product
        parts[chunk][...] = product.astype(BF16).reshape(8, 80, width)
        sent = []
        for k in range(1, 8):
            to = lax.rem(z + k, 8)
            copy = remote(
                parts[chunk].at[to], rss[chunk].at[k],
                rs_send.at[chunk * 8 + k], rs_recv.at[chunk * 8 + k], z_peer[k - 1],
            )
            copy.start()
            sent.append(copy)
        return sent

    def group_spread(chunk, sums):
        rows = totals[chunk][pl.ds(pl.multiple_of(z * 80, 8), 80), :]
        for k in range(1, 8):
            sums[k - 1].wait_recv()
            rows = rows + rss[chunk][k].astype(F32)
        ggs[chunk][group] = rows.astype(BF16)
        sent = []
        for k in range(1, 8):
            own = ggs[chunk].at[group]
            copy = remote(
                own, own, gg_send.at[chunk * 8 + k], gg_recv.at[chunk * 8 + k], g_peer[k - 1]
            )
            copy.start()
            sent.append(copy)
        return sent

    block = jnp.int32(0)
    for b in range(8):
        block = jnp.where(owner_ref[b] == group, b // 4 * 4 + SWAP[b % 4], block)

    def pick(chunk, spread):
        offset, width = CHUNKS[chunk]
        for copy in spread:
            copy.wait_recv()
        grad_ref[z, :, offset : offset + width] = ggs[chunk][block]
        sems = ((z0_send, z0_recv), (z1_send, z1_recv))[chunk]

        def piece(i, part):
            start, count = ((0, 80), (0, 48), (48, 32))[part]
            return grad_ref.at[i, pl.ds(start, count), pl.ds(offset, width)]

        near = Near(piece, *sems, z_peer, z)
        near.start()
        return near

    sums0 = z_sum(0)
    y_send(1, ON_OWN)
    y_send(1, ON_PAIR)
    sums1 = z_sum(1)
    stats.arrived(3)
    spread0 = group_spread(0, sums0)
    near0 = pick(0, spread0)
    spread1 = group_spread(1, sums1)
    near0.relay()
    near1 = pick(1, spread1)
    near1.relay()
    near0.finish()
    near1.finish()

    def drain():
        near0.drain()
        near1.drain()
        stats.drain()
        for copy in spread0 + spread1 + sums0 + sums1 + [x_copy(0), x_copy(1)]:
            copy.wait_send()
        for chunk in range(2):
            for kind in range(4):
                for way in range(2):
                    y_copy(chunk, kind, way).wait_send()

        @pl.when(same)
        def _():
            for k in range(4):
                for part in range(2):
                    a_send(k, part, k, partner).wait_send()
                    a_send(k, part, 4 + k, twin).wait_send()
                    a_send(k, part, 8 + k, twin).wait_send()

        @pl.when(root)
        def _():
            for k in range(4):
                for part in range(2):
                    a_send(k, part, 12 + k, outer).wait_send()

    return drain


def dot(a, b):
    return jnp.dot(a, b, preferred_element_type=F32)


def finish_part(
    grad_ref, stats_ref, old_ref, rotation_ref, update_ref, stats_out, roots_out,
    both, moment, wide, low1, low2, low3, low_w, scales, rot0, rot1, rot2,
    a_send, a_recv, az_send, az_recv, ay_send, ay_recv, bz_send, bz_recv,
    x_send, x_recv, y_send, y_recv, p_send, p_recv, f_send, f_recv, q_send, q_recv,
    c_send, c_recv, rot_send, rot_recv,
):
    x_lo, y, z, x_hi, core = place()
    group = x_lo * 4 + y
    other_x = 1 - x_lo
    pair = other_x * 4 + y
    y_up, y_down, y_far = lax.rem(y + 1, 4), lax.rem(y + 3, 4), lax.rem(y + 2, 4)
    partner = device(other_x, y, z, x_hi, core)
    up_y = device(x_lo, y_up, z, x_hi, core)
    down_y = device(x_lo, y_down, z, x_hi, core)
    up_z = device(x_lo, y, lax.rem(z + 1, 8), x_hi, core)
    down_z = device(x_lo, y, lax.rem(z + 7, 8), x_hi, core)
    g_peer = []
    for k in range(1, 8):
        g = lax.rem(group + k, 8)
        g_peer.append(device(g // 4, lax.rem(g, 4), z, x_hi, core))
    z_peer = [device(x_lo, y, lax.rem(z + k, 8), x_hi, core) for k in range(1, 8)]
    rots = (rot0, rot1, rot2)

    def rotate(step):
        return remote(
            rots[step].at[0], rots[step].at[1], rot_send.at[step], rot_recv.at[step],
            g_peer[(1 << step) - 1],
        )

    def rotated(step):
        rotate(step).wait_recv()
        bit = lax.rem(rotation_ref[0] // (1 << step), 2)
        return rots[step][bit]

    side = z // 4
    quarter = pl.multiple_of(lax.rem(z, 4) * 160, 16)
    eighth = pl.multiple_of(z * 80, 16)
    grad = grad_ref[...].reshape(640, 640)
    both[0] = grad
    both[1] = grad.T

    def advance(now, later, s):
        w = dot(now[s], now[s]) - 10.0 * moment[s]
        wide[s] = w
        low_w[s] = w.astype(BF16)
        h = dot(low_w[s], low_w[s]) + 50.0 * wide[s]
        low_w[s] = h.astype(BF16)
        m = (625.0 * moment[s] + dot(now[s], low_w[s])) * (1.0 / 256.0)
        moment[s] = m
        later[s] = m.astype(BF16)

    def grow(s):
        old = stats_ref[pl.ds(s * 4, 4)].reshape(640, 640).astype(F32)
        a = BETA * old + (1.0 - BETA) * dot(both[s], both[1 - s])
        moment[s] = a
        scale = 2.5 / jnp.sqrt(jnp.sum(a * a, keepdims=True))
        scales[s] = jnp.broadcast_to(jnp.sqrt(jnp.sqrt(scale)), (8, 128))
        m = moment[s] * scale
        moment[s] = m
        low1[s] = m.astype(BF16)
        advance(low1, low2, s)
        advance(low2, low3, s)

    def factor(r, low, s):
        return 1.25 * r - 0.25 * dot(r.astype(BF16), low[s])

    def chain(r, s):
        r = factor(r, low2, s)
        r = factor(r, low3, s)
        t = r
        for _ in range(4):
            t = factor(t, low3, s)
        return 1.25 * r - 0.25 * dot(t.astype(BF16), low3[s])

    def identity(rows, offset):
        across = lax.broadcasted_iota(jnp.int32, (rows, 640), 1)
        down = lax.broadcasted_iota(jnp.int32, (rows, 640), 0) + offset
        return (across == down).astype(F32)

    def first(rows, offset, s):
        m = low1[s, pl.ds(offset, rows), :].astype(F32)
        return (1.25 * identity(rows, offset) - 0.25 * m) * scales[s, 0:1, 0:1]

    grow(side)
    rot0[0] = chain(first(160, quarter, side), side).astype(BF16)
    rotate(0).start()
    grow(1 - side)
    left = chain(first(80, eighth, 0), 0)
    rot1[0] = rotated(0)
    rotate(1).start()
    high = left.astype(BF16)
    low = (left - high.astype(F32)).astype(BF16)
    right = dot(high, both[0]) + dot(low, both[0])
    right = factor(right, low1, 1) * scales[1, 0:1, 0:1]
    right = chain(right, 1)
    update_ref[group, z] = right.astype(BF16)

    def slot(r):
        return lax.rem(z + r, 8)

    def rows(g, r, start, count):
        return update_ref.at[g, slot(r), pl.ds(start, count)]

    sent = []

    def send(ref, sems, index, peer):
        copy = remote(ref, ref, sems[0].at[index], sems[1].at[index], peer)
        copy.start()
        sent.append(copy)

    def landed(ref, sems, index):
        remote(ref, ref, sems[0].at[index], sems[1].at[index], partner).wait_recv()

    xs, ys, ps = (x_send, x_recv), (y_send, y_recv), (p_send, p_recv)
    fs, qs, cs = (f_send, f_recv), (q_send, q_recv), (c_send, c_recv)
    low, high, far = x_lo * 4 + y_down, x_lo * 4 + y_up, x_lo * 4 + y_far
    p_low, p_high, p_far = other_x * 4 + y_down, other_x * 4 + y_up, other_x * 4 + y_far

    def piece(i, part):
        start, count = ((32, 48), (32, 32), (64, 16))[part]
        return update_ref.at[group, i, pl.ds(start, count)]

    near = Near(piece, bz_send, bz_recv, z_peer, z)
    ring_a = Ring(
        lambda i: update_ref.at[pl.ds(0, 4), i, pl.ds(0, 32)], az_send, az_recv, (up_z, down_z), z
    )
    ring_c = Ring(
        lambda i: update_ref.at[pl.ds(4, 4), i, pl.ds(0, 32)], ay_send, ay_recv, (up_z, down_z), z, True
    )

    def own_out(r):
        send(rows(group, r, 32, 48), xs, r, partner)
        send(rows(group, r, 32, 48), ys, r, up_y)
        send(rows(group, r, 32, 48), ys, 8 + r, down_y)

    def pair_out(r):
        landed(rows(pair, r, 32, 48), xs, r)
        send(rows(pair, r, 32, 32), ps, r, up_y)
        send(rows(pair, r, 32, 32), ps, 8 + r, down_y)

    def own_on(r):
        landed(rows(low, r, 32, 48), ys, r)
        if r < 4:
            send(rows(low, r, 32, 48), fs, r, up_y)
        landed(rows(high, r, 32, 48), ys, 8 + r)
        if r >= 4:
            send(rows(high, r, 32, 48), fs, r, down_y)

    def pair_on(r):
        landed(rows(p_low, r, 32, 32), ps, r)
        if r < 4:
            send(rows(p_low, r, 32, 32), qs, r, up_y)
        landed(rows(p_high, r, 32, 32), ps, 8 + r)
        if r >= 4:
            send(rows(p_high, r, 32, 32), qs, r, down_y)

    def across(g, index):
        send(update_ref.at[g, :, pl.ds(64, 16)], cs, index, partner)

    over = []
    for k in range(1, 8):
        own = update_ref.at[group, z, pl.ds(0, 32)]
        copy = remote(own, own, a_send.at[k], a_recv.at[k], g_peer[k - 1])
        copy.start()
        over.append(copy)
    near.start()
    own_out(0)

    own = dot(both[side, pl.ds(quarter, 160), :], both[1 - side])
    stats_out[...] = BETA * old_ref[...] + (1.0 - BETA) * own
    near.relay()
    for copy in over:
        copy.wait_recv()
    ring_a.start(0)
    ring_c.start(0)
    own_out(6)
    own_out(2)
    near.landed(2)
    own_out(7)
    near.landed(3)
    own_out(1)
    pair_out(0)
    own_on(0)
    for r in (6, 2, 7, 1):
        pair_out(r)
    near.landed(4)
    own_out(5)
    near.landed(5)
    own_out(3)
    near.landed(6)
    near.landed(7)
    own_out(4)
    ring_a.arrived(0)
    ring_a.start(1)
    ring_c.arrived(0)
    ring_c.start(1)
    for r in (6, 2, 7, 1):
        own_on(r)
    for r in (5, 3, 4):
        pair_out(r)
    for r in (5, 3, 4):
        own_on(r)
    ring_a.arrived(1)
    ring_a.start(2)
    ring_c.arrived(1)
    ring_c.start(2)
    across(low, 0)
    across(high, 1)
    rot2[0] = rotated(1)
    rotate(2).start()
    for r in (0, 6, 2, 7, 1):
        pair_on(r)
    ring_a.arrived(2)
    ring_a.start(3)
    ring_c.arrived(2)
    ring_c.start(3)
    for r in (5, 3, 4):
        pair_on(r)
    for r in range(8):
        landed(rows(far, r, 32, 48), fs, r)
    across(far, 2)
    roots_out[...] = rotated(2).astype(F32)
    for r in range(8):
        landed(rows(p_far, r, 32, 32), qs, r)
    for index, g in enumerate((p_low, p_high, p_far)):
        landed(update_ref.at[g, :, pl.ds(64, 16)], cs, index)
    ring_a.arrived(3)
    ring_c.arrived(3)

    near.drain()
    ring_a.drain()
    ring_c.drain()
    for copy in sent + over:
        copy.wait_send()
    for step in range(3):
        rotate(step).wait_send()


GATHER_REFS = 30


def step_kernel(
    act_ref, gout_ref, old_ref, owner_ref, rotation_ref, update_ref, stats_out, roots_out,
    grad_ref, stats_ref, old_in, *rest,
):
    drain = gather_part(
        act_ref, gout_ref, old_ref, owner_ref, grad_ref, stats_ref, old_in, *rest[:GATHER_REFS]
    )
    finish_part(
        grad_ref, stats_ref, old_in, rotation_ref, update_ref, stats_out, roots_out,
        *rest[GATHER_REFS:],
    )
    drain()


def shampoo_step(activations, grad_out, old_rows, owner_map, rotation):
    hbm = pl.BlockSpec(memory_space=pltpu.HBM)
    widths = [width for _, width in CHUNKS]

    def sems(*counts):
        return [pltpu.SemaphoreType.DMA((count,)) for count in counts]

    return pl.pallas_call(
        step_kernel,
        out_shape=(
            jax.ShapeDtypeStruct((8, 8, 80, 640), BF16),
            jax.ShapeDtypeStruct((160, 640), F32),
            jax.ShapeDtypeStruct((160, 640), F32),
        ),
        in_specs=[hbm, hbm, hbm, SMEM, SMEM],
        out_specs=(VMEM, VMEM, VMEM),
        scratch_shapes=[
            pltpu.VMEM((8, 80, 640), BF16),
            pltpu.VMEM((8, 160, 640), BF16),
            pltpu.VMEM((160, 640), F32),
            pltpu.VMEM((256, 640), BF16),
            pltpu.VMEM((640, 256), BF16),
            pltpu.VMEM((640, 2048), BF16),
            pltpu.VMEM((8, 256, 640), BF16),
            *[pltpu.VMEM((640, width), F32) for width in widths],
            *[pltpu.VMEM((8, 80, width), BF16) for _ in range(3) for width in widths],
            *sems(2, 2, 2, 32, 16, 16, 16, 7, 7, 16, 16, 16, 16, 8, 8, 8, 8, 3),
            pltpu.VMEM((2, 640, 640), BF16),
            pltpu.VMEM((2, 640, 640), F32),
            pltpu.VMEM((2, 640, 640), F32),
            pltpu.VMEM((2, 640, 640), BF16),
            pltpu.VMEM((2, 640, 640), BF16),
            pltpu.VMEM((2, 640, 640), BF16),
            pltpu.VMEM((2, 640, 640), BF16),
            pltpu.VMEM((2, 8, 128), F32),
            pltpu.VMEM((2, 160, 640), BF16),
            pltpu.VMEM((2, 160, 640), BF16),
            pltpu.VMEM((2, 160, 640), BF16),
            *sems(8, 8, 7, 7, 7, 7, 8, 8, 8, 8, 16, 16, 16, 16, 8, 8, 8, 8, 3, 3, 3, 3),
        ],
        compiler_params=pltpu.CompilerParams(
            collective_id=0, has_side_effects=True, vmem_limit_bytes=44 * 2**20
        ),
        name="shampoo_step",
    )(activations, grad_out, old_rows, owner_map, rotation)


def order_kernel(owner_ref, in_ref, stats_ref, roots_ref, out_ref, stats_out, roots_out, sems):
    copies = [
        pltpu.make_async_copy(in_ref.at[owner_ref[b]], out_ref.at[b], sems.at[b]) for b in range(8)
    ]
    copies.append(pltpu.make_async_copy(stats_ref, stats_out, sems.at[8]))
    copies.append(pltpu.make_async_copy(roots_ref, roots_out, sems.at[9]))
    for copy in copies:
        copy.start()
    for copy in copies:
        copy.wait()


def order_blocks(by_place, stats_new, roots_new, owner_map):
    hbm = pl.BlockSpec(memory_space=pltpu.HBM)
    return pl.pallas_call(
        order_kernel,
        out_shape=(
            jax.ShapeDtypeStruct((8, 640, 640), BF16),
            jax.ShapeDtypeStruct((160, 640), F32),
            jax.ShapeDtypeStruct((160, 640), F32),
        ),
        in_specs=[SMEM, VMEM, VMEM, VMEM],
        out_specs=(hbm, hbm, hbm),
        scratch_shapes=[pltpu.SemaphoreType.DMA((10,))],
        compiler_params=pltpu.CompilerParams(vmem_limit_bytes=16 * 2**20),
        name="order_blocks",
    )(owner_map, by_place, stats_new, roots_new)


def local(activations, grad_out, stats_old, owner_map, rotation):
    old_rows = stats_old.reshape(160, 640)
    activations, grad_out, old_rows = (
        pltpu.with_memory_space_constraint(x, pltpu.HBM)
        for x in (activations, grad_out, old_rows)
    )
    by_place, stats_new, roots_new = shampoo_step(
        activations, grad_out, old_rows, owner_map, rotation
    )
    update, stats_new, roots_new = order_blocks(
        by_place.reshape(8, 640, 640), stats_new, roots_new, owner_map
    )
    return (
        update.reshape(2, 2560, 640),
        stats_new.reshape(stats_old.shape),
        roots_new.reshape(stats_old.shape),
    )


def solution(mesh):
    return jax.shard_map(
        local,
        mesh=mesh,
        in_specs=(P("dp", "mp"), P("dp", "mp"), P("mp", None, "dp", None, None), P(), P()),
        out_specs=(
            P("mp", None, None),
            P("mp", None, "dp", None, None),
            P("mp", None, "dp", None, None),
        ),
        check_vma=False,
    )
```

```python
import jax
import jax.numpy as jnp
from jax import lax
from jax.experimental import pallas as pl
from jax.experimental.pallas import tpu as pltpu
from jax.sharding import PartitionSpec as P

BETA = 0.9
MESH = pl.DeviceIdType.MESH
VMEM = pl.BlockSpec(memory_space=pltpu.VMEM)
SMEM = pl.BlockSpec(memory_space=pltpu.SMEM)
F32 = jnp.float32
BF16 = jnp.bfloat16


def place():
    dp = lax.axis_index("dp")
    mp = lax.axis_index("mp")
    return dp // 32, lax.rem(dp // 8, 4), lax.rem(dp, 8), mp // 2, lax.rem(mp, 2)


def device(x_lo, y, z, x_hi, core):
    return {"dp": x_lo * 32 + y * 8 + z, "mp": x_hi * 2 + core}


def remote(src, dst, send, recv, peer):
    return pltpu.make_async_remote_copy(
        src_ref=src, dst_ref=dst, send_sem=send, recv_sem=recv, device_id=peer, device_id_type=MESH
    )


class Ring:
    def __init__(self, slot, send, recv, peers, z, down_last=False):
        self.slot, self.send, self.recv = slot, send, recv
        self.up, self.down = peers
        self.z = z
        self.steps = (3, 4) if down_last else (4, 3)

    def copy_up(self, step):
        i = lax.rem(self.z - step + 8, 8)
        return remote(self.slot(i), self.slot(i), self.send.at[step], self.recv.at[step], self.up)

    def copy_down(self, step):
        i = lax.rem(self.z + step, 8)
        index = self.steps[0] + step
        return remote(
            self.slot(i), self.slot(i), self.send.at[index], self.recv.at[index], self.down
        )

    def copies(self, step):
        ways = ((self.copy_up, self.steps[0]), (self.copy_down, self.steps[1]))
        return [copy(step) for copy, steps in ways if step < steps]

    def start(self, step):
        for copy in self.copies(step):
            copy.start()

    def arrived(self, step):
        for copy in self.copies(step):
            copy.wait_recv()

    def drain(self):
        for step in range(4):
            for copy in self.copies(step):
                copy.wait_send()


class Near:
    def __init__(self, piece, send, recv, peers, z):
        self.piece, self.send, self.recv, self.peers = piece, send, recv, peers
        self.z = z

    def copy(self, index):
        ahead, behind, part = (
            (2, 0, 0), (-2, 0, 0), (1, 0, 0), (-1, 0, 0), (1, 2, 0), (-1, 2, 0), (2, 2, 1), (-2, 2, 2)
        )[index]
        way = 1 if ahead > 0 else -1
        ref = self.piece(lax.rem(self.z - way * behind + 8, 8), part)
        return remote(ref, ref, self.send.at[index], self.recv.at[index], self.peers[ahead % 8 - 1])

    def landed(self, index):
        ahead, behind, part = (
            (2, 0, 0), (-2, 0, 0), (1, 0, 0), (-1, 0, 0), (1, 2, 0), (-1, 2, 0), (2, 2, 1), (-2, 2, 2)
        )[index]
        way = 1 if ahead > 0 else -1
        ref = self.piece(lax.rem(self.z - ahead - way * behind + 8, 8), part)
        remote(ref, ref, self.send.at[index], self.recv.at[index], self.peers[0]).wait_recv()

    def start(self):
        for index in range(4):
            self.copy(index).start()

    def relay(self):
        for index in (0, 1):
            self.landed(index)
            self.copy(4 + index).start()
            self.copy(6 + index).start()

    def finish(self):
        for index in (2, 3, 4, 5, 6, 7):
            self.landed(index)

    def drain(self):
        for index in range(8):
            self.copy(index).wait_send()


def swap(v):
    return lax.rem(v, 2) * 2 + v // 2


SWAP = (0, 2, 1, 3)
CHUNKS = ((0, 384), (384, 256))
OWN, PAIR, ON_OWN, ON_PAIR = range(4)


def gather_part(
    act_ref, gout_ref, old_ref, owner_ref, grad_ref, stats_ref, old_in,
    act_in, act_t, actg, goutg, total0, total1, part0, part1, rs0, rs1, gg0, gg1,
    x_send, x_recv, a1_sem, a2_send, a_recv, g_send, g_recv,
    st_send, st_recv, rs_send, rs_recv, gg_send, gg_recv, z0_send, z0_recv, z1_send, z1_recv,
    loc_sem,
):
    totals, parts, rss, ggs = (total0, total1), (part0, part1), (rs0, rs1), (gg0, gg1)
    x_lo, y, z, x_hi, core = place()
    mp = x_hi * 2 + core
    group = x_lo * 4 + y
    y_up, y_down, y_far = lax.rem(y + 1, 4), lax.rem(y + 3, 4), lax.rem(y + 2, 4)
    other_x = 1 - x_lo
    partner = device(other_x, y, z, x_hi, core)
    outer = device(other_x, y, z, 1 - x_hi, core)
    twin = device(x_lo, y, z, x_hi, 1 - core)
    z_peer = [device(x_lo, y, lax.rem(z + k, 8), x_hi, core) for k in range(1, 8)]
    y_peer = (device(x_lo, y_up, z, x_hi, core), device(x_lo, y_down, z, x_hi, core))
    g_peer = []
    for k in range(1, 8):
        g = lax.rem(group + k, 8)
        g_peer.append(device(g // 4, lax.rem(g, 4), z, x_hi, core))

    load_act = pltpu.make_async_copy(act_ref, act_in, loc_sem.at[0])
    load_act.start()
    load_old = pltpu.make_async_copy(old_ref, old_in, loc_sem.at[1])
    load_old.start()
    peers = z_peer + g_peer + [outer, twin]
    barrier = pltpu.get_barrier_semaphore()
    for peer in peers:
        pl.semaphore_signal(barrier, inc=1, device_id=peer, device_id_type=MESH)
    load_act.wait()
    act_t[...] = act_in[...].T
    load_old.wait()
    stats_ref[z] = old_in[...].astype(BF16)
    pl.semaphore_wait(barrier, len(peers))

    feature = swap(y)
    same = core == lax.rem(feature, 2)
    root = jnp.logical_and(same, x_hi == feature // 2)
    mid = jnp.logical_and(same, x_hi != feature // 2)
    stray = feature != mp

    def out_columns(side, chunk):
        offset, width = CHUNKS[chunk]
        return gout_ref.at[:, pl.ds(pl.multiple_of(side * 640 + offset, 128), width)]

    def g_slot(slot, chunk):
        offset, width = CHUNKS[chunk]
        return goutg.at[slot, :, pl.ds(offset, width)]

    def g_half(slot, chunk, way):
        offset, width = CHUNKS[chunk]
        return goutg.at[slot, pl.ds(way * 128, 128), pl.ds(offset, width)]

    def x_copy(chunk):
        return remote(
            out_columns(other_x, chunk), g_slot(group, chunk),
            x_send.at[chunk], x_recv.at[chunk], partner,
        )

    def x_landed(chunk):
        ref = g_slot(other_x * 4 + y, chunk)
        remote(ref, ref, x_send.at[chunk], x_recv.at[chunk], partner).wait_recv()

    def y_copy(chunk, kind, way):
        index = chunk * 8 + kind * 2 + way
        column = other_x if kind in (PAIR, ON_PAIR) else x_lo
        if kind in (OWN, PAIR):
            dst = g_slot(column * 4 + y, chunk)
            src = out_columns(x_lo, chunk) if kind == OWN else dst
        else:
            dst = g_half(column * 4 + (y_down if way == 0 else y_up), chunk, way)
            src = dst
        return remote(src, dst, g_send.at[index], g_recv.at[index], y_peer[way])

    def y_landed(chunk, kind, way):
        index = chunk * 8 + kind * 2 + way
        column = other_x if kind in (PAIR, ON_PAIR) else x_lo
        if kind in (OWN, PAIR):
            ref = g_slot(column * 4 + (y_down if way == 0 else y_up), chunk)
        else:
            ref = g_half(column * 4 + y_far, chunk, way)
        remote(ref, ref, g_send.at[index], g_recv.at[index], y_peer[way]).wait_recv()

    def y_send(chunk, kind):
        for way in range(2):
            if kind in (ON_OWN, ON_PAIR):
                y_landed(chunk, kind - 2, way)
            y_copy(chunk, kind, way).start()

    def a_slot(slot, part):
        return actg.at[pl.ds(part * 320, 320), pl.ds(pl.multiple_of(slot * 256, 256), 256)]

    def a_copy(slot, part, send, peer, own=False):
        dst = a_slot(slot, part)
        src = act_t.at[pl.ds(part * 320, 320)] if own else dst
        return remote(src, dst, send, a_recv.at[slot * 2 + part], peer)

    def a_landed(slot, part):
        a_copy(slot, part, a1_sem.at[part], partner).wait_recv()

    def a_send(slot, part, index, peer, own=False):
        return a_copy(slot, part, a2_send.at[index * 2 + part], peer, own)

    arrivals = (y, y_down, y_up, y_far)
    def a1_copy(part):
        target = device(x_lo, swap(mp), z, x_hi, core)
        return a_copy(group, part, a1_sem.at[part], target, True)

    def from_root(i):
        slot = x_lo * 4 + arrivals[i]
        for part in range(2):
            if i > 0:
                a_landed(slot, part)
            a_send(slot, part, i, partner, i == 0).start()
            a_send(slot, part, 12 + i, outer, i == 0).start()
            a_send(slot, part, 4 + i, twin, i == 0).start()

    def from_mid(i):
        slot = other_x * 4 + arrivals[i]
        for part in range(2):
            a_landed(slot, part)
            a_send(slot, part, i, partner).start()
            a_send(slot, part, 4 + i, twin).start()

    stats = Ring(lambda i: stats_ref.at[i], st_send, st_recv, (z_peer[0], z_peer[6]), z)

    @pl.when(stray)
    def _():
        a1_copy(0).start()
        a1_copy(1).start()

    x_copy(0).start()
    pl.when(root)(lambda: from_root(0))
    stats.start(0)
    x_copy(1).start()
    keep = pltpu.make_async_copy(
        gout_ref.at[:, pl.ds(pl.multiple_of(x_lo * 640, 128), 640)], goutg.at[group], loc_sem.at[2]
    )
    keep.start()

    @pl.when(jnp.logical_not(stray))
    def _():
        actg[:, pl.ds(pl.multiple_of(group * 256, 256), 256)] = act_t[...]

    @pl.when(stray)
    def _():
        a1_copy(0).wait_send()
        a1_copy(1).wait_send()

    y_send(0, OWN)
    pl.when(root)(lambda: from_root(1))
    x_landed(0)
    y_send(0, PAIR)
    stats.arrived(0)
    stats.start(1)

    @pl.when(root)
    def _():
        from_root(2)
        from_root(3)

    pl.when(mid)(lambda: from_mid(0))
    y_send(1, OWN)
    x_landed(1)
    y_send(1, PAIR)
    y_send(0, ON_OWN)
    pl.when(mid)(lambda: from_mid(1))
    stats.arrived(1)
    stats.start(2)
    y_send(0, ON_PAIR)
    pl.when(mid)(lambda: from_mid(2))
    stats.arrived(2)
    stats.start(3)
    pl.when(mid)(lambda: from_mid(3))

    first = jnp.where(root, x_lo, other_x)

    @pl.when(same)
    def _():
        for i in range(4):
            slot = (1 - first) * 4 + arrivals[i]
            for part in range(2):
                a_landed(slot, part)
                a_send(slot, part, 8 + i, twin).start()

    @pl.when(jnp.logical_not(same))
    def _():
        for slot in range(8):
            a_landed(slot, 0)
            a_landed(slot, 1)

    keep.wait()

    def z_sum(chunk):
        offset, width = CHUNKS[chunk]
        for kind in (ON_OWN, ON_PAIR):
            for way in range(2):
                y_landed(chunk, kind, way)
        right = goutg[:, :, offset : offset + width].reshape(2048, width)
        product = jnp.dot(actg[...], right, preferred_element_type=F32)
        totals[chunk][...] = product
        parts[chunk][...] = product.astype(BF16).reshape(8, 80, width)
        sent = []
        for k in range(1, 8):
            to = lax.rem(z + k, 8)
            copy = remote(
                parts[chunk].at[to], rss[chunk].at[k],
                rs_send.at[chunk * 8 + k], rs_recv.at[chunk * 8 + k], z_peer[k - 1],
            )
            copy.start()
            sent.append(copy)
        return sent

    def group_spread(chunk, sums):
        rows = totals[chunk][pl.ds(pl.multiple_of(z * 80, 8), 80), :]
        for k in range(1, 8):
            sums[k - 1].wait_recv()
            rows = rows + rss[chunk][k].astype(F32)
        ggs[chunk][group] = rows.astype(BF16)
        sent = []
        for k in range(1, 8):
            own = ggs[chunk].at[group]
            copy = remote(
                own, own, gg_send.at[chunk * 8 + k], gg_recv.at[chunk * 8 + k], g_peer[k - 1]
            )
            copy.start()
            sent.append(copy)
        return sent

    block = jnp.int32(0)
    for b in range(8):
        block = jnp.where(owner_ref[b] == group, b // 4 * 4 + SWAP[b % 4], block)

    def pick(chunk, spread):
        offset, width = CHUNKS[chunk]
        for copy in spread:
            copy.wait_recv()
        grad_ref[z, :, offset : offset + width] = ggs[chunk][block]
        sems = ((z0_send, z0_recv), (z1_send, z1_recv))[chunk]

        def piece(i, part):
            start, count = ((0, 80), (0, 48), (48, 32))[part]
            return grad_ref.at[i, pl.ds(start, count), pl.ds(offset, width)]

        near = Near(piece, *sems, z_peer, z)
        near.start()
        return near

    sums0 = z_sum(0)
    y_send(1, ON_OWN)
    y_send(1, ON_PAIR)
    sums1 = z_sum(1)
    stats.arrived(3)
    spread0 = group_spread(0, sums0)
    near0 = pick(0, spread0)
    spread1 = group_spread(1, sums1)
    near0.relay()
    near1 = pick(1, spread1)
    near1.relay()
    near0.finish()
    near1.finish()

    def drain():
        near0.drain()
        near1.drain()
        stats.drain()
        for copy in spread0 + spread1 + sums0 + sums1 + [x_copy(0), x_copy(1)]:
            copy.wait_send()
        for chunk in range(2):
            for kind in range(4):
                for way in range(2):
                    y_copy(chunk, kind, way).wait_send()

        @pl.when(same)
        def _():
            for k in range(4):
                for part in range(2):
                    a_send(k, part, k, partner).wait_send()
                    a_send(k, part, 4 + k, twin).wait_send()
                    a_send(k, part, 8 + k, twin).wait_send()

        @pl.when(root)
        def _():
            for k in range(4):
                for part in range(2):
                    a_send(k, part, 12 + k, outer).wait_send()

    return drain


def dot(a, b):
    return jnp.dot(a, b, preferred_element_type=F32)


def finish_part(
    grad_ref, stats_ref, old_ref, rotation_ref, update_ref, stats_out, roots_out,
    both, moment, wide, low1, low2, low3, low_w, scales, rot0, rot1, rot2,
    a_send, a_recv, az_send, az_recv, ay_send, ay_recv, bz_send, bz_recv,
    x_send, x_recv, y_send, y_recv, p_send, p_recv, f_send, f_recv, q_send, q_recv,
    c_send, c_recv, rot_send, rot_recv,
):
    x_lo, y, z, x_hi, core = place()
    group = x_lo * 4 + y
    other_x = 1 - x_lo
    pair = other_x * 4 + y
    y_up, y_down, y_far = lax.rem(y + 1, 4), lax.rem(y + 3, 4), lax.rem(y + 2, 4)
    partner = device(other_x, y, z, x_hi, core)
    up_y = device(x_lo, y_up, z, x_hi, core)
    down_y = device(x_lo, y_down, z, x_hi, core)
    up_z = device(x_lo, y, lax.rem(z + 1, 8), x_hi, core)
    down_z = device(x_lo, y, lax.rem(z + 7, 8), x_hi, core)
    g_peer = []
    for k in range(1, 8):
        g = lax.rem(group + k, 8)
        g_peer.append(device(g // 4, lax.rem(g, 4), z, x_hi, core))
    z_peer = [device(x_lo, y, lax.rem(z + k, 8), x_hi, core) for k in range(1, 8)]
    rots = (rot0, rot1, rot2)

    def rotate(step):
        return remote(
            rots[step].at[0], rots[step].at[1], rot_send.at[step], rot_recv.at[step],
            g_peer[(1 << step) - 1],
        )

    def rotated(step):
        rotate(step).wait_recv()
        bit = lax.rem(rotation_ref[0] // (1 << step), 2)
        return rots[step][bit]

    side = z // 4
    quarter = pl.multiple_of(lax.rem(z, 4) * 160, 16)
    eighth = pl.multiple_of(z * 80, 16)
    grad = grad_ref[...].reshape(640, 640)
    both[0] = grad
    both[1] = grad.T

    def advance(now, later, s):
        w = dot(now[s], now[s]) - 10.0 * moment[s]
        wide[s] = w
        low_w[s] = w.astype(BF16)
        h = dot(low_w[s], low_w[s]) + 50.0 * wide[s]
        low_w[s] = h.astype(BF16)
        m = (625.0 * moment[s] + dot(now[s], low_w[s])) * (1.0 / 256.0)
        moment[s] = m
        later[s] = m.astype(BF16)

    def grow(s):
        old = stats_ref[pl.ds(s * 4, 4)].reshape(640, 640).astype(F32)
        a = BETA * old + (1.0 - BETA) * dot(both[s], both[1 - s])
        moment[s] = a
        scale = 2.5 / jnp.sqrt(jnp.sum(a * a, keepdims=True))
        scales[s] = jnp.broadcast_to(jnp.sqrt(jnp.sqrt(scale)), (8, 128))
        m = moment[s] * scale
        moment[s] = m
        low1[s] = m.astype(BF16)
        advance(low1, low2, s)
        advance(low2, low3, s)

    def factor(r, low, s):
        return 1.25 * r - 0.25 * dot(r.astype(BF16), low[s])

    def chain(r, s):
        r = factor(r, low2, s)
        r = factor(r, low3, s)
        t = r
        for _ in range(4):
            t = factor(t, low3, s)
        return 1.25 * r - 0.25 * dot(t.astype(BF16), low3[s])

    def identity(rows, offset):
        across = lax.broadcasted_iota(jnp.int32, (rows, 640), 1)
        down = lax.broadcasted_iota(jnp.int32, (rows, 640), 0) + offset
        return (across == down).astype(F32)

    def first(rows, offset, s):
        m = low1[s, pl.ds(offset, rows), :].astype(F32)
        return (1.25 * identity(rows, offset) - 0.25 * m) * scales[s, 0:1, 0:1]

    grow(side)
    rot0[0] = chain(first(160, quarter, side), side).astype(BF16)
    rotate(0).start()
    grow(1 - side)
    left = chain(first(80, eighth, 0), 0)
    rot1[0] = rotated(0)
    rotate(1).start()
    high = left.astype(BF16)
    low = (left - high.astype(F32)).astype(BF16)
    right = dot(high, both[0]) + dot(low, both[0])
    right = factor(right, low1, 1) * scales[1, 0:1, 0:1]
    right = chain(right, 1)
    update_ref[group, z] = right.astype(BF16)

    def slot(r):
        return lax.rem(z + r, 8)

    def rows(g, r, start, count):
        return update_ref.at[g, slot(r), pl.ds(start, count)]

    sent = []

    def send(ref, sems, index, peer):
        copy = remote(ref, ref, sems[0].at[index], sems[1].at[index], peer)
        copy.start()
        sent.append(copy)

    def landed(ref, sems, index):
        remote(ref, ref, sems[0].at[index], sems[1].at[index], partner).wait_recv()

    xs, ys, ps = (x_send, x_recv), (y_send, y_recv), (p_send, p_recv)
    fs, qs, cs = (f_send, f_recv), (q_send, q_recv), (c_send, c_recv)
    low, high, far = x_lo * 4 + y_down, x_lo * 4 + y_up, x_lo * 4 + y_far
    p_low, p_high, p_far = other_x * 4 + y_down, other_x * 4 + y_up, other_x * 4 + y_far

    def piece(i, part):
        start, count = ((32, 48), (32, 32), (64, 16))[part]
        return update_ref.at[group, i, pl.ds(start, count)]

    near = Near(piece, bz_send, bz_recv, z_peer, z)
    ring_a = Ring(
        lambda i: update_ref.at[pl.ds(0, 4), i, pl.ds(0, 32)], az_send, az_recv, (up_z, down_z), z
    )
    ring_c = Ring(
        lambda i: update_ref.at[pl.ds(4, 4), i, pl.ds(0, 32)], ay_send, ay_recv, (up_z, down_z), z, True
    )

    def own_out(r):
        send(rows(group, r, 32, 48), xs, r, partner)
        send(rows(group, r, 32, 48), ys, r, up_y)
        send(rows(group, r, 32, 48), ys, 8 + r, down_y)

    def pair_out(r):
        landed(rows(pair, r, 32, 48), xs, r)
        send(rows(pair, r, 32, 32), ps, r, up_y)
        send(rows(pair, r, 32, 32), ps, 8 + r, down_y)

    def own_on(r):
        landed(rows(low, r, 32, 48), ys, r)
        if r < 4:
            send(rows(low, r, 32, 48), fs, r, up_y)
        landed(rows(high, r, 32, 48), ys, 8 + r)
        if r >= 4:
            send(rows(high, r, 32, 48), fs, r, down_y)

    def pair_on(r):
        landed(rows(p_low, r, 32, 32), ps, r)
        if r < 4:
            send(rows(p_low, r, 32, 32), qs, r, up_y)
        landed(rows(p_high, r, 32, 32), ps, 8 + r)
        if r >= 4:
            send(rows(p_high, r, 32, 32), qs, r, down_y)

    def across(g, index):
        send(update_ref.at[g, :, pl.ds(64, 16)], cs, index, partner)

    over = []
    for k in range(1, 8):
        own = update_ref.at[group, z, pl.ds(0, 32)]
        copy = remote(own, own, a_send.at[k], a_recv.at[k], g_peer[k - 1])
        copy.start()
        over.append(copy)
    near.start()
    own_out(0)

    own = dot(both[side, pl.ds(quarter, 160), :], both[1 - side])
    stats_out[...] = BETA * old_ref[...] + (1.0 - BETA) * own
    near.relay()
    for copy in over:
        copy.wait_recv()
    ring_a.start(0)
    ring_c.start(0)
    own_out(6)
    own_out(2)
    near.landed(2)
    own_out(7)
    near.landed(3)
    own_out(1)
    pair_out(0)
    own_on(0)
    for r in (6, 2, 7, 1):
        pair_out(r)
    near.landed(4)
    own_out(5)
    near.landed(5)
    own_out(3)
    near.landed(6)
    near.landed(7)
    own_out(4)
    ring_a.arrived(0)
    ring_a.start(1)
    ring_c.arrived(0)
    ring_c.start(1)
    for r in (6, 2, 7, 1):
        own_on(r)
    for r in (5, 3, 4):
        pair_out(r)
    for r in (5, 3, 4):
        own_on(r)
    ring_a.arrived(1)
    ring_a.start(2)
    ring_c.arrived(1)
    ring_c.start(2)
    across(low, 0)
    across(high, 1)
    rot2[0] = rotated(1)
    rotate(2).start()
    for r in (0, 6, 2, 7, 1):
        pair_on(r)
    ring_a.arrived(2)
    ring_a.start(3)
    ring_c.arrived(2)
    ring_c.start(3)
    for r in (5, 3, 4):
        pair_on(r)
    for r in range(8):
        landed(rows(far, r, 32, 48), fs, r)
    across(far, 2)
    roots_out[...] = rotated(2).astype(F32)
    for r in range(8):
        landed(rows(p_far, r, 32, 32), qs, r)
    for index, g in enumerate((p_low, p_high, p_far)):
        landed(update_ref.at[g, :, pl.ds(64, 16)], cs, index)
    ring_a.arrived(3)
    ring_c.arrived(3)

    near.drain()
    ring_a.drain()
    ring_c.drain()
    for copy in sent + over:
        copy.wait_send()
    for step in range(3):
        rotate(step).wait_send()


GATHER_REFS = 30


def step_kernel(
    act_ref, gout_ref, old_ref, owner_ref, rotation_ref, update_ref, stats_out, roots_out,
    grad_ref, stats_ref, old_in, *rest,
):
    drain = gather_part(
        act_ref, gout_ref, old_ref, owner_ref, grad_ref, stats_ref, old_in, *rest[:GATHER_REFS]
    )
    finish_part(
        grad_ref, stats_ref, old_in, rotation_ref, update_ref, stats_out, roots_out,
        *rest[GATHER_REFS:],
    )
    drain()


def shampoo_step(activations, grad_out, old_rows, owner_map, rotation):
    hbm = pl.BlockSpec(memory_space=pltpu.HBM)
    widths = [width for _, width in CHUNKS]

    def sems(*counts):
        return [pltpu.SemaphoreType.DMA((count,)) for count in counts]

    return pl.pallas_call(
        step_kernel,
        out_shape=(
            jax.ShapeDtypeStruct((8, 8, 80, 640), BF16),
            jax.ShapeDtypeStruct((160, 640), F32),
            jax.ShapeDtypeStruct((160, 640), F32),
        ),
        in_specs=[hbm, hbm, hbm, SMEM, SMEM],
        out_specs=(VMEM, VMEM, VMEM),
        scratch_shapes=[
            pltpu.VMEM((8, 80, 640), BF16),
            pltpu.VMEM((8, 160, 640), BF16),
            pltpu.VMEM((160, 640), F32),
            pltpu.VMEM((256, 640), BF16),
            pltpu.VMEM((640, 256), BF16),
            pltpu.VMEM((640, 2048), BF16),
            pltpu.VMEM((8, 256, 640), BF16),
            *[pltpu.VMEM((640, width), F32) for width in widths],
            *[pltpu.VMEM((8, 80, width), BF16) for _ in range(3) for width in widths],
            *sems(2, 2, 2, 32, 16, 16, 16, 7, 7, 16, 16, 16, 16, 8, 8, 8, 8, 3),
            pltpu.VMEM((2, 640, 640), BF16),
            pltpu.VMEM((2, 640, 640), F32),
            pltpu.VMEM((2, 640, 640), F32),
            pltpu.VMEM((2, 640, 640), BF16),
            pltpu.VMEM((2, 640, 640), BF16),
            pltpu.VMEM((2, 640, 640), BF16),
            pltpu.VMEM((2, 640, 640), BF16),
            pltpu.VMEM((2, 8, 128), F32),
            pltpu.VMEM((2, 160, 640), BF16),
            pltpu.VMEM((2, 160, 640), BF16),
            pltpu.VMEM((2, 160, 640), BF16),
            *sems(8, 8, 7, 7, 7, 7, 8, 8, 8, 8, 16, 16, 16, 16, 8, 8, 8, 8, 3, 3, 3, 3),
        ],
        compiler_params=pltpu.CompilerParams(
            collective_id=0, has_side_effects=True, vmem_limit_bytes=44 * 2**20
        ),
        name="shampoo_step",
    )(activations, grad_out, old_rows, owner_map, rotation)


def order_kernel(owner_ref, in_ref, stats_ref, roots_ref, out_ref, stats_out, roots_out, sems):
    copies = [
        pltpu.make_async_copy(
            in_ref.at[owner_ref[b], pl.ds(half * 320, 320)],
            out_ref.at[b, pl.ds(half * 320, 320)],
            sems.at[b * 2 + half],
        )
        for b in range(8)
        for half in range(2)
    ]
    copies.append(pltpu.make_async_copy(stats_ref, stats_out, sems.at[16]))
    copies.append(pltpu.make_async_copy(roots_ref, roots_out, sems.at[17]))
    for copy in copies:
        copy.start()
    for copy in copies:
        copy.wait()


def order_blocks(by_place, stats_new, roots_new, owner_map):
    hbm = pl.BlockSpec(memory_space=pltpu.HBM)
    return pl.pallas_call(
        order_kernel,
        out_shape=(
            jax.ShapeDtypeStruct((8, 640, 640), BF16),
            jax.ShapeDtypeStruct((160, 640), F32),
            jax.ShapeDtypeStruct((160, 640), F32),
        ),
        in_specs=[SMEM, VMEM, VMEM, VMEM],
        out_specs=(hbm, hbm, hbm),
        scratch_shapes=[pltpu.SemaphoreType.DMA((18,))],
        compiler_params=pltpu.CompilerParams(vmem_limit_bytes=16 * 2**20),
        name="order_blocks",
    )(owner_map, by_place, stats_new, roots_new)


def local(activations, grad_out, stats_old, owner_map, rotation):
    old_rows = stats_old.reshape(160, 640)
    activations, grad_out, old_rows = (
        pltpu.with_memory_space_constraint(x, pltpu.HBM)
        for x in (activations, grad_out, old_rows)
    )
    by_place, stats_new, roots_new = shampoo_step(
        activations, grad_out, old_rows, owner_map, rotation
    )
    update, stats_new, roots_new = order_blocks(
        by_place.reshape(8, 640, 640), stats_new, roots_new, owner_map
    )
    return (
        update.reshape(2, 2560, 640),
        stats_new.reshape(stats_old.shape),
        roots_new.reshape(stats_old.shape),
    )


def solution(mesh):
    return jax.shard_map(
        local,
        mesh=mesh,
        in_specs=(P("dp", "mp"), P("dp", "mp"), P("mp", None, "dp", None, None), P(), P()),
        out_specs=(
            P("mp", None, None),
            P("mp", None, "dp", None, None),
            P("mp", None, "dp", None, None),
        ),
        check_vma=False,
    )
```
